32 devices in a mesh: dp: 8 (over z, x), replica: 4 (over y, core).
Axes of the slice: x: 2, y: 2, z: 4, core: 2. Of those that a mesh axis runs over, the one named last changes fastest.
Arguments:
- states: bfloat16 [4, 1536, 376], P('replica', 'dp'), may hold values from -6 to 6
- actions: bfloat16 [4, 1536, 17], P('replica', 'dp'), may hold values from -1 to 1
- target_forward: bfloat16 [4, 1536, 256], P('replica', 'dp'), may hold values from -5 to 5
- next_index: int32 [4, 1536], P('replica', 'dp'), may hold values from 0 to 191
- latent_ids: int32 [4, 1536], P('replica', 'dp'), may hold values from 0 to 255
- latents: bfloat16 [256, 256], replicated, may hold values from -5 to 5
- f_state: bfloat16 [376, 1536], replicated, may hold values from -0.25 to 0.25
- f_action: bfloat16 [17, 1536], replicated, may hold values from -0.25 to 0.25
- f_latent: bfloat16 [256, 1536], replicated, may hold values from -0.25 to 0.25
- f_output: bfloat16 [1536, 256], replicated, may hold values from -0.15625 to 0.15625
- b_state: bfloat16 [376, 1536], replicated, may hold values from -0.3125 to 0.3125
- b_output: bfloat16 [1536, 256], replicated, may hold values from -1 to 1
Outputs:
- grad_f_state: bfloat16 [376, 1536], P(None, 'dp')
- grad_f_action: bfloat16 [17, 1536], P(None, 'dp')
- grad_f_latent: bfloat16 [256, 1536], P(None, 'dp')
- grad_f_output: bfloat16 [1536, 256], P('dp')
- grad_b_state: bfloat16 [376, 1536], P(None, 'dp')
- grad_b_output: bfloat16 [1536, 256], P('dp')
- loss_value: float32 [], replicated
The draws below stay inside these ranges and needn't reach their ends.
Inputs may be any that keep to these rules, and one draw needn't show every extreme that they name: `next_index`: the next state lies in the same aligned block of 192 rows as the transition.
All inputs are finite; a program needn't handle non-finite values.
Results may differ from the reference program's by a relative error of at most 0.0056.
Values may be sent and summed in bfloat16 or wider, within the bound.
No kernel may reach another device: no remote copies, remote signals or barrier semaphores. Data moves between devices by JAX's collectives and lax.ppermute only.
A program may use at most 128 MiB of HBM per device.

```python
import math
import jax
import jax.numpy as jnp
from jax import lax

OBS = 376
ACT = 17
R = 256
H = 1536
ZCOUNT = 256
ROWS = 192
GROUP = 1536
REPLICAS = 4


def common_direction(key):
    return jnp.clip(jax.random.normal(jax.random.fold_in(key, 101), (R,), jnp.float32), -4.0, 4.0)


def draw_target_forward(key, part):
    direction = common_direction(key)
    key = jax.random.fold_in(key, 7)
    noise_key = jax.random.fold_in(key, 1)
    share_key = jax.random.fold_in(key, 2)
    position = jnp.arange(GROUP, dtype=jnp.float32) / max(GROUP - 1, 1)
    growth = 0.35 + 0.7 * position
    values = jax.random.normal(noise_key, (REPLICAS, GROUP, R), jnp.float32)
    shares = jax.random.uniform(share_key, (REPLICAS, GROUP, 1), jnp.float32, 0.15, 0.35)
    scaled = jnp.clip(values * growth[None, :, None] + shares * direction[None, None, :], -5.0, 5.0)
    return scaled.astype(jnp.bfloat16)


def draw_b_output(key, part):
    direction = common_direction(key)
    key = jax.random.fold_in(key, 11)
    random_part = jnp.clip(jax.random.normal(key, (H, R), jnp.float32), -5.0, 5.0)
    strength = 0.4
    root = math.sqrt(H)
    matrix = (random_part + strength * direction[None, :] / root) / root
    return matrix.astype(jnp.bfloat16)


def plant(result, own_key, smallest, largest):
    longest = result.shape.index(max(result.shape))
    spots = []
    for shift in (0, 1):
        where = [jax.random.randint(jax.random.fold_in(own_key, axis), (), 0, length) for axis, length in enumerate(result.shape)]
        where[longest] = (where[longest] + shift) % result.shape[longest]
        spots.append(tuple(where))
    return result.at[spots[0]].set(smallest).at[spots[1]].set(largest)


def steps_of(stream_key, dims, cuts, smallest, top_value):
    def one(dim, blocks):
        draws = jax.random.uniform(jax.random.fold_in(jax.random.fold_in(stream_key, 6), dim), (blocks,), jnp.float32, smallest / len(cuts), top_value / len(cuts))
        return jnp.repeat(jnp.exp(draws), dims[dim] // blocks).reshape((-1,) + (1,) * (len(dims) - dim - 1))

    gain = one(*cuts[0])
    for cut in cuts[1:]:
        gain = gain * one(*cut)
    return gain


def bell_draw(rng, dims, spread, reach, shards=(), kind=jnp.bfloat16):
    entries = spread * jax.random.normal(rng, dims, jnp.float32)
    if shards:
        entries = entries * steps_of(rng, dims, shards, -0.22, 0.18)
    return jnp.clip(entries, -reach, reach).astype(kind)


def setup_inputs(seed: int = 0) -> dict:
    key_of = jax.random.split(jax.random.key(seed), 13)
    states = bell_draw(key_of[0], (REPLICAS, GROUP, OBS), 1.0, 6.0, ((0, 4), (1, 8)))
    actions = jnp.clip(jax.random.uniform(key_of[1], (REPLICAS, GROUP, ACT), jnp.float32, -1.0, 1.0) * steps_of(key_of[1], (REPLICAS, GROUP, ACT), ((0, 4), (1, 8)), -0.4, 0.0), -1.0, 1.0).astype(jnp.bfloat16)
    target_forward = draw_target_forward(jax.random.fold_in(key_of[12], 71), 0)
    next_index = plant(jax.random.randint(key_of[3], (REPLICAS, GROUP), 0, ROWS), jax.random.fold_in(key_of[3], 1), 0, ROWS - 1).astype(jnp.int32)
    latent_ids = plant(jax.random.randint(key_of[4], (REPLICAS, GROUP), 0, ZCOUNT), jax.random.fold_in(key_of[4], 1), 0, ZCOUNT - 1).astype(jnp.int32)
    latents = bell_draw(key_of[5], (ZCOUNT, R), 1.0, 5.0)
    f_state = bell_draw(key_of[6], (OBS, H), (OBS + ACT + R) ** -0.5, 0.25)
    f_action = bell_draw(key_of[7], (ACT, H), (OBS + ACT + R) ** -0.5, 0.25)
    f_latent = bell_draw(key_of[8], (R, H), (OBS + ACT + R) ** -0.5, 0.25)
    f_output = bell_draw(key_of[9], (H, R), H ** -0.5, 0.15625)
    b_state = bell_draw(key_of[10], (OBS, H), OBS ** -0.5, 0.3125)
    b_output = draw_b_output(jax.random.fold_in(key_of[12], 71), 0)
    return dict(states=states, actions=actions, target_forward=target_forward, next_index=next_index, latent_ids=latent_ids, latents=latents, f_state=f_state, f_action=f_action, f_latent=f_latent, f_output=f_output, b_state=b_state, b_output=b_output)


GAMMA = 0.98
EPSILON = 1e-06
HIGH = lax.Precision.HIGHEST

def forward_pass(current, later, moves, latent_rows, f_state, f_action, f_latent, f_output, b_state, b_output):
    f_pre = jnp.dot(current, f_state, preferred_element_type=jnp.float32) + jnp.dot(moves, f_action, preferred_element_type=jnp.float32) + jnp.dot(latent_rows, f_latent, preferred_element_type=jnp.float32)
    f_hidden = jnp.maximum(f_pre, 0.0).astype(jnp.bfloat16)
    forward_emb = jnp.dot(f_hidden, f_output, preferred_element_type=jnp.float32).astype(jnp.bfloat16)
    b_pre = jnp.dot(later, b_state, preferred_element_type=jnp.float32)
    b_hidden = jnp.maximum(b_pre, 0.0).astype(jnp.bfloat16)
    b_raw = jnp.dot(b_hidden, b_output, preferred_element_type=jnp.float32)
    b_scale = lax.rsqrt(lax.optimization_barrier(jnp.mean(b_raw * b_raw, axis=-1, keepdims=True)) + EPSILON)
    backward_emb = (b_raw * b_scale).astype(jnp.bfloat16)
    return (f_pre, f_hidden, forward_emb, b_pre, b_hidden, b_raw, b_scale, backward_emb)

def backward_pass(grad_forward, grad_backward, current, later, moves, latent_rows, f_pre, f_hidden, b_pre, b_hidden, b_raw, b_scale, f_output, b_output):
    inner = lax.optimization_barrier(jnp.mean(b_raw * grad_backward, axis=-1, keepdims=True))
    grad_raw = (b_scale * grad_backward - b_raw * b_scale * b_scale * b_scale * inner).astype(jnp.bfloat16)
    part_b_output = jnp.dot(b_hidden.T, grad_raw, preferred_element_type=jnp.float32)
    b_back = jnp.dot(grad_raw, b_output.T, preferred_element_type=jnp.float32)
    b_delta = jnp.where(b_pre > 0, b_back, 0.0).astype(jnp.bfloat16)
    part_b_state = jnp.dot(later.T, b_delta, preferred_element_type=jnp.float32)
    part_f_output = jnp.dot(f_hidden.T, grad_forward, preferred_element_type=jnp.float32)
    f_back = jnp.dot(grad_forward, f_output.T, preferred_element_type=jnp.float32)
    f_delta = jnp.where(f_pre > 0, f_back, 0.0).astype(jnp.bfloat16)
    part_f_state = jnp.dot(current.T, f_delta, preferred_element_type=jnp.float32)
    part_f_action = jnp.dot(moves.T, f_delta, preferred_element_type=jnp.float32)
    part_f_latent = jnp.dot(latent_rows.T, f_delta, preferred_element_type=jnp.float32)
    return (part_f_state, part_f_action, part_f_latent, part_f_output, part_b_state, part_b_output)

def reference(states, actions, target_forward, next_index, latent_ids, latents, f_state, f_action, f_latent, f_output, b_state, b_output):
    replica_count = states.shape[0]
    group = states.shape[1]
    total = replica_count * group
    factor = 1.0 / math.sqrt(total)
    base = jnp.arange(group, dtype=jnp.int32) // ROWS * ROWS
    totals = None
    loss_sum = jnp.float32(0.0)
    for which in range(replica_count):
        current = states[which]
        moves = actions[which]
        later = jnp.take(current, (base + next_index[which]).astype(jnp.int32), axis=0)
        latent_rows = jnp.take(latents, latent_ids[which].astype(jnp.int32), axis=0)
        f_pre, f_hidden, forward_emb, b_pre, b_hidden, b_raw, b_scale, backward_emb = forward_pass(current, later, moves, latent_rows, f_state, f_action, f_latent, f_output, b_state, b_output)
        forward32 = forward_emb.astype(jnp.float32)
        back32 = backward_emb.astype(jnp.float32)
        error = forward32 - GAMMA * target_forward[which].astype(jnp.float32)
        gram = jnp.dot(backward_emb.T, backward_emb, preferred_element_type=jnp.float32)
        cross = jnp.dot(forward32.T, error, precision=HIGH, preferred_element_type=jnp.float32)
        error_gram = jnp.dot(error.T, error, precision=HIGH, preferred_element_type=jnp.float32)
        square_sum = jnp.sum(error_gram * gram)
        diagonal_sum = jnp.sum(forward32 * back32)
        loss_sum = loss_sum + 0.5 / group * square_sum - diagonal_sum
        pulled = jnp.dot(error, gram, precision=HIGH, preferred_element_type=jnp.float32)
        pushed = jnp.dot(back32, cross.T, precision=HIGH, preferred_element_type=jnp.float32)
        grad_forward = (factor * (pulled / group - back32)).astype(jnp.bfloat16)
        grad_backward = factor * (pushed / group - forward32)
        parts = backward_pass(grad_forward, grad_backward, current, later, moves, latent_rows, f_pre, f_hidden, b_pre, b_hidden, b_raw, b_scale, f_output, b_output)
        if totals is None:
            totals = parts
        else:
            totals = tuple((left + right for left, right in zip(totals, parts)))
    grads = tuple((item.astype(jnp.bfloat16) for item in totals))
    return (grads[0], grads[1], grads[2], grads[3], grads[4], grads[5], loss_sum / total)
```

```python
import functools
import math

import jax
import jax.numpy as jnp
from jax import lax
from jax.experimental import pallas as pl
from jax.experimental.pallas import tpu as pltpu
from jax.sharding import PartitionSpec as P

GAMMA = 0.98
EPSILON = 1e-06
HIGH = lax.Precision.HIGHEST
BF16 = jnp.bfloat16
F32 = jnp.float32
LANES = 128
ROW_TILE = 16
VMEM_LIMIT = 56 * 1024 * 1024
KERNEL_GROUP_LIMIT = 2048


def round_up(value, unit):
    return -(-value // unit) * unit


def dot_nn(left, right):
    return lax.dot_general(left, right, (((1,), (0,)), ((), ())), preferred_element_type=F32)


def dot_nt(left, right):
    return lax.dot_general(left, right, (((1,), (1,)), ((), ())), preferred_element_type=F32)


def dot_tn(left, right):
    return lax.dot_general(left, right, (((0,), (0,)), ((), ())), preferred_element_type=F32)


def split_two(value):
    high = value.astype(BF16)
    return high, (value - high.astype(F32)).astype(BF16)


def step_kernel(
    cfg,
    *refs,
):
    chunks = cfg["chunks"]
    x_refs = refs[:chunks]
    (
        wf_ref,
        wb_ref,
        fo_ref,
        bo_ref,
        lat_ref,
        wfb_ref,
        wbb_ref,
        fob_ref,
        bob_ref,
        send_ref,
        keep_ref,
        loss_ref,
        a_ref,
        later_ref,
        f_ref,
        b_ref,
        u_ref,
        t_ref,
        part_ref,
    ) = refs[chunks:]
    rows, obs, act, rank = cfg["rows"], cfg["obs"], cfg["act"], cfg["rank"]
    obs_pad, x_pad, hidden, zcount = cfg["obs_pad"], cfg["x_pad"], cfg["hidden"], cfg["zcount"]
    group, total, block = cfg["group"], cfg["total"], cfg["block"]
    tile = cfg["tile"]
    inner_chunks = cfg["inner"]
    m = rows * inner_chunks
    steps = chunks // inner_chunks

    for j in range(chunks):
        a_ref[pl.ds(j * rows, rows), pl.ds(0, x_pad)] = x_refs[j][:, :x_pad]
        t_ref[pl.ds(j * rows, rows), :] = x_refs[j][:, x_pad:]

    def forward(step, carry):
        gram, ftf, ftt = carry
        base = pl.multiple_of(step * m, ROW_TILE)
        here = pl.ds(base, m)
        xx = a_ref[here, pl.ds(0, x_pad)]
        next_col = xx[:, obs + act : obs + act + 1].astype(F32)
        id_col = xx[:, obs + act + 1 : obs + act + 2].astype(F32)
        spots = lax.broadcasted_iota(jnp.int32, (m, zcount), 1).astype(F32)
        picks = jnp.where(id_col == spots, 1.0, 0.0).astype(BF16)
        z = dot_nn(picks, lat_ref[...]).astype(BF16)
        a_ref[here, pl.ds(x_pad, rank)] = z
        row_spots = lax.broadcasted_iota(jnp.int32, (rows, rows), 1).astype(F32)
        pieces = []
        for j in range(inner_chunks):
            near = xx[j * rows : (j + 1) * rows, :obs_pad]
            hot = jnp.where(next_col[j * rows : (j + 1) * rows] == row_spots, 1.0, 0.0).astype(BF16)
            pieces.append(dot_nn(hot, near).astype(BF16))
        later = jnp.concatenate(pieces, axis=0) if inner_chunks > 1 else pieces[0]
        later_ref[here, :] = later
        whole = a_ref[here, :]
        f_acc = jnp.zeros((m, rank), F32)
        u = jnp.zeros((m, rank), F32)
        for n in range(0, hidden, tile):
            h = jnp.maximum(dot_nn(whole, wf_ref[:, n : n + tile]), 0.0).astype(BF16)
            f_acc = f_acc + dot_nn(h, fo_ref[n : n + tile, :])
            g = jnp.maximum(dot_nn(later, wb_ref[:, n : n + tile]), 0.0).astype(BF16)
            u = u + dot_nn(g, bo_ref[n : n + tile, :])
        emb = f_acc.astype(BF16)
        scale = lax.rsqrt(jnp.mean(u * u, axis=-1, keepdims=True) + EPSILON)
        back = (u * scale).astype(BF16)
        f_ref[here, :] = emb
        b_ref[here, :] = back
        u_ref[here, :] = u
        target = t_ref[here, :]
        gram = gram + dot_tn(back, back)
        ftf = ftf + dot_tn(emb, emb)
        ftt = ftt + dot_tn(target, emb)
        return gram, ftf, ftt

    zero = jnp.zeros((rank, rank), F32)
    gram, ftf, ttf = lax.fori_loop(0, steps, forward, (zero, zero, zero))
    cross_t = ftf - GAMMA * ttf
    gram_hi, gram_lo = split_two(gram)
    cross_hi, cross_lo = split_two(cross_t)
    factor = 1.0 / math.sqrt(total)
    part_ref[...] = jnp.zeros_like(part_ref)
    c0, c1, c2, c3 = cfg["cols"]

    def backward(step, carry):
        square, diagonal = carry
        base = pl.multiple_of(step * m, ROW_TILE)
        here = pl.ds(base, m)
        emb = f_ref[here, :]
        emb32 = emb.astype(F32)
        back = b_ref[here, :]
        back32 = back.astype(F32)
        error = emb32 - GAMMA * t_ref[here, :].astype(F32)
        err_hi, err_lo = split_two(error)
        pulled = dot_nn(err_hi, gram_hi) + (dot_nn(err_hi, gram_lo) + dot_nn(err_lo, gram_hi))
        square = square + jnp.sum(pulled * error, axis=0, keepdims=True)
        diagonal = diagonal + jnp.sum(emb32 * back32, axis=0, keepdims=True)
        d_f = (factor * (pulled / group - back32)).astype(BF16)
        pushed = dot_nn(back, cross_hi) + dot_nn(back, cross_lo)
        d_b = factor * (pushed / group - emb32)
        u = u_ref[here, :]
        scale = lax.rsqrt(jnp.mean(u * u, axis=-1, keepdims=True) + EPSILON)
        inner = jnp.mean(u * d_b, axis=-1, keepdims=True)
        d_u = (scale * d_b - u * (scale * scale * scale * inner)).astype(BF16)
        whole = a_ref[here, :]
        later = later_ref[here, :]
        f_pre = dot_nt(wfb_ref[...], whole)
        f_hid = jnp.maximum(f_pre, 0.0).astype(BF16)
        f_delta = jnp.where(f_pre > 0, dot_nt(fob_ref[...], d_f), 0.0).astype(BF16)
        part_ref[:, c0:c1] += dot_nn(f_delta, whole)
        part_ref[:, c1:c2] += dot_nn(f_hid, d_f)
        b_pre = dot_nt(wbb_ref[...], later)
        b_hid = jnp.maximum(b_pre, 0.0).astype(BF16)
        b_delta = jnp.where(b_pre > 0, dot_nt(bob_ref[...], d_u), 0.0).astype(BF16)
        part_ref[:, c2:c3] += dot_nn(b_delta, later)
        part_ref[:, c3:] += dot_nn(b_hid, d_u)
        return square, diagonal

    line = jnp.zeros((1, rank), F32)
    square, diagonal = lax.fori_loop(0, steps, backward, (line, line))
    loss = (0.5 / group) * jnp.sum(square) - jnp.sum(diagonal)
    loss_ref[...] = jnp.full(loss_ref.shape, loss, F32)
    core = lax.rem(lax.axis_index("replica"), 2)
    half = block // 2
    mine = pl.multiple_of(core * half, ROW_TILE)
    other = pl.multiple_of((1 - core) * half, ROW_TILE)
    keep_ref[...] = part_ref[pl.ds(mine, half), :]
    send_ref[...] = part_ref[pl.ds(other, half), :].astype(BF16)


def finish_kernel(cfg, low_ref, high_ref, fs_ref, fa_ref, fl_ref, fo_ref, bs_ref, bo_ref, full_ref):
    obs, act, rank, x_pad = cfg["obs"], cfg["act"], cfg["rank"], cfg["x_pad"]
    half = cfg["block"] // 2
    c0, c1, c2, c3 = cfg["cols"]
    core = lax.rem(lax.axis_index("replica"), 2)
    mine = pl.multiple_of(core * half, ROW_TILE)
    other = pl.multiple_of((1 - core) * half, ROW_TILE)
    full_ref[pl.ds(mine, half), :] = low_ref[...].astype(F32)
    full_ref[pl.ds(other, half), :] = high_ref[...].astype(F32)
    front = full_ref[:, :x_pad].T
    fs_ref[...] = front[:obs].astype(BF16)
    fa_ref[...] = front[obs : obs + act].astype(BF16)
    fl_ref[...] = full_ref[:, x_pad:c1].T.astype(BF16)
    fo_ref[...] = full_ref[:, c1:c2].astype(BF16)
    bs_ref[...] = full_ref[:, c2:c3].T[:obs].astype(BF16)
    bo_ref[...] = full_ref[:, c3:].astype(BF16)


def exchange(array, axis, size, bit):
    return lax.ppermute(array, axis, [(i, i ^ bit) for i in range(size)])


def gather_chunks(own, size):
    found = {0: own}
    bit = size // 2
    wide = [step for step in range(2, size, 2)]
    found[1] = exchange(own, "dp", size, 1)
    for step in wide:
        found[step] = exchange(own, "dp", size, step)
    for step in wide:
        found[step ^ 1] = exchange(found[step], "dp", size, 1)
    return [found[j] for j in range(size)]


def fast_local(
    states,
    actions,
    target_forward,
    next_index,
    latent_ids,
    latents,
    f_state,
    f_action,
    f_latent,
    f_output,
    b_state,
    b_output,
):
    size = lax.axis_size("dp")
    replicas = lax.axis_size("replica")
    rows, obs = states.shape[1:]
    act = actions.shape[2]
    zcount, rank = latents.shape
    hidden = f_state.shape[1]
    block = hidden // size
    group = rows * size
    total = group * replicas
    x_pad = round_up(obs + act + 2, LANES)
    obs_pad = round_up(obs, LANES)
    c1 = x_pad + rank
    c2 = c1 + rank
    c3 = c2 + obs_pad
    width = c3 + rank
    cfg = dict(
        chunks=size,
        rows=rows,
        obs=obs,
        act=act,
        rank=rank,
        obs_pad=obs_pad,
        x_pad=x_pad,
        hidden=hidden,
        zcount=zcount,
        group=group,
        total=total,
        block=block,
        tile=512,
        inner=2,
        cols=(0, c1, c2, c3),
    )
    own = jnp.concatenate(
        [
            states[0],
            actions[0],
            next_index[0][:, None].astype(BF16),
            latent_ids[0][:, None].astype(BF16),
            jnp.zeros((rows, x_pad - obs - act - 2), BF16),
            target_forward[0],
        ],
        axis=1,
    )
    xs = gather_chunks(own, size)
    wf = jnp.concatenate(
        [f_state, f_action, jnp.zeros((x_pad - obs - act, hidden), BF16), f_latent], axis=0
    )
    wb = jnp.concatenate([b_state, jnp.zeros((obs_pad - obs, hidden), BF16)], axis=0)
    start = lax.axis_index("dp") * block
    wfb = lax.dynamic_slice_in_dim(wf, start, block, 1).T
    wbb = lax.dynamic_slice_in_dim(wb, start, block, 1).T
    fob = lax.dynamic_slice_in_dim(f_output, start, block, 0)
    bob = lax.dynamic_slice_in_dim(b_output, start, block, 0)
    flops = 2 * group * (c1 + 2 * rank + obs_pad) * hidden
    send, keep, loss = pl.pallas_call(
        functools.partial(step_kernel, cfg),
        out_shape=(
            jax.ShapeDtypeStruct((block // 2, width), BF16),
            jax.ShapeDtypeStruct((block // 2, width), F32),
            jax.ShapeDtypeStruct((8, LANES), F32),
        ),
        scratch_shapes=[
            pltpu.VMEM((group, x_pad + rank), BF16),
            pltpu.VMEM((group, obs_pad), BF16),
            pltpu.VMEM((group, rank), BF16),
            pltpu.VMEM((group, rank), BF16),
            pltpu.VMEM((group, rank), F32),
            pltpu.VMEM((group, rank), BF16),
            pltpu.VMEM((block, width), F32),
        ],
        compiler_params=pltpu.CompilerParams(vmem_limit_bytes=VMEM_LIMIT),
        cost_estimate=pl.CostEstimate(
            flops=flops, bytes_accessed=12_000_000, transcendentals=2 * group
        ),
        name="step",
    )(*xs, wf, wb, f_output, b_output, latents, wfb, wbb, fob, bob)
    got = exchange(send, "replica", replicas, 1)
    loss = loss + exchange(loss, "replica", replicas, 1)
    first = (keep + got.astype(F32)).astype(BF16)
    second = exchange(first, "replica", replicas, 2)
    loss = loss + exchange(loss, "replica", replicas, 2)
    mine = (first.astype(F32) + second.astype(F32)).astype(BF16)
    other = exchange(mine, "replica", replicas, 1)
    outs = pl.pallas_call(
        functools.partial(finish_kernel, cfg),
        out_shape=(
            jax.ShapeDtypeStruct((obs, block), BF16),
            jax.ShapeDtypeStruct((act, block), BF16),
            jax.ShapeDtypeStruct((rank, block), BF16),
            jax.ShapeDtypeStruct((block, rank), BF16),
            jax.ShapeDtypeStruct((obs, block), BF16),
            jax.ShapeDtypeStruct((block, rank), BF16),
        ),
        scratch_shapes=[pltpu.VMEM((block, width), F32)],
        compiler_params=pltpu.CompilerParams(vmem_limit_bytes=16 * 1024 * 1024),
        name="finish",
    )(mine, other)
    return (*outs, loss[0, 0] / total)


def forward_pass(
    current, later, moves, latent_rows, f_state, f_action, f_latent, f_output, b_state, b_output
):
    f_pre = (
        jnp.dot(current, f_state, preferred_element_type=F32)
        + jnp.dot(moves, f_action, preferred_element_type=F32)
        + jnp.dot(latent_rows, f_latent, preferred_element_type=F32)
    )
    f_hidden = jnp.maximum(f_pre, 0.0).astype(BF16)
    forward_emb = jnp.dot(f_hidden, f_output, preferred_element_type=F32).astype(BF16)
    b_pre = jnp.dot(later, b_state, preferred_element_type=F32)
    b_hidden = jnp.maximum(b_pre, 0.0).astype(BF16)
    b_raw = jnp.dot(b_hidden, b_output, preferred_element_type=F32)
    b_scale = lax.rsqrt(jnp.mean(b_raw * b_raw, axis=-1, keepdims=True) + EPSILON)
    backward_emb = (b_raw * b_scale).astype(BF16)
    return (f_pre, f_hidden, forward_emb, b_pre, b_hidden, b_raw, b_scale, backward_emb)


def general_local(
    states,
    actions,
    target_forward,
    next_index,
    latent_ids,
    latents,
    f_state,
    f_action,
    f_latent,
    f_output,
    b_state,
    b_output,
):
    current = states[0]
    moves = actions[0]
    later = jnp.take(current, next_index[0], axis=0)
    latent_rows = jnp.take(latents, latent_ids[0], axis=0)
    f_pre, f_hidden, forward_emb, b_pre, b_hidden, b_raw, b_scale, backward_emb = forward_pass(
        current, later, moves, latent_rows, f_state, f_action, f_latent, f_output, b_state, b_output
    )
    group = current.shape[0] * lax.axis_size("dp")
    total = group * lax.axis_size("replica")
    factor = 1.0 / math.sqrt(total)
    forward32 = forward_emb.astype(F32)
    back32 = backward_emb.astype(F32)
    error = forward32 - GAMMA * target_forward[0].astype(F32)
    gram, cross = lax.psum(
        (
            jnp.dot(backward_emb.T, backward_emb, preferred_element_type=F32),
            jnp.dot(forward32.T, error, precision=HIGH, preferred_element_type=F32),
        ),
        "dp",
    )
    pulled = jnp.dot(error, gram, precision=HIGH, preferred_element_type=F32)
    pushed = jnp.dot(back32, cross.T, precision=HIGH, preferred_element_type=F32)
    partial_loss = 0.5 / group * jnp.sum(pulled * error) - jnp.sum(forward32 * back32)
    grad_forward = (factor * (pulled / group - back32)).astype(BF16)
    grad_backward = factor * (pushed / group - forward32)
    inner = jnp.mean(b_raw * grad_backward, axis=-1, keepdims=True)
    grad_raw = (b_scale * grad_backward - b_raw * b_scale * b_scale * b_scale * inner).astype(BF16)
    part_bo = jnp.dot(b_hidden.T, grad_raw, preferred_element_type=F32)
    b_back = jnp.dot(grad_raw, b_output.T, preferred_element_type=F32)
    b_delta = jnp.where(b_pre > 0, b_back, 0.0).astype(BF16)
    part_bs = jnp.dot(later.T, b_delta, preferred_element_type=F32)
    part_fo = jnp.dot(f_hidden.T, grad_forward, preferred_element_type=F32)
    f_back = jnp.dot(grad_forward, f_output.T, preferred_element_type=F32)
    f_delta = jnp.where(f_pre > 0, f_back, 0.0).astype(BF16)
    part_fs = jnp.dot(current.T, f_delta, preferred_element_type=F32)
    part_fa = jnp.dot(moves.T, f_delta, preferred_element_type=F32)
    part_fl = jnp.dot(latent_rows.T, f_delta, preferred_element_type=F32)
    places = (1, 1, 1, 0, 1, 0)
    parts = (part_fs, part_fa, part_fl, part_fo, part_bs, part_bo)
    shares = tuple(
        lax.psum_scatter(part, "dp", scatter_dimension=place, tiled=True)
        for part, place in zip(parts, places)
    )
    summed = lax.psum(shares, "replica")
    loss_sum = lax.psum(partial_loss, ("dp", "replica"))
    return (*(item.astype(BF16) for item in summed), loss_sum / total)


def local(*args):
    size, replicas = lax.axis_size("dp"), lax.axis_size("replica")
    rows, hidden = args[0].shape[1], args[6].shape[1]
    fits = size == 8 and replicas == 4 and rows * size <= KERNEL_GROUP_LIMIT
    whole = rows % ROW_TILE == 0 and hidden % (size * 2 * ROW_TILE) == 0 and hidden % 512 == 0
    exact = rows <= 256 and args[5].shape[0] <= 256
    return (fast_local if fits and whole and exact else general_local)(*args)


def solution(mesh):
    in_specs = (
        P("replica", "dp", None),
        P("replica", "dp", None),
        P("replica", "dp", None),
        P("replica", "dp"),
        P("replica", "dp"),
        P(),
        P(),
        P(),
        P(),
        P(),
        P(),
        P(),
    )
    out_specs = (
        P(None, "dp"),
        P(None, "dp"),
        P(None, "dp"),
        P("dp", None),
        P(None, "dp"),
        P("dp", None),
        P(),
    )
    return jax.shard_map(local, mesh=mesh, in_specs=in_specs, out_specs=out_specs, check_vma=False)
```

```python
import functools
import math

import jax
import jax.numpy as jnp
from jax import lax
from jax.experimental import pallas as pl
from jax.experimental.pallas import tpu as pltpu
from jax.sharding import PartitionSpec as P

GAMMA = 0.98
EPSILON = 1e-06
HIGH = lax.Precision.HIGHEST
BF16 = jnp.bfloat16
F32 = jnp.float32
LANES = 128
ROW_TILE = 16
VMEM_LIMIT = 56 * 1024 * 1024
KERNEL_GROUP_LIMIT = 2048


def round_up(value, unit):
    return -(-value // unit) * unit


def dot_nn(left, right):
    return lax.dot_general(left, right, (((1,), (0,)), ((), ())), preferred_element_type=F32)


def dot_nt(left, right):
    return lax.dot_general(left, right, (((1,), (1,)), ((), ())), preferred_element_type=F32)


def dot_tn(left, right):
    return lax.dot_general(left, right, (((0,), (0,)), ((), ())), preferred_element_type=F32)


def split_two(value):
    high = value.astype(BF16)
    return high, (value - high.astype(F32)).astype(BF16)


def pack_kernel(cfg, state_ref, move_ref, next_ref, latent_ref, target_ref, out_ref, side_ref):
    rows, obs, act, obs_pad, side = (cfg[k] for k in ("rows", "obs", "act", "obs_pad", "side"))
    lane = side_ref.shape[1]
    side_ref[...] = jnp.zeros_like(side_ref)
    side_ref[0:act, 0:rows] = move_ref[...].astype(F32)
    side_ref[act : act + 1, 0:rows] = next_ref[...].astype(F32)
    side_ref[act + 1 : act + 2, 0:rows] = latent_ref[...].astype(F32)
    gap = jnp.zeros((rows, obs_pad - obs), BF16)
    out_ref[0:rows, 0:obs_pad] = jnp.concatenate([state_ref[0], gap], axis=1)
    out_ref[0:rows, obs_pad:] = target_ref[0]
    half = side // 2
    out_ref[rows:, :] = jnp.zeros((half, out_ref.shape[1]), BF16)
    out_ref[rows:, 0:lane] = side_ref[0:half, :].astype(BF16)
    out_ref[rows:, lane : 2 * lane] = side_ref[half:side, :].astype(BF16)


def weights_kernel(cfg, fs_ref, fa_ref, fl_ref, bs_ref, wf_ref, wb_ref, wfb_ref, wbb_ref):
    obs, obs_pad, x_pad = cfg["obs"], cfg["obs_pad"], cfg["x_pad"]
    hidden, block, act = cfg["hidden"], cfg["block"], cfg["act"]
    gap = jnp.zeros((obs_pad - obs, hidden), BF16)
    wf_ref[0:obs_pad, :] = jnp.concatenate([fs_ref[...], gap], axis=0)
    wf_ref[obs_pad:x_pad, :] = fa_ref[...]
    wf_ref[x_pad:, :] = fl_ref[...]
    wb_ref[...] = jnp.concatenate([bs_ref[...], gap], axis=0)
    me = lax.axis_index("dp")
    start = me * block
    base = pl.multiple_of(start // LANES * LANES, LANES)
    odd = lax.rem(me, 2) == 1
    span = pl.ds(base, 2 * LANES)

    def pick(ref):
        near = ref[:, span].astype(F32).T
        return jnp.where(odd, near[2 * LANES - block :], near[:block]).astype(BF16)

    wfb_ref[...] = pick(wf_ref)
    wbb_ref[...] = pick(wb_ref)


def forward_rows(cfg, xs, weights, outs):
    wf_ref, wb_ref, fo_ref, bo_ref, lat_ref, wfb_ref, wbb_ref = weights
    a_ref, later_ref, f_ref, u_ref, fh_ref, bh_ref = outs
    rows, act, rank, side = cfg["rows"], cfg["act"], cfg["rank"], cfg["side"]
    obs_pad, x_pad, hidden, zcount = cfg["obs_pad"], cfg["x_pad"], cfg["hidden"], cfg["zcount"]
    tile, lane = cfg["tile"], cfg["lane"]
    m = rows * len(xs)
    half = side // 2
    row_spots = lax.broadcasted_iota(jnp.int32, (rows, rows), 1).astype(F32)
    spots = lax.broadcasted_iota(jnp.int32, (rows, zcount), 1).astype(F32)
    blank = jnp.zeros((rows, x_pad - obs_pad - side), BF16)
    for j, x_ref in enumerate(xs):
        here = slice(j * rows, (j + 1) * rows)
        few = jnp.concatenate(
            [x_ref[rows:, 0:lane].astype(F32), x_ref[rows:, lane : 2 * lane].astype(F32)], axis=0
        ).T[:rows]
        near = x_ref[0:rows, 0:obs_pad]
        picks = jnp.where(few[:, act + 1 : act + 2] == spots, 1.0, 0.0).astype(BF16)
        hot = jnp.where(few[:, act : act + 1] == row_spots, 1.0, 0.0).astype(BF16)
        a_ref[here, 0:obs_pad] = near
        a_ref[here, obs_pad:x_pad] = jnp.concatenate([few.astype(BF16), blank], axis=1)
        a_ref[here, x_pad:] = dot_nn(picks, lat_ref[...]).astype(BF16)
        later_ref[here, :] = dot_nn(hot, near).astype(BF16)
    whole = a_ref[...]
    later = later_ref[...]
    f_acc = jnp.zeros((m, rank), F32)
    u = jnp.zeros((m, rank), F32)
    for n in range(0, hidden, tile):
        h = jnp.maximum(dot_nn(whole, wf_ref[:, n : n + tile]), 0.0).astype(BF16)
        f_acc = f_acc + dot_nn(h, fo_ref[n : n + tile, :])
        g = jnp.maximum(dot_nn(later, wb_ref[:, n : n + tile]), 0.0).astype(BF16)
        u = u + dot_nn(g, bo_ref[n : n + tile, :])
    emb = f_acc.astype(BF16)
    back = (u * lax.rsqrt(jnp.mean(u * u, axis=-1, keepdims=True) + EPSILON)).astype(BF16)
    f_ref[...] = emb
    u_ref[...] = u
    fh_ref[...] = jnp.maximum(dot_nt(wfb_ref[...], whole), 0.0).astype(BF16)
    bh_ref[...] = jnp.maximum(dot_nt(wbb_ref[...], later), 0.0).astype(BF16)
    cross = dot_tn(emb, emb)
    for j, x_ref in enumerate(xs):
        cross = cross - GAMMA * dot_tn(x_ref[0:rows, obs_pad:], emb[j * rows : (j + 1) * rows])
    return dot_tn(back, back), cross


def forward_kernel(cfg, count, *refs):
    xs, refs = refs[:count], refs[count:]
    weights, refs = refs[:7], refs[7:]
    gram_in, refs = refs[0], refs[1:]
    outs, gram_out = refs[:6], refs[6]
    gram, cross = forward_rows(cfg, xs, weights, outs)
    rank = cfg["rank"]
    gram_out[:, :rank] = gram_in[:, :rank] + gram
    gram_out[:, rank:] = gram_in[:, rank:] + cross


def last_kernel(cfg, early, count, *refs):
    groups = []
    for size in early:
        groups.append((refs[:size], refs[size : size + 6]))
        refs = refs[size + 6 :]
    xs, refs = refs[:count], refs[count:]
    weights, refs = refs[:7], refs[7:]
    gram_in, send_ref, keep_ref = refs[:3]
    outs, part_ref = refs[3:9], refs[9]
    rank, block, rows, obs_pad = cfg["rank"], cfg["block"], cfg["rows"], cfg["obs_pad"]
    group, replicas = cfg["group"], cfg["replicas"]
    factor = 1.0 / math.sqrt(cfg["total"])
    c1, c2, c3 = cfg["cols"]
    gram, cross = forward_rows(cfg, xs, weights, outs)
    gram_hi, gram_lo = split_two(gram_in[:, :rank] + gram)
    cross_hi, cross_lo = split_two(gram_in[:, rank:] + cross)
    groups.append((xs, outs))
    me = pl.multiple_of(lax.axis_index("dp") * block, ROW_TILE)
    fo = weights[2][pl.ds(me, block), :]
    bo = weights[3][pl.ds(me, block), :]
    square = jnp.zeros((1, rank), F32)
    diagonal = jnp.zeros((1, rank), F32)
    for index, (x_refs, (a_ref, later_ref, f_ref, u_ref, fh_ref, bh_ref)) in enumerate(groups):
        emb32 = f_ref[...].astype(F32)
        targets = [x_ref[0:rows, obs_pad:] for x_ref in x_refs]
        target = jnp.concatenate(targets, axis=0) if len(targets) > 1 else targets[0]
        error = emb32 - GAMMA * target.astype(F32)
        err_hi, err_lo = split_two(error)
        u = u_ref[...]
        scale = lax.rsqrt(jnp.mean(u * u, axis=-1, keepdims=True) + EPSILON)
        back = (u * scale).astype(BF16)
        back32 = back.astype(F32)
        pulled = dot_nn(err_hi, gram_hi) + (dot_nn(err_hi, gram_lo) + dot_nn(err_lo, gram_hi))
        square = square + jnp.sum(pulled * error, axis=0, keepdims=True)
        diagonal = diagonal + jnp.sum(emb32 * back32, axis=0, keepdims=True)
        d_f = (factor * (pulled / group - back32)).astype(BF16)
        pushed = dot_nn(back, cross_hi) + dot_nn(back, cross_lo)
        d_b = factor * (pushed / group - emb32)
        inner = jnp.mean(u * d_b, axis=-1, keepdims=True)
        d_u = (scale * d_b - u * (scale * scale * scale * inner)).astype(BF16)
        f_hid, b_hid = fh_ref[...], bh_ref[...]
        zero = jnp.zeros_like(f_hid)
        f_delta = jnp.where(f_hid > 0, dot_nt(fo, d_f).astype(BF16), zero)
        b_delta = jnp.where(b_hid > 0, dot_nt(bo, d_u).astype(BF16), zero)
        sums = (
            (0, c1, dot_nn(f_delta, a_ref[...])),
            (c1, c2, dot_nn(f_hid, d_f)),
            (c2, c3, dot_nn(b_delta, later_ref[...])),
            (c3, part_ref.shape[1], dot_nn(b_hid, d_u)),
        )
        for low, high, value in sums:
            if index == 0:
                part_ref[:, low:high] = value
            else:
                part_ref[:, low:high] += value
    loss = (0.5 / group) * jnp.sum(square) - jnp.sum(diagonal)
    lanes = lax.broadcasted_iota(jnp.int32, (block, LANES), 1)
    spot = cfg["loss_spot"]
    base = spot // LANES * LANES
    first = spot - base + 3 * lax.axis_index("replica")
    rest = jnp.full((block, LANES), loss, F32)
    piece_tile = part_ref[:, base : base + LANES]
    piece_tile = jnp.where(lanes >= spot - base, 0.0, piece_tile)
    for j in range(3):
        piece = rest.astype(BF16).astype(F32)
        piece_tile = jnp.where(lanes == first + j, piece, piece_tile)
        rest = rest - piece
    part_ref[:, base : base + LANES] = piece_tile
    core = lax.rem(lax.axis_index("replica"), 2)
    half = block // 2
    keep_ref[...] = part_ref[pl.ds(pl.multiple_of(core * half, ROW_TILE), half), :]
    other = pl.multiple_of((1 - core) * half, ROW_TILE)
    send_ref[...] = part_ref[pl.ds(other, half), :].astype(BF16)


def finish_kernel(cfg, one_ref, two_ref, far_ref, fs, fa, fl, fo, bs, bo, loss_ref, act_ref):
    obs, act, rank, x_pad, obs_pad = (cfg[k] for k in ("obs", "act", "rank", "x_pad", "obs_pad"))
    half = cfg["block"] // 2
    c1, c2, c3 = cfg["cols"]
    core = lax.rem(lax.axis_index("replica"), 2)
    mine32 = one_ref[...].astype(F32) + two_ref[...].astype(F32)
    mine = mine32.astype(BF16)
    far = far_ref[...]
    for start, value in ((core * half, mine), ((1 - core) * half, far)):
        here = pl.ds(pl.multiple_of(start, ROW_TILE), half)
        fs[here, :] = value[:, :obs]
        fl[here, :] = value[:, x_pad:c1]
        fo[here, :] = value[:, c1:c2]
        bs[here, :] = value[:, c2 : c2 + obs]
        bo[here, :] = value[:, c3:]
        act_ref[here, :] = value[:, obs_pad : obs_pad + LANES].astype(F32)
    fa[...] = act_ref[...].T[:act].astype(BF16)
    spot = cfg["loss_spot"]
    base = spot // LANES * LANES
    pieces = mine32[0:8, base : base + LANES]
    lanes = lax.broadcasted_iota(jnp.int32, (8, LANES), 1)
    rows = lax.broadcasted_iota(jnp.int32, (8, LANES), 0)
    ours = (lanes >= spot - base) & (lanes < spot - base + 3 * cfg["replicas"]) & (rows == 0)
    loss_ref[0, 0] = jnp.sum(jnp.where(ours, pieces, 0.0)) / cfg["total"]


def exchange(array, axis, size, bit):
    return lax.ppermute(array, axis, [(i, i ^ bit) for i in range(size)])


def shape(dims, kind):
    return jax.ShapeDtypeStruct(dims, kind)


def fast_local(
    states,
    actions,
    target_forward,
    next_index,
    latent_ids,
    latents,
    f_state,
    f_action,
    f_latent,
    f_output,
    b_state,
    b_output,
):
    size = lax.axis_size("dp")
    replicas = lax.axis_size("replica")
    rows, obs = states.shape[1:]
    act = actions.shape[2]
    zcount, rank = latents.shape
    hidden = f_state.shape[1]
    block = hidden // size
    group = rows * size
    side = round_up(act + 2, 2 * ROW_TILE)
    lane = round_up(rows, LANES)
    obs_pad = round_up(obs, LANES)
    x_pad = obs_pad + LANES
    c1 = x_pad + rank
    c2 = c1 + rank
    c3 = c2 + obs_pad
    width = c3 + rank
    cfg = dict(
        rows=rows,
        obs=obs,
        act=act,
        rank=rank,
        obs_pad=obs_pad,
        x_pad=x_pad,
        hidden=hidden,
        zcount=zcount,
        side=side,
        lane=lane,
        group=group,
        replicas=replicas,
        total=group * replicas,
        block=block,
        tile=512,
        cols=(c1, c2, c3),
        loss_spot=obs_pad + side,
    )
    params = pltpu.CompilerParams(vmem_limit_bytes=VMEM_LIMIT)
    own = pl.pallas_call(
        functools.partial(pack_kernel, cfg),
        out_shape=shape((rows + side // 2, obs_pad + rank), BF16),
        scratch_shapes=[pltpu.VMEM((side, lane), F32)],
        compiler_params=pltpu.CompilerParams(vmem_limit_bytes=8 * 1024 * 1024),
        name="pack",
    )(states, actions[0].T, next_index, latent_ids, target_forward)
    x = {0: own}
    x[2] = exchange(own, "dp", size, 2)
    x[1] = exchange(own, "dp", size, 1)
    x[6] = exchange(own, "dp", size, 6)
    x[4] = exchange(own, "dp", size, 4)
    for step in (2, 6, 4):
        x[step ^ 1] = exchange(x[step], "dp", size, 1)
    moves = jnp.pad(f_action, ((0, x_pad - obs_pad - act), (0, 0)))
    wf, wb, wfb, wbb = pl.pallas_call(
        functools.partial(weights_kernel, cfg),
        out_shape=(
            shape((x_pad + rank, hidden), BF16),
            shape((obs_pad, hidden), BF16),
            shape((block, x_pad + rank), BF16),
            shape((block, obs_pad), BF16),
        ),
        compiler_params=pltpu.CompilerParams(vmem_limit_bytes=24 * 1024 * 1024),
        cost_estimate=pl.CostEstimate(flops=0, bytes_accessed=8_000_000, transcendentals=0),
        name="weights",
    )(f_state, moves, f_latent, b_state)
    weights = (wf, wb, f_output, b_output, latents, wfb, wbb)
    row_flops = 2 * (c1 + 2 * rank + obs_pad) * hidden + 8 * rank * rank

    def kept(count):
        m = rows * count
        return (
            ((m, x_pad + rank), BF16),
            ((m, obs_pad), BF16),
            ((m, rank), BF16),
            ((m, rank), F32),
            ((block, m), BF16),
            ((block, m), BF16),
        )

    grams = jnp.zeros((rank, 2 * rank), F32)
    plan = ((0,), (1, 2), (6, 4), (3, 7))
    early = []
    for steps in plan:
        count = len(steps)
        xs = [x[step] for step in steps]
        *saved, grams = pl.pallas_call(
            functools.partial(forward_kernel, cfg, count),
            out_shape=(*(shape(*item) for item in kept(count)), shape((rank, 2 * rank), F32)),
            compiler_params=params,
            cost_estimate=pl.CostEstimate(
                flops=2 * rows * count * row_flops, bytes_accessed=8_000_000, transcendentals=0
            ),
            name="forward",
        )(*xs, *weights, grams)
        early.append((xs, saved))
    left = [x[step] for step in range(size) if all(step not in steps for steps in plan)]
    operands = []
    for xs, saved in early:
        operands += [*xs, *saved]
    send, keep = pl.pallas_call(
        functools.partial(last_kernel, cfg, [len(xs) for xs, _ in early], len(left)),
        out_shape=(shape((block // 2, width), BF16), shape((block // 2, width), F32)),
        scratch_shapes=[
            *(pltpu.VMEM(*item) for item in kept(len(left))),
            pltpu.VMEM((block, width), F32),
        ],
        compiler_params=params,
        cost_estimate=pl.CostEstimate(
            flops=4 * group * width * block, bytes_accessed=16_000_000, transcendentals=0
        ),
        name="last",
    )(*operands, *left, *weights, grams)
    got = exchange(send, "replica", replicas, 1)
    one = (keep + got.astype(F32)).astype(BF16)
    two = exchange(one, "replica", replicas, 2)
    mine = (one.astype(F32) + two.astype(F32)).astype(BF16)
    far = exchange(mine, "replica", replicas, 1)
    fs, fa, fl, fo, bs, bo, loss = pl.pallas_call(
        functools.partial(finish_kernel, cfg),
        out_shape=(
            shape((block, obs), BF16),
            shape((act, block), BF16),
            shape((block, rank), BF16),
            shape((block, rank), BF16),
            shape((block, obs), BF16),
            shape((block, rank), BF16),
            shape((1, 1), F32),
        ),
        out_specs=(
            *(pl.BlockSpec(memory_space=pltpu.VMEM) for _ in range(6)),
            pl.BlockSpec(memory_space=pltpu.SMEM),
        ),
        scratch_shapes=[pltpu.VMEM((block, LANES), F32)],
        compiler_params=pltpu.CompilerParams(vmem_limit_bytes=16 * 1024 * 1024),
        name="finish",
    )(one, two, far)
    return (fs.T, fa, fl.T, fo, bs.T, bo, loss.reshape(()))


def forward_pass(
    current, later, moves, latent_rows, f_state, f_action, f_latent, f_output, b_state, b_output
):
    f_pre = (
        jnp.dot(current, f_state, preferred_element_type=F32)
        + jnp.dot(moves, f_action, preferred_element_type=F32)
        + jnp.dot(latent_rows, f_latent, preferred_element_type=F32)
    )
    f_hidden = jnp.maximum(f_pre, 0.0).astype(BF16)
    forward_emb = jnp.dot(f_hidden, f_output, preferred_element_type=F32).astype(BF16)
    b_pre = jnp.dot(later, b_state, preferred_element_type=F32)
    b_hidden = jnp.maximum(b_pre, 0.0).astype(BF16)
    b_raw = jnp.dot(b_hidden, b_output, preferred_element_type=F32)
    b_scale = lax.rsqrt(jnp.mean(b_raw * b_raw, axis=-1, keepdims=True) + EPSILON)
    backward_emb = (b_raw * b_scale).astype(BF16)
    return (f_pre, f_hidden, forward_emb, b_pre, b_hidden, b_raw, b_scale, backward_emb)


def general_local(
    states,
    actions,
    target_forward,
    next_index,
    latent_ids,
    latents,
    f_state,
    f_action,
    f_latent,
    f_output,
    b_state,
    b_output,
):
    current = states[0]
    moves = actions[0]
    later = jnp.take(current, next_index[0], axis=0)
    latent_rows = jnp.take(latents, latent_ids[0], axis=0)
    f_pre, f_hidden, forward_emb, b_pre, b_hidden, b_raw, b_scale, backward_emb = forward_pass(
        current, later, moves, latent_rows, f_state, f_action, f_latent, f_output, b_state, b_output
    )
    group = current.shape[0] * lax.axis_size("dp")
    total = group * lax.axis_size("replica")
    factor = 1.0 / math.sqrt(total)
    forward32 = forward_emb.astype(F32)
    back32 = backward_emb.astype(F32)
    error = forward32 - GAMMA * target_forward[0].astype(F32)
    gram, cross = lax.psum(
        (
            jnp.dot(backward_emb.T, backward_emb, preferred_element_type=F32),
            jnp.dot(forward32.T, error, precision=HIGH, preferred_element_type=F32),
        ),
        "dp",
    )
    pulled = jnp.dot(error, gram, precision=HIGH, preferred_element_type=F32)
    pushed = jnp.dot(back32, cross.T, precision=HIGH, preferred_element_type=F32)
    partial_loss = 0.5 / group * jnp.sum(pulled * error) - jnp.sum(forward32 * back32)
    grad_forward = (factor * (pulled / group - back32)).astype(BF16)
    grad_backward = factor * (pushed / group - forward32)
    inner = jnp.mean(b_raw * grad_backward, axis=-1, keepdims=True)
    grad_raw = (b_scale * grad_backward - b_raw * b_scale * b_scale * b_scale * inner).astype(BF16)
    part_bo = jnp.dot(b_hidden.T, grad_raw, preferred_element_type=F32)
    b_back = jnp.dot(grad_raw, b_output.T, preferred_element_type=F32)
    b_delta = jnp.where(b_pre > 0, b_back, 0.0).astype(BF16)
    part_bs = jnp.dot(later.T, b_delta, preferred_element_type=F32)
    part_fo = jnp.dot(f_hidden.T, grad_forward, preferred_element_type=F32)
    f_back = jnp.dot(grad_forward, f_output.T, preferred_element_type=F32)
    f_delta = jnp.where(f_pre > 0, f_back, 0.0).astype(BF16)
    part_fs = jnp.dot(current.T, f_delta, preferred_element_type=F32)
    part_fa = jnp.dot(moves.T, f_delta, preferred_element_type=F32)
    part_fl = jnp.dot(latent_rows.T, f_delta, preferred_element_type=F32)
    places = (1, 1, 1, 0, 1, 0)
    parts = (part_fs, part_fa, part_fl, part_fo, part_bs, part_bo)
    shares = tuple(
        lax.psum_scatter(part, "dp", scatter_dimension=place, tiled=True)
        for part, place in zip(parts, places)
    )
    summed = lax.psum(shares, "replica")
    loss_sum = lax.psum(partial_loss, ("dp", "replica"))
    return (*(item.astype(BF16) for item in summed), loss_sum / total)


def local(*args):
    size, replicas = lax.axis_size("dp"), lax.axis_size("replica")
    rows, hidden = args[0].shape[1], args[6].shape[1]
    fits = size == 8 and replicas == 4 and rows * size <= KERNEL_GROUP_LIMIT
    block = hidden // size
    whole = rows % ROW_TILE == 0 and hidden % (size * 64) == 0 and hidden % 512 == 0
    whole = whole and LANES < block <= 2 * LANES - 64 and args[6].shape[0] % 8 == 0
    exact = rows <= 256 and args[5].shape[0] <= 256
    return (fast_local if fits and whole and exact else general_local)(*args)


def solution(mesh):
    in_specs = (
        P("replica", "dp", None),
        P("replica", "dp", None),
        P("replica", "dp", None),
        P("replica", "dp"),
        P("replica", "dp"),
        P(),
        P(),
        P(),
        P(),
        P(),
        P(),
        P(),
    )
    out_specs = (
        P(None, "dp"),
        P(None, "dp"),
        P(None, "dp"),
        P("dp", None),
        P(None, "dp"),
        P("dp", None),
        P(),
    )
    return jax.shard_map(local, mesh=mesh, in_specs=in_specs, out_specs=out_specs, check_vma=False)
```

```python
import functools
import math

import jax
import jax.numpy as jnp
from jax import lax
from jax.experimental import pallas as pl
from jax.experimental.pallas import tpu as pltpu
from jax.sharding import PartitionSpec as P

GAMMA = 0.98
EPSILON = 1e-06
HIGH = lax.Precision.HIGHEST
BF16 = jnp.bfloat16
F32 = jnp.float32
LANES = 128
ROW_TILE = 16
VMEM_LIMIT = 56 * 1024 * 1024
KERNEL_GROUP_LIMIT = 2048


def round_up(value, unit):
    return -(-value // unit) * unit


def dot_nn(left, right):
    return lax.dot_general(left, right, (((1,), (0,)), ((), ())), preferred_element_type=F32)


def dot_nt(left, right):
    return lax.dot_general(left, right, (((1,), (1,)), ((), ())), preferred_element_type=F32)


def dot_tn(left, right):
    return lax.dot_general(left, right, (((0,), (0,)), ((), ())), preferred_element_type=F32)


def split_two(value):
    high = value.astype(BF16)
    return high, (value - high.astype(F32)).astype(BF16)


def pack_kernel(cfg, state_ref, move_ref, next_ref, latent_ref, target_ref, out_ref, side_ref):
    rows, obs, act, obs_pad, side = (cfg[k] for k in ("rows", "obs", "act", "obs_pad", "side"))
    lane = side_ref.shape[1]
    side_ref[...] = jnp.zeros_like(side_ref)
    side_ref[0:act, 0:rows] = move_ref[...].astype(F32)
    side_ref[act : act + 1, 0:rows] = next_ref[...].astype(F32)
    side_ref[act + 1 : act + 2, 0:rows] = latent_ref[...].astype(F32)
    gap = jnp.zeros((rows, obs_pad - obs), BF16)
    out_ref[0:rows, 0:obs_pad] = jnp.concatenate([state_ref[0], gap], axis=1)
    out_ref[0:rows, obs_pad:] = target_ref[0]
    half = side // 2
    out_ref[rows:, :] = jnp.zeros((half, out_ref.shape[1]), BF16)
    out_ref[rows:, 0:lane] = side_ref[0:half, :].astype(BF16)
    out_ref[rows:, lane : 2 * lane] = side_ref[half:side, :].astype(BF16)


def weights_kernel(cfg, fs_ref, fa_ref, fl_ref, bs_ref, wf_ref, wb_ref, wfb_ref, wbb_ref):
    obs, obs_pad, x_pad = cfg["obs"], cfg["obs_pad"], cfg["x_pad"]
    hidden, block, act = cfg["hidden"], cfg["block"], cfg["act"]
    gap = jnp.zeros((obs_pad - obs, hidden), BF16)
    wf_ref[0:obs_pad, :] = jnp.concatenate([fs_ref[...], gap], axis=0)
    wf_ref[obs_pad:x_pad, :] = jnp.zeros((x_pad - obs_pad, hidden), BF16)
    wf_ref[obs_pad : obs_pad + act, :] = fa_ref[...]
    wf_ref[x_pad:, :] = fl_ref[...]
    wb_ref[...] = jnp.concatenate([bs_ref[...], gap], axis=0)
    me = lax.axis_index("dp")
    start = me * block
    base = pl.multiple_of(start // LANES * LANES, LANES)
    odd = lax.rem(me, 2) == 1
    span = pl.ds(base, 2 * LANES)

    def pick(ref):
        near = ref[:, span].astype(F32).T
        return jnp.where(odd, near[2 * LANES - block :], near[:block]).astype(BF16)

    wfb_ref[...] = pick(wf_ref)
    wbb_ref[...] = pick(wb_ref)


def forward_rows(cfg, xs, weights, outs):
    wf_ref, wb_ref, fo_ref, bo_ref, lat_ref, wfb_ref, wbb_ref = weights
    a_ref, later_ref, f_ref, u_ref, fh_ref, bh_ref = outs
    rows, act, rank, side = cfg["rows"], cfg["act"], cfg["rank"], cfg["side"]
    obs_pad, x_pad, hidden, zcount = cfg["obs_pad"], cfg["x_pad"], cfg["hidden"], cfg["zcount"]
    tile, lane = cfg["tile"], cfg["lane"]
    m = rows * len(xs)
    half = side // 2
    row_spots = lax.broadcasted_iota(jnp.int32, (rows, rows), 1).astype(F32)
    spots = lax.broadcasted_iota(jnp.int32, (rows, zcount), 1).astype(F32)
    blank = jnp.zeros((rows, x_pad - obs_pad - side), BF16)
    for j, x_ref in enumerate(xs):
        here = slice(j * rows, (j + 1) * rows)
        few = jnp.concatenate(
            [x_ref[rows:, 0:lane].astype(F32), x_ref[rows:, lane : 2 * lane].astype(F32)], axis=0
        ).T[:rows]
        near = x_ref[0:rows, 0:obs_pad]
        picks = jnp.where(few[:, act + 1 : act + 2] == spots, 1.0, 0.0).astype(BF16)
        hot = jnp.where(few[:, act : act + 1] == row_spots, 1.0, 0.0).astype(BF16)
        a_ref[here, 0:obs_pad] = near
        a_ref[here, obs_pad:x_pad] = jnp.concatenate([few.astype(BF16), blank], axis=1)
        a_ref[here, x_pad:] = dot_nn(picks, lat_ref[...]).astype(BF16)
        later_ref[here, :] = dot_nn(hot, near).astype(BF16)
    whole = a_ref[...]
    later = later_ref[...]
    f_acc = jnp.zeros((m, rank), F32)
    u = jnp.zeros((m, rank), F32)
    for n in range(0, hidden, tile):
        h = jnp.maximum(dot_nn(whole, wf_ref[:, n : n + tile]), 0.0).astype(BF16)
        f_acc = f_acc + dot_nn(h, fo_ref[n : n + tile, :])
        g = jnp.maximum(dot_nn(later, wb_ref[:, n : n + tile]), 0.0).astype(BF16)
        u = u + dot_nn(g, bo_ref[n : n + tile, :])
    emb = f_acc.astype(BF16)
    back = (u * lax.rsqrt(jnp.mean(u * u, axis=-1, keepdims=True) + EPSILON)).astype(BF16)
    f_ref[...] = emb
    u_ref[...] = u
    fh_ref[...] = jnp.maximum(dot_nt(wfb_ref[...], whole), 0.0).astype(BF16)
    bh_ref[...] = jnp.maximum(dot_nt(wbb_ref[...], later), 0.0).astype(BF16)
    cross = dot_tn(emb, emb)
    for j, x_ref in enumerate(xs):
        cross = cross - GAMMA * dot_tn(x_ref[0:rows, obs_pad:], emb[j * rows : (j + 1) * rows])
    return dot_tn(back, back), cross


def forward_kernel(cfg, count, first, *refs):
    xs, refs = refs[:count], refs[count:]
    weights, refs = refs[:7], refs[7:]
    if not first:
        gram_in, refs = refs[0], refs[1:]
    outs, gram_out = refs[:6], refs[6]
    gram, cross = forward_rows(cfg, xs, weights, outs)
    rank = cfg["rank"]
    gram_out[:, :rank] = gram if first else gram_in[:, :rank] + gram
    gram_out[:, rank:] = cross if first else gram_in[:, rank:] + cross


def last_kernel(cfg, early, count, *refs):
    groups = []
    for size in early:
        groups.append((refs[:size], refs[size : size + 6]))
        refs = refs[size + 6 :]
    xs, refs = refs[:count], refs[count:]
    weights, refs = refs[:7], refs[7:]
    gram_in, send_ref, keep_ref = refs[:3]
    outs, part_ref = refs[3:9], refs[9]
    rank, block, rows, obs_pad = cfg["rank"], cfg["block"], cfg["rows"], cfg["obs_pad"]
    group, replicas = cfg["group"], cfg["replicas"]
    factor = 1.0 / math.sqrt(cfg["total"])
    c1, c2, c3 = cfg["cols"]
    gram, cross = forward_rows(cfg, xs, weights, outs)
    gram_hi, gram_lo = split_two(gram_in[:, :rank] + gram)
    cross_hi, cross_lo = split_two(gram_in[:, rank:] + cross)
    groups.append((xs, outs))
    me = pl.multiple_of(lax.axis_index("dp") * block, ROW_TILE)
    fo = weights[2][pl.ds(me, block), :]
    bo = weights[3][pl.ds(me, block), :]
    square = jnp.zeros((1, rank), F32)
    diagonal = jnp.zeros((1, rank), F32)
    for index, (x_refs, (a_ref, later_ref, f_ref, u_ref, fh_ref, bh_ref)) in enumerate(groups):
        emb32 = f_ref[...].astype(F32)
        targets = [x_ref[0:rows, obs_pad:] for x_ref in x_refs]
        target = jnp.concatenate(targets, axis=0) if len(targets) > 1 else targets[0]
        error = emb32 - GAMMA * target.astype(F32)
        err_hi, err_lo = split_two(error)
        u = u_ref[...]
        scale = lax.rsqrt(jnp.mean(u * u, axis=-1, keepdims=True) + EPSILON)
        back = (u * scale).astype(BF16)
        back32 = back.astype(F32)
        pulled = dot_nn(err_hi, gram_hi) + (dot_nn(err_hi, gram_lo) + dot_nn(err_lo, gram_hi))
        square = square + jnp.sum(pulled * error, axis=0, keepdims=True)
        diagonal = diagonal + jnp.sum(emb32 * back32, axis=0, keepdims=True)
        d_f = (factor * (pulled / group - back32)).astype(BF16)
        pushed = dot_nn(back, cross_hi) + dot_nn(back, cross_lo)
        d_b = factor * (pushed / group - emb32)
        inner = jnp.mean(u * d_b, axis=-1, keepdims=True)
        d_u = (scale * d_b - u * (scale * scale * scale * inner)).astype(BF16)
        f_hid, b_hid = fh_ref[...], bh_ref[...]
        zero = jnp.zeros_like(f_hid)
        f_delta = jnp.where(f_hid > 0, dot_nt(fo, d_f).astype(BF16), zero)
        b_delta = jnp.where(b_hid > 0, dot_nt(bo, d_u).astype(BF16), zero)
        sums = (
            (0, c1, dot_nn(f_delta, a_ref[...])),
            (c1, c2, dot_nn(f_hid, d_f)),
            (c2, c3, dot_nn(b_delta, later_ref[...])),
            (c3, part_ref.shape[1], dot_nn(b_hid, d_u)),
        )
        for low, high, value in sums:
            if index == 0:
                part_ref[:, low:high] = value
            else:
                part_ref[:, low:high] += value
    loss = (0.5 / group) * jnp.sum(square) - jnp.sum(diagonal)
    lanes = lax.broadcasted_iota(jnp.int32, (block, LANES), 1)
    spot = cfg["loss_spot"]
    base = spot // LANES * LANES
    first = spot - base + 3 * lax.axis_index("replica")
    rest = jnp.full((block, LANES), loss, F32)
    piece_tile = part_ref[:, base : base + LANES]
    piece_tile = jnp.where(lanes >= spot - base, 0.0, piece_tile)
    for j in range(3):
        piece = rest.astype(BF16).astype(F32)
        piece_tile = jnp.where(lanes == first + j, piece, piece_tile)
        rest = rest - piece
    part_ref[:, base : base + LANES] = piece_tile
    core = lax.rem(lax.axis_index("replica"), 2)
    half = block // 2
    keep_ref[...] = part_ref[pl.ds(pl.multiple_of(core * half, ROW_TILE), half), :]
    other = pl.multiple_of((1 - core) * half, ROW_TILE)
    send_ref[...] = part_ref[pl.ds(other, half), :].astype(BF16)


def finish_kernel(cfg, one_ref, two_ref, far_ref, fs, fa, fl, fo, bs, bo, loss_ref, act_ref):
    obs, act, rank, x_pad, obs_pad = (cfg[k] for k in ("obs", "act", "rank", "x_pad", "obs_pad"))
    half = cfg["block"] // 2
    c1, c2, c3 = cfg["cols"]
    core = lax.rem(lax.axis_index("replica"), 2)
    mine32 = one_ref[...].astype(F32) + two_ref[...].astype(F32)
    mine = mine32.astype(BF16)
    far = far_ref[...]
    for start, value in ((core * half, mine), ((1 - core) * half, far)):
        here = pl.ds(pl.multiple_of(start, ROW_TILE), half)
        fs[here, :] = value[:, :obs]
        fl[here, :] = value[:, x_pad:c1]
        fo[here, :] = value[:, c1:c2]
        bs[here, :] = value[:, c2 : c2 + obs]
        bo[here, :] = value[:, c3:]
        act_ref[here, :] = value[:, obs_pad : obs_pad + LANES].astype(F32)
    fa[...] = act_ref[...].T[:act].astype(BF16)
    spot = cfg["loss_spot"]
    base = spot // LANES * LANES
    pieces = mine32[0:8, base : base + LANES]
    lanes = lax.broadcasted_iota(jnp.int32, (8, LANES), 1)
    rows = lax.broadcasted_iota(jnp.int32, (8, LANES), 0)
    ours = (lanes >= spot - base) & (lanes < spot - base + 3 * cfg["replicas"]) & (rows == 0)
    loss_ref[0, 0] = jnp.sum(jnp.where(ours, pieces, 0.0)) / cfg["total"]


def exchange(array, axis, size, bit):
    return lax.ppermute(array, axis, [(i, i ^ bit) for i in range(size)])


def shape(dims, kind):
    return jax.ShapeDtypeStruct(dims, kind)


def fast_local(
    states,
    actions,
    target_forward,
    next_index,
    latent_ids,
    latents,
    f_state,
    f_action,
    f_latent,
    f_output,
    b_state,
    b_output,
):
    size = lax.axis_size("dp")
    replicas = lax.axis_size("replica")
    rows, obs = states.shape[1:]
    act = actions.shape[2]
    zcount, rank = latents.shape
    hidden = f_state.shape[1]
    block = hidden // size
    group = rows * size
    side = round_up(act + 2, 2 * ROW_TILE)
    lane = round_up(rows, LANES)
    obs_pad = round_up(obs, LANES)
    x_pad = obs_pad + LANES
    c1 = x_pad + rank
    c2 = c1 + rank
    c3 = c2 + obs_pad
    width = c3 + rank
    cfg = dict(
        rows=rows,
        obs=obs,
        act=act,
        rank=rank,
        obs_pad=obs_pad,
        x_pad=x_pad,
        hidden=hidden,
        zcount=zcount,
        side=side,
        lane=lane,
        group=group,
        replicas=replicas,
        total=group * replicas,
        block=block,
        tile=512,
        cols=(c1, c2, c3),
        loss_spot=obs_pad + side,
    )
    params = pltpu.CompilerParams(vmem_limit_bytes=20 * 1024 * 1024)
    last_params = pltpu.CompilerParams(vmem_limit_bytes=28 * 1024 * 1024)
    own = pl.pallas_call(
        functools.partial(pack_kernel, cfg),
        out_shape=shape((rows + side // 2, obs_pad + rank), BF16),
        scratch_shapes=[pltpu.VMEM((side, lane), F32)],
        compiler_params=pltpu.CompilerParams(vmem_limit_bytes=VMEM_LIMIT),
        name="pack",
    )(states, actions[0].T, next_index, latent_ids, target_forward)
    x = {0: own}
    for step in (4, 6, 1, 2):
        x[step] = exchange(own, "dp", size, step)
    wf, wb, wfb, wbb = pl.pallas_call(
        functools.partial(weights_kernel, cfg),
        out_shape=(
            shape((x_pad + rank, hidden), BF16),
            shape((obs_pad, hidden), BF16),
            shape((block, x_pad + rank), BF16),
            shape((block, obs_pad), BF16),
        ),
        compiler_params=pltpu.CompilerParams(vmem_limit_bytes=24 * 1024 * 1024),
        cost_estimate=pl.CostEstimate(flops=0, bytes_accessed=8_000_000, transcendentals=0),
        name="weights",
    )(f_state, f_action, f_latent, b_state)
    weights = (wf, wb, f_output, b_output, latents, wfb, wbb)
    row_flops = 2 * (c1 + 2 * rank + obs_pad) * hidden + 8 * rank * rank

    def kept(count):
        m = rows * count
        return (
            ((m, x_pad + rank), BF16),
            ((m, obs_pad), BF16),
            ((m, rank), BF16),
            ((m, rank), F32),
            ((block, m), BF16),
            ((block, m), BF16),
        )

    grams = ()
    plan = ((0,), (1, 2), (6, 4), (3, 7))
    early = []
    for steps in plan:
        count = len(steps)
        if steps == (1, 2):
            x[3] = exchange(x[2], "dp", size, 1)
        if steps == (6, 4):
            far, near, grams = lax.optimization_barrier((x[6], x[4], grams))
            x[5] = exchange(near, "dp", size, 1)
            x[7] = exchange(far, "dp", size, 1)
        xs = [x[step] for step in steps]
        *saved, total_grams = pl.pallas_call(
            functools.partial(forward_kernel, cfg, count, not early),
            out_shape=(*(shape(*item) for item in kept(count)), shape((rank, 2 * rank), F32)),
            compiler_params=params,
            cost_estimate=pl.CostEstimate(
                flops=2 * rows * count * row_flops, bytes_accessed=8_000_000, transcendentals=0
            ),
            name="forward",
        )(*xs, *weights, *grams)
        grams = (total_grams,)
        early.append((xs, saved))
    left = [x[step] for step in range(size) if all(step not in steps for steps in plan)]
    operands = []
    for xs, saved in early:
        operands += [*xs, *saved]
    send, keep = pl.pallas_call(
        functools.partial(last_kernel, cfg, [len(xs) for xs, _ in early], len(left)),
        out_shape=(shape((block // 2, width), BF16), shape((block // 2, width), F32)),
        scratch_shapes=[
            *(pltpu.VMEM(*item) for item in kept(len(left))),
            pltpu.VMEM((block, width), F32),
        ],
        compiler_params=last_params,
        cost_estimate=pl.CostEstimate(
            flops=4 * group * width * block, bytes_accessed=16_000_000, transcendentals=0
        ),
        name="last",
    )(*operands, *left, *weights, *grams)
    got = exchange(send, "replica", replicas, 1)
    one = (keep + got.astype(F32)).astype(BF16)
    two = exchange(one, "replica", replicas, 2)
    mine = (one.astype(F32) + two.astype(F32)).astype(BF16)
    far = exchange(mine, "replica", replicas, 1)
    fs, fa, fl, fo, bs, bo, loss = pl.pallas_call(
        functools.partial(finish_kernel, cfg),
        out_shape=(
            shape((block, obs), BF16),
            shape((act, block), BF16),
            shape((block, rank), BF16),
            shape((block, rank), BF16),
            shape((block, obs), BF16),
            shape((block, rank), BF16),
            shape((1, 1), F32),
        ),
        out_specs=(
            *(pl.BlockSpec(memory_space=pltpu.VMEM) for _ in range(6)),
            pl.BlockSpec(memory_space=pltpu.SMEM),
        ),
        scratch_shapes=[pltpu.VMEM((block, LANES), F32)],
        compiler_params=pltpu.CompilerParams(vmem_limit_bytes=16 * 1024 * 1024),
        name="finish",
    )(one, two, far)
    return (fs.T, fa, fl.T, fo, bs.T, bo, loss.reshape(()))


def forward_pass(
    current, later, moves, latent_rows, f_state, f_action, f_latent, f_output, b_state, b_output
):
    f_pre = (
        jnp.dot(current, f_state, preferred_element_type=F32)
        + jnp.dot(moves, f_action, preferred_element_type=F32)
        + jnp.dot(latent_rows, f_latent, preferred_element_type=F32)
    )
    f_hidden = jnp.maximum(f_pre, 0.0).astype(BF16)
    forward_emb = jnp.dot(f_hidden, f_output, preferred_element_type=F32).astype(BF16)
    b_pre = jnp.dot(later, b_state, preferred_element_type=F32)
    b_hidden = jnp.maximum(b_pre, 0.0).astype(BF16)
    b_raw = jnp.dot(b_hidden, b_output, preferred_element_type=F32)
    b_scale = lax.rsqrt(jnp.mean(b_raw * b_raw, axis=-1, keepdims=True) + EPSILON)
    backward_emb = (b_raw * b_scale).astype(BF16)
    return (f_pre, f_hidden, forward_emb, b_pre, b_hidden, b_raw, b_scale, backward_emb)


def general_local(
    states,
    actions,
    target_forward,
    next_index,
    latent_ids,
    latents,
    f_state,
    f_action,
    f_latent,
    f_output,
    b_state,
    b_output,
):
    current = states[0]
    moves = actions[0]
    later = jnp.take(current, next_index[0], axis=0)
    latent_rows = jnp.take(latents, latent_ids[0], axis=0)
    f_pre, f_hidden, forward_emb, b_pre, b_hidden, b_raw, b_scale, backward_emb = forward_pass(
        current, later, moves, latent_rows, f_state, f_action, f_latent, f_output, b_state, b_output
    )
    group = current.shape[0] * lax.axis_size("dp")
    total = group * lax.axis_size("replica")
    factor = 1.0 / math.sqrt(total)
    forward32 = forward_emb.astype(F32)
    back32 = backward_emb.astype(F32)
    error = forward32 - GAMMA * target_forward[0].astype(F32)
    gram, cross = lax.psum(
        (
            jnp.dot(backward_emb.T, backward_emb, preferred_element_type=F32),
            jnp.dot(forward32.T, error, precision=HIGH, preferred_element_type=F32),
        ),
        "dp",
    )
    pulled = jnp.dot(error, gram, precision=HIGH, preferred_element_type=F32)
    pushed = jnp.dot(back32, cross.T, precision=HIGH, preferred_element_type=F32)
    partial_loss = 0.5 / group * jnp.sum(pulled * error) - jnp.sum(forward32 * back32)
    grad_forward = (factor * (pulled / group - back32)).astype(BF16)
    grad_backward = factor * (pushed / group - forward32)
    inner = jnp.mean(b_raw * grad_backward, axis=-1, keepdims=True)
    grad_raw = (b_scale * grad_backward - b_raw * b_scale * b_scale * b_scale * inner).astype(BF16)
    part_bo = jnp.dot(b_hidden.T, grad_raw, preferred_element_type=F32)
    b_back = jnp.dot(grad_raw, b_output.T, preferred_element_type=F32)
    b_delta = jnp.where(b_pre > 0, b_back, 0.0).astype(BF16)
    part_bs = jnp.dot(later.T, b_delta, preferred_element_type=F32)
    part_fo = jnp.dot(f_hidden.T, grad_forward, preferred_element_type=F32)
    f_back = jnp.dot(grad_forward, f_output.T, preferred_element_type=F32)
    f_delta = jnp.where(f_pre > 0, f_back, 0.0).astype(BF16)
    part_fs = jnp.dot(current.T, f_delta, preferred_element_type=F32)
    part_fa = jnp.dot(moves.T, f_delta, preferred_element_type=F32)
    part_fl = jnp.dot(latent_rows.T, f_delta, preferred_element_type=F32)
    places = (1, 1, 1, 0, 1, 0)
    parts = (part_fs, part_fa, part_fl, part_fo, part_bs, part_bo)
    shares = tuple(
        lax.psum_scatter(part, "dp", scatter_dimension=place, tiled=True)
        for part, place in zip(parts, places)
    )
    summed = lax.psum(shares, "replica")
    loss_sum = lax.psum(partial_loss, ("dp", "replica"))
    return (*(item.astype(BF16) for item in summed), loss_sum / total)


def local(*args):
    size, replicas = lax.axis_size("dp"), lax.axis_size("replica")
    rows, hidden = args[0].shape[1], args[6].shape[1]
    fits = size == 8 and replicas == 4 and rows * size <= KERNEL_GROUP_LIMIT
    block = hidden // size
    whole = rows % ROW_TILE == 0 and hidden % (size * 64) == 0 and hidden % 512 == 0
    whole = whole and LANES < block <= 2 * LANES - 64 and args[6].shape[0] % 8 == 0
    exact = rows <= 256 and args[5].shape[0] <= 256
    return (fast_local if fits and whole and exact else general_local)(*args)


def solution(mesh):
    in_specs = (
        P("replica", "dp", None),
        P("replica", "dp", None),
        P("replica", "dp", None),
        P("replica", "dp"),
        P("replica", "dp"),
        P(),
        P(),
        P(),
        P(),
        P(),
        P(),
        P(),
    )
    out_specs = (
        P(None, "dp"),
        P(None, "dp"),
        P(None, "dp"),
        P("dp", None),
        P(None, "dp"),
        P("dp", None),
        P(),
    )
    return jax.shard_map(local, mesh=mesh, in_specs=in_specs, out_specs=out_specs, check_vma=False)
```

```python
import functools
import math

import jax
import jax.numpy as jnp
from jax import lax
from jax.experimental import pallas as pl
from jax.experimental.pallas import tpu as pltpu
from jax.sharding import PartitionSpec as P

GAMMA = 0.98
EPSILON = 1e-06
HIGH = lax.Precision.HIGHEST
BF16 = jnp.bfloat16
F32 = jnp.float32
LANES = 128
ROW_TILE = 16
VMEM_LIMIT = 56 * 1024 * 1024
KERNEL_GROUP_LIMIT = 2048


def round_up(value, unit):
    return -(-value // unit) * unit


def dot_nn(left, right):
    return lax.dot_general(left, right, (((1,), (0,)), ((), ())), preferred_element_type=F32)


def dot_nt(left, right):
    return lax.dot_general(left, right, (((1,), (1,)), ((), ())), preferred_element_type=F32)


def dot_tn(left, right):
    return lax.dot_general(left, right, (((0,), (0,)), ((), ())), preferred_element_type=F32)


def split_two(value):
    high = value.astype(BF16)
    return high, (value - high.astype(F32)).astype(BF16)


def pack_kernel(cfg, state_ref, move_ref, next_ref, latent_ref, target_ref, out_ref, side_ref):
    rows, obs, act, obs_pad, side = (cfg[k] for k in ("rows", "obs", "act", "obs_pad", "side"))
    lane = side_ref.shape[1]
    side_ref[...] = jnp.zeros_like(side_ref)
    side_ref[0:act, 0:rows] = move_ref[...].astype(F32)
    side_ref[act : act + 1, 0:rows] = next_ref[...].astype(F32)
    side_ref[act + 1 : act + 2, 0:rows] = latent_ref[...].astype(F32)
    gap = jnp.zeros((rows, obs_pad - obs), BF16)
    out_ref[0:rows, 0:obs_pad] = jnp.concatenate([state_ref[0], gap], axis=1)
    out_ref[0:rows, obs_pad:] = target_ref[0]
    half = side // 2
    out_ref[rows:, :] = jnp.zeros((half, out_ref.shape[1]), BF16)
    out_ref[rows:, 0:lane] = side_ref[0:half, :].astype(BF16)
    out_ref[rows:, lane : 2 * lane] = side_ref[half:side, :].astype(BF16)


def weights_kernel(cfg, fs_hbm, fa_hbm, fl_hbm, bs_hbm, *refs):
    obs, obs_pad, x_pad = cfg["obs"], cfg["obs_pad"], cfg["x_pad"]
    hidden, block, act = cfg["hidden"], cfg["block"], cfg["act"]
    wf_ref, wb_ref, wfb_ref, wbb_ref, fs_ref, fa_ref, fl_ref, bs_ref, sems = refs
    pairs = ((fs_hbm, fs_ref), (bs_hbm, bs_ref), (fl_hbm, fl_ref), (fa_hbm, fa_ref))
    copies = [pltpu.make_async_copy(a, b, sems.at[i]) for i, (a, b) in enumerate(pairs)]
    for copy in copies:
        copy.start()
    gap = jnp.zeros((obs_pad - obs, hidden), BF16)
    wf_ref[obs_pad:x_pad, :] = jnp.zeros((x_pad - obs_pad, hidden), BF16)
    copies[0].wait()
    wf_ref[0:obs_pad, :] = jnp.concatenate([fs_ref[...], gap], axis=0)
    copies[1].wait()
    wb_ref[...] = jnp.concatenate([bs_ref[...], gap], axis=0)
    copies[2].wait()
    wf_ref[x_pad:, :] = fl_ref[...]
    copies[3].wait()
    wf_ref[obs_pad : obs_pad + act, :] = fa_ref[...]
    me = lax.axis_index("dp")
    start = me * block
    base = pl.multiple_of(start // LANES * LANES, LANES)
    odd = lax.rem(me, 2) == 1
    span = pl.ds(base, 2 * LANES)

    def pick(ref):
        near = ref[:, span].astype(F32).T
        return jnp.where(odd, near[2 * LANES - block :], near[:block]).astype(BF16)

    wfb_ref[...] = pick(wf_ref)
    wbb_ref[...] = pick(wb_ref)


def forward_rows(cfg, xs, weights, outs):
    wf_ref, wb_ref, fo_ref, bo_ref, lat_ref, wfb_ref, wbb_ref = weights
    a_ref, later_ref, f_ref, u_ref, fh_ref, bh_ref = outs
    rows, act, rank, side = cfg["rows"], cfg["act"], cfg["rank"], cfg["side"]
    obs_pad, x_pad, hidden, zcount = cfg["obs_pad"], cfg["x_pad"], cfg["hidden"], cfg["zcount"]
    tile, lane = cfg["tile"], cfg["lane"]
    m = rows * len(xs)
    half = side // 2
    row_spots = lax.broadcasted_iota(jnp.int32, (rows, rows), 1).astype(F32)
    spots = lax.broadcasted_iota(jnp.int32, (rows, zcount), 1).astype(F32)
    blank = jnp.zeros((rows, x_pad - obs_pad - side), BF16)
    for j, x_ref in enumerate(xs):
        here = slice(j * rows, (j + 1) * rows)
        few = jnp.concatenate(
            [x_ref[rows:, 0:lane].astype(F32), x_ref[rows:, lane : 2 * lane].astype(F32)], axis=0
        ).T[:rows]
        near = x_ref[0:rows, 0:obs_pad]
        picks = jnp.where(few[:, act + 1 : act + 2] == spots, 1.0, 0.0).astype(BF16)
        hot = jnp.where(few[:, act : act + 1] == row_spots, 1.0, 0.0).astype(BF16)
        a_ref[here, 0:obs_pad] = near
        a_ref[here, obs_pad:x_pad] = jnp.concatenate([few.astype(BF16), blank], axis=1)
        a_ref[here, x_pad:] = dot_nn(picks, lat_ref[...]).astype(BF16)
        later_ref[here, :] = dot_nn(hot, near).astype(BF16)
    whole = a_ref[...]
    later = later_ref[...]
    f_acc = jnp.zeros((m, rank), F32)
    u = jnp.zeros((m, rank), F32)
    for n in range(0, hidden, tile):
        h = jnp.maximum(dot_nn(whole, wf_ref[:, n : n + tile]), 0.0).astype(BF16)
        f_acc = f_acc + dot_nn(h, fo_ref[n : n + tile, :])
        g = jnp.maximum(dot_nn(later, wb_ref[:, n : n + tile]), 0.0).astype(BF16)
        u = u + dot_nn(g, bo_ref[n : n + tile, :])
    emb = f_acc.astype(BF16)
    back = (u * lax.rsqrt(jnp.mean(u * u, axis=-1, keepdims=True) + EPSILON)).astype(BF16)
    f_ref[...] = emb
    u_ref[...] = u
    fh_ref[...] = jnp.maximum(dot_nt(wfb_ref[...], whole), 0.0).astype(BF16)
    bh_ref[...] = jnp.maximum(dot_nt(wbb_ref[...], later), 0.0).astype(BF16)
    cross = dot_tn(emb, emb)
    for j, x_ref in enumerate(xs):
        cross = cross - GAMMA * dot_tn(x_ref[0:rows, obs_pad:], emb[j * rows : (j + 1) * rows])
    return dot_tn(back, back), cross


def forward_kernel(cfg, count, first, *refs):
    xs, refs = refs[:count], refs[count:]
    weights, refs = refs[:7], refs[7:]
    if not first:
        gram_in, refs = refs[0], refs[1:]
    outs, gram_out = refs[:6], refs[6]
    gram, cross = forward_rows(cfg, xs, weights, outs)
    rank = cfg["rank"]
    gram_out[:, :rank] = gram if first else gram_in[:, :rank] + gram
    gram_out[:, rank:] = cross if first else gram_in[:, rank:] + cross


def last_kernel(cfg, early, count, *refs):
    groups = []
    for size in early:
        groups.append((refs[:size], refs[size : size + 6]))
        refs = refs[size + 6 :]
    xs, refs = refs[:count], refs[count:]
    weights, refs = refs[:7], refs[7:]
    gram_in, send_ref, keep_ref = refs[:3]
    outs, part_ref = refs[3:9], refs[9]
    rank, block, rows, obs_pad = cfg["rank"], cfg["block"], cfg["rows"], cfg["obs_pad"]
    group, replicas = cfg["group"], cfg["replicas"]
    factor = 1.0 / math.sqrt(cfg["total"])
    c1, c2, c3 = cfg["cols"]
    gram, cross = forward_rows(cfg, xs, weights, outs)
    gram_hi, gram_lo = split_two(gram_in[:, :rank] + gram)
    cross_hi, cross_lo = split_two(gram_in[:, rank:] + cross)
    groups.append((xs, outs))
    me = pl.multiple_of(lax.axis_index("dp") * block, ROW_TILE)
    fo = weights[2][pl.ds(me, block), :]
    bo = weights[3][pl.ds(me, block), :]
    square = jnp.zeros((1, rank), F32)
    diagonal = jnp.zeros((1, rank), F32)
    for index, (x_refs, (a_ref, later_ref, f_ref, u_ref, fh_ref, bh_ref)) in enumerate(groups):
        emb32 = f_ref[...].astype(F32)
        targets = [x_ref[0:rows, obs_pad:] for x_ref in x_refs]
        target = jnp.concatenate(targets, axis=0) if len(targets) > 1 else targets[0]
        error = emb32 - GAMMA * target.astype(F32)
        err_hi, err_lo = split_two(error)
        u = u_ref[...]
        scale = lax.rsqrt(jnp.mean(u * u, axis=-1, keepdims=True) + EPSILON)
        back = (u * scale).astype(BF16)
        back32 = back.astype(F32)
        pulled = dot_nn(err_hi, gram_hi) + (dot_nn(err_hi, gram_lo) + dot_nn(err_lo, gram_hi))
        square = square + jnp.sum(pulled * error, axis=0, keepdims=True)
        diagonal = diagonal + jnp.sum(emb32 * back32, axis=0, keepdims=True)
        d_f = (factor * (pulled / group - back32)).astype(BF16)
        pushed = dot_nn(back, cross_hi) + dot_nn(back, cross_lo)
        d_b = factor * (pushed / group - emb32)
        inner = jnp.mean(u * d_b, axis=-1, keepdims=True)
        d_u = (scale * d_b - u * (scale * scale * scale * inner)).astype(BF16)
        f_hid, b_hid = fh_ref[...], bh_ref[...]
        zero = jnp.zeros_like(f_hid)
        f_delta = jnp.where(f_hid > 0, dot_nt(fo, d_f).astype(BF16), zero)
        b_delta = jnp.where(b_hid > 0, dot_nt(bo, d_u).astype(BF16), zero)
        sums = (
            (0, c1, dot_nn(f_delta, a_ref[...])),
            (c1, c2, dot_nn(f_hid, d_f)),
            (c2, c3, dot_nn(b_delta, later_ref[...])),
            (c3, part_ref.shape[1], dot_nn(b_hid, d_u)),
        )
        for low, high, value in sums:
            if index == 0:
                part_ref[:, low:high] = value
            else:
                part_ref[:, low:high] += value
    loss = (0.5 / group) * jnp.sum(square) - jnp.sum(diagonal)
    lanes = lax.broadcasted_iota(jnp.int32, (block, LANES), 1)
    spot = cfg["loss_spot"]
    base = spot // LANES * LANES
    first = spot - base + 3 * lax.axis_index("replica")
    rest = jnp.full((block, LANES), loss, F32)
    piece_tile = part_ref[:, base : base + LANES]
    piece_tile = jnp.where(lanes >= spot - base, 0.0, piece_tile)
    for j in range(3):
        piece = rest.astype(BF16).astype(F32)
        piece_tile = jnp.where(lanes == first + j, piece, piece_tile)
        rest = rest - piece
    part_ref[:, base : base + LANES] = piece_tile
    core = lax.rem(lax.axis_index("replica"), 2)
    half = block // 2
    keep_ref[...] = part_ref[pl.ds(pl.multiple_of(core * half, ROW_TILE), half), :]
    other = pl.multiple_of((1 - core) * half, ROW_TILE)
    send_ref[...] = part_ref[pl.ds(other, half), :].astype(BF16)


def finish_kernel(cfg, one_ref, two_ref, far_ref, fs, fa, fl, fo, bs, bo, loss_ref, act_ref):
    obs, act, rank, x_pad, obs_pad = (cfg[k] for k in ("obs", "act", "rank", "x_pad", "obs_pad"))
    half = cfg["block"] // 2
    c1, c2, c3 = cfg["cols"]
    core = lax.rem(lax.axis_index("replica"), 2)
    mine32 = one_ref[...].astype(F32) + two_ref[...].astype(F32)
    mine = mine32.astype(BF16)
    far = far_ref[...]
    for start, value in ((core * half, mine), ((1 - core) * half, far)):
        here = pl.ds(pl.multiple_of(start, ROW_TILE), half)
        fs[here, :] = value[:, :obs]
        fl[here, :] = value[:, x_pad:c1]
        fo[here, :] = value[:, c1:c2]
        bs[here, :] = value[:, c2 : c2 + obs]
        bo[here, :] = value[:, c3:]
        act_ref[here, :] = value[:, obs_pad : obs_pad + LANES].astype(F32)
    fa[...] = act_ref[...].T[:act].astype(BF16)
    spot = cfg["loss_spot"]
    base = spot // LANES * LANES
    pieces = mine32[0:8, base : base + LANES]
    lanes = lax.broadcasted_iota(jnp.int32, (8, LANES), 1)
    rows = lax.broadcasted_iota(jnp.int32, (8, LANES), 0)
    ours = (lanes >= spot - base) & (lanes < spot - base + 3 * cfg["replicas"]) & (rows == 0)
    loss_ref[0, 0] = jnp.sum(jnp.where(ours, pieces, 0.0)) / cfg["total"]


def exchange(array, axis, size, bit):
    return lax.ppermute(array, axis, [(i, i ^ bit) for i in range(size)])


def shape(dims, kind):
    return jax.ShapeDtypeStruct(dims, kind)


def fast_local(
    states,
    actions,
    target_forward,
    next_index,
    latent_ids,
    latents,
    f_state,
    f_action,
    f_latent,
    f_output,
    b_state,
    b_output,
):
    size = lax.axis_size("dp")
    replicas = lax.axis_size("replica")
    rows, obs = states.shape[1:]
    act = actions.shape[2]
    zcount, rank = latents.shape
    hidden = f_state.shape[1]
    block = hidden // size
    group = rows * size
    side = round_up(act + 2, 2 * ROW_TILE)
    lane = round_up(rows, LANES)
    obs_pad = round_up(obs, LANES)
    x_pad = obs_pad + LANES
    c1 = x_pad + rank
    c2 = c1 + rank
    c3 = c2 + obs_pad
    width = c3 + rank
    cfg = dict(
        rows=rows,
        obs=obs,
        act=act,
        rank=rank,
        obs_pad=obs_pad,
        x_pad=x_pad,
        hidden=hidden,
        zcount=zcount,
        side=side,
        lane=lane,
        group=group,
        replicas=replicas,
        total=group * replicas,
        block=block,
        tile=512,
        cols=(c1, c2, c3),
        loss_spot=obs_pad + side,
    )
    params = pltpu.CompilerParams(vmem_limit_bytes=20 * 1024 * 1024)
    last_params = pltpu.CompilerParams(vmem_limit_bytes=28 * 1024 * 1024)
    own = pl.pallas_call(
        functools.partial(pack_kernel, cfg),
        out_shape=shape((rows + side // 2, obs_pad + rank), BF16),
        scratch_shapes=[pltpu.VMEM((side, lane), F32)],
        compiler_params=pltpu.CompilerParams(vmem_limit_bytes=VMEM_LIMIT),
        name="pack",
    )(states, actions[0].T, next_index, latent_ids, target_forward)
    x = {"own": own}
    middle = [(2 + i, 4 + i) for i in range(2)] + [(4 + i, 2 + i) for i in range(2)]
    outward = [(2 + i, i) for i in range(2)] + [(4 + i, 6 + i) for i in range(2)]
    across = lax.ppermute(own, "dp", middle)
    x["x own"] = exchange(own, "dp", size, 1)
    x["half"] = exchange(own, "dp", size, 2)
    handed = lax.ppermute(across, "dp", outward)
    x["x half"] = exchange(x["half"], "dp", size, 1)
    across_two = lax.ppermute(x["half"], "dp", middle)
    x["second"] = across + handed
    x["x second"] = exchange(x["second"], "dp", size, 1)
    handed_two = lax.ppermute(across_two, "dp", outward)
    x["third"] = across_two + handed_two
    x["x third"] = exchange(x["third"], "dp", size, 1)
    wf, wb, wfb, wbb = pl.pallas_call(
        functools.partial(weights_kernel, cfg),
        out_shape=(
            shape((x_pad + rank, hidden), BF16),
            shape((obs_pad, hidden), BF16),
            shape((block, x_pad + rank), BF16),
            shape((block, obs_pad), BF16),
        ),
        in_specs=[pl.BlockSpec(memory_space=pl.ANY)] * 4,
        scratch_shapes=[
            pltpu.VMEM((obs, hidden), BF16),
            pltpu.VMEM((act, hidden), BF16),
            pltpu.VMEM((rank, hidden), BF16),
            pltpu.VMEM((obs, hidden), BF16),
            pltpu.SemaphoreType.DMA((4,)),
        ],
        compiler_params=pltpu.CompilerParams(vmem_limit_bytes=16 * 1024 * 1024),
        cost_estimate=pl.CostEstimate(flops=0, bytes_accessed=8_000_000, transcendentals=0),
        name="weights",
    )(*(pltpu.with_memory_space_constraint(w, pltpu.HBM) for w in (f_state, f_action, f_latent, b_state)))
    weights = (wf, wb, f_output, b_output, latents, wfb, wbb)
    row_flops = 2 * (c1 + 2 * rank + obs_pad) * hidden + 8 * rank * rank

    def kept(count):
        m = rows * count
        return (
            ((m, x_pad + rank), BF16),
            ((m, obs_pad), BF16),
            ((m, rank), BF16),
            ((m, rank), F32),
            ((block, m), BF16),
            ((block, m), BF16),
        )

    grams = ()
    plan = (("own", "half"), ("x own", "x half"), ("second", "third"), ("x second",))
    early = []
    for steps in plan:
        count = len(steps)
        xs = [x[step] for step in steps]
        *saved, total_grams = pl.pallas_call(
            functools.partial(forward_kernel, cfg, count, not early),
            out_shape=(*(shape(*item) for item in kept(count)), shape((rank, 2 * rank), F32)),
            compiler_params=params,
            cost_estimate=pl.CostEstimate(
                flops=2 * rows * count * row_flops, bytes_accessed=8_000_000, transcendentals=0
            ),
            name="forward",
        )(*xs, *weights, *grams)
        grams = (total_grams,)
        early.append((xs, saved))
    left = [x["x third"]]
    operands = []
    for xs, saved in early:
        operands += [*xs, *saved]
    send, keep = pl.pallas_call(
        functools.partial(last_kernel, cfg, [len(xs) for xs, _ in early], len(left)),
        out_shape=(shape((block // 2, width), BF16), shape((block // 2, width), F32)),
        scratch_shapes=[
            *(pltpu.VMEM(*item) for item in kept(len(left))),
            pltpu.VMEM((block, width), F32),
        ],
        compiler_params=last_params,
        cost_estimate=pl.CostEstimate(
            flops=4 * group * width * block, bytes_accessed=16_000_000, transcendentals=0
        ),
        name="last",
    )(*operands, *left, *weights, *grams)
    got = exchange(send, "replica", replicas, 1)
    one = (keep + got.astype(F32)).astype(BF16)
    two = exchange(one, "replica", replicas, 2)
    mine = (one.astype(F32) + two.astype(F32)).astype(BF16)
    far = exchange(mine, "replica", replicas, 1)
    fs, fa, fl, fo, bs, bo, loss = pl.pallas_call(
        functools.partial(finish_kernel, cfg),
        out_shape=(
            shape((block, obs), BF16),
            shape((act, block), BF16),
            shape((block, rank), BF16),
            shape((block, rank), BF16),
            shape((block, obs), BF16),
            shape((block, rank), BF16),
            shape((1, 1), F32),
        ),
        out_specs=(
            *(pl.BlockSpec(memory_space=pltpu.VMEM) for _ in range(6)),
            pl.BlockSpec(memory_space=pltpu.SMEM),
        ),
        scratch_shapes=[pltpu.VMEM((block, LANES), F32)],
        compiler_params=pltpu.CompilerParams(vmem_limit_bytes=16 * 1024 * 1024),
        name="finish",
    )(one, two, far)
    return (fs.T, fa, fl.T, fo, bs.T, bo, loss.reshape(()))


def forward_pass(
    current, later, moves, latent_rows, f_state, f_action, f_latent, f_output, b_state, b_output
):
    f_pre = (
        jnp.dot(current, f_state, preferred_element_type=F32)
        + jnp.dot(moves, f_action, preferred_element_type=F32)
        + jnp.dot(latent_rows, f_latent, preferred_element_type=F32)
    )
    f_hidden = jnp.maximum(f_pre, 0.0).astype(BF16)
    forward_emb = jnp.dot(f_hidden, f_output, preferred_element_type=F32).astype(BF16)
    b_pre = jnp.dot(later, b_state, preferred_element_type=F32)
    b_hidden = jnp.maximum(b_pre, 0.0).astype(BF16)
    b_raw = jnp.dot(b_hidden, b_output, preferred_element_type=F32)
    b_scale = lax.rsqrt(jnp.mean(b_raw * b_raw, axis=-1, keepdims=True) + EPSILON)
    backward_emb = (b_raw * b_scale).astype(BF16)
    return (f_pre, f_hidden, forward_emb, b_pre, b_hidden, b_raw, b_scale, backward_emb)


def general_local(
    states,
    actions,
    target_forward,
    next_index,
    latent_ids,
    latents,
    f_state,
    f_action,
    f_latent,
    f_output,
    b_state,
    b_output,
):
    current = states[0]
    moves = actions[0]
    later = jnp.take(current, next_index[0], axis=0)
    latent_rows = jnp.take(latents, latent_ids[0], axis=0)
    f_pre, f_hidden, forward_emb, b_pre, b_hidden, b_raw, b_scale, backward_emb = forward_pass(
        current, later, moves, latent_rows, f_state, f_action, f_latent, f_output, b_state, b_output
    )
    group = current.shape[0] * lax.axis_size("dp")
    total = group * lax.axis_size("replica")
    factor = 1.0 / math.sqrt(total)
    forward32 = forward_emb.astype(F32)
    back32 = backward_emb.astype(F32)
    error = forward32 - GAMMA * target_forward[0].astype(F32)
    gram, cross = lax.psum(
        (
            jnp.dot(backward_emb.T, backward_emb, preferred_element_type=F32),
            jnp.dot(forward32.T, error, precision=HIGH, preferred_element_type=F32),
        ),
        "dp",
    )
    pulled = jnp.dot(error, gram, precision=HIGH, preferred_element_type=F32)
    pushed = jnp.dot(back32, cross.T, precision=HIGH, preferred_element_type=F32)
    partial_loss = 0.5 / group * jnp.sum(pulled * error) - jnp.sum(forward32 * back32)
    grad_forward = (factor * (pulled / group - back32)).astype(BF16)
    grad_backward = factor * (pushed / group - forward32)
    inner = jnp.mean(b_raw * grad_backward, axis=-1, keepdims=True)
    grad_raw = (b_scale * grad_backward - b_raw * b_scale * b_scale * b_scale * inner).astype(BF16)
    part_bo = jnp.dot(b_hidden.T, grad_raw, preferred_element_type=F32)
    b_back = jnp.dot(grad_raw, b_output.T, preferred_element_type=F32)
    b_delta = jnp.where(b_pre > 0, b_back, 0.0).astype(BF16)
    part_bs = jnp.dot(later.T, b_delta, preferred_element_type=F32)
    part_fo = jnp.dot(f_hidden.T, grad_forward, preferred_element_type=F32)
    f_back = jnp.dot(grad_forward, f_output.T, preferred_element_type=F32)
    f_delta = jnp.where(f_pre > 0, f_back, 0.0).astype(BF16)
    part_fs = jnp.dot(current.T, f_delta, preferred_element_type=F32)
    part_fa = jnp.dot(moves.T, f_delta, preferred_element_type=F32)
    part_fl = jnp.dot(latent_rows.T, f_delta, preferred_element_type=F32)
    places = (1, 1, 1, 0, 1, 0)
    parts = (part_fs, part_fa, part_fl, part_fo, part_bs, part_bo)
    shares = tuple(
        lax.psum_scatter(part, "dp", scatter_dimension=place, tiled=True)
        for part, place in zip(parts, places)
    )
    summed = lax.psum(shares, "replica")
    loss_sum = lax.psum(partial_loss, ("dp", "replica"))
    return (*(item.astype(BF16) for item in summed), loss_sum / total)


def local(*args):
    size, replicas = lax.axis_size("dp"), lax.axis_size("replica")
    rows, hidden = args[0].shape[1], args[6].shape[1]
    fits = size == 8 and replicas == 4 and rows * size <= KERNEL_GROUP_LIMIT
    block = hidden // size
    whole = rows % ROW_TILE == 0 and hidden % (size * 64) == 0 and hidden % 512 == 0
    whole = whole and LANES < block <= 2 * LANES - 64 and args[6].shape[0] % 8 == 0
    exact = rows <= 256 and args[5].shape[0] <= 256
    return (fast_local if fits and whole and exact else general_local)(*args)


def solution(mesh):
    in_specs = (
        P("replica", "dp", None),
        P("replica", "dp", None),
        P("replica", "dp", None),
        P("replica", "dp"),
        P("replica", "dp"),
        P(),
        P(),
        P(),
        P(),
        P(),
        P(),
        P(),
    )
    out_specs = (
        P(None, "dp"),
        P(None, "dp"),
        P(None, "dp"),
        P("dp", None),
        P(None, "dp"),
        P("dp", None),
        P(),
    )
    return jax.shard_map(local, mesh=mesh, in_specs=in_specs, out_specs=out_specs, check_vma=False)
```

```python
import functools
import math

import jax
import jax.numpy as jnp
from jax import lax
from jax.experimental import pallas as pl
from jax.experimental.pallas import tpu as pltpu
from jax.sharding import PartitionSpec as P

GAMMA = 0.98
EPSILON = 1e-06
HIGH = lax.Precision.HIGHEST
BF16 = jnp.bfloat16
F32 = jnp.float32
LANES = 128
ROW_TILE = 16
VMEM_LIMIT = 56 * 1024 * 1024
KERNEL_GROUP_LIMIT = 2048


def round_up(value, unit):
    return -(-value // unit) * unit


def dot_nn(left, right):
    return lax.dot_general(left, right, (((1,), (0,)), ((), ())), preferred_element_type=F32)


def dot_nt(left, right):
    return lax.dot_general(left, right, (((1,), (1,)), ((), ())), preferred_element_type=F32)


def dot_tn(left, right):
    return lax.dot_general(left, right, (((0,), (0,)), ((), ())), preferred_element_type=F32)


def split_two(value):
    high = value.astype(BF16)
    return high, (value - high.astype(F32)).astype(BF16)


def pack_kernel(cfg, state_ref, move_ref, next_ref, latent_ref, target_ref, out_ref, side_ref):
    rows, obs, act, obs_pad, side = (cfg[k] for k in ("rows", "obs", "act", "obs_pad", "side"))
    lane = side_ref.shape[1]
    side_ref[...] = jnp.zeros_like(side_ref)
    side_ref[0:act, 0:rows] = move_ref[...].astype(F32)
    side_ref[act : act + 1, 0:rows] = next_ref[...].astype(F32)
    side_ref[act + 1 : act + 2, 0:rows] = latent_ref[...].astype(F32)
    gap = jnp.zeros((rows, obs_pad - obs), BF16)
    out_ref[0:rows, 0:obs_pad] = jnp.concatenate([state_ref[0], gap], axis=1)
    out_ref[0:rows, obs_pad:] = target_ref[0]
    half = side // 2
    out_ref[rows:, :] = jnp.zeros((half, out_ref.shape[1]), BF16)
    out_ref[rows:, 0:lane] = side_ref[0:half, :].astype(BF16)
    out_ref[rows:, lane : 2 * lane] = side_ref[half:side, :].astype(BF16)


def weights_kernel(cfg, fs_hbm, fa_hbm, fl_hbm, bs_hbm, *refs):
    obs, obs_pad, x_pad = cfg["obs"], cfg["obs_pad"], cfg["x_pad"]
    hidden, block, act = cfg["hidden"], cfg["block"], cfg["act"]
    wf_ref, wb_ref, wfb_ref, wbb_ref, fs_ref, fa_ref, fl_ref, bs_ref, sems = refs
    pairs = ((fs_hbm, fs_ref), (bs_hbm, bs_ref), (fl_hbm, fl_ref), (fa_hbm, fa_ref))
    copies = [pltpu.make_async_copy(a, b, sems.at[i]) for i, (a, b) in enumerate(pairs)]
    for copy in copies:
        copy.start()
    gap = jnp.zeros((obs_pad - obs, hidden), BF16)
    wf_ref[obs_pad:x_pad, :] = jnp.zeros((x_pad - obs_pad, hidden), BF16)
    copies[0].wait()
    wf_ref[0:obs_pad, :] = jnp.concatenate([fs_ref[...], gap], axis=0)
    copies[1].wait()
    wb_ref[...] = jnp.concatenate([bs_ref[...], gap], axis=0)
    copies[2].wait()
    wf_ref[x_pad:, :] = fl_ref[...]
    copies[3].wait()
    wf_ref[obs_pad : obs_pad + act, :] = fa_ref[...]
    me = lax.axis_index("dp")
    start = me * block
    base = pl.multiple_of(start // LANES * LANES, LANES)
    odd = lax.rem(me, 2) == 1
    span = pl.ds(base, 2 * LANES)

    def pick(ref):
        near = ref[:, span].astype(F32).T
        return jnp.where(odd, near[2 * LANES - block :], near[:block]).astype(BF16)

    wfb_ref[...] = pick(wf_ref)
    wbb_ref[...] = pick(wb_ref)


def forward_rows(cfg, xs, weights, outs):
    wf_ref, wb_ref, fo_ref, bo_ref, lat_ref, wfb_ref, wbb_ref = weights
    a_ref, later_ref, f_ref, u_ref, fh_ref, bh_ref = outs
    rows, act, rank, side = cfg["rows"], cfg["act"], cfg["rank"], cfg["side"]
    obs_pad, x_pad, hidden, zcount = cfg["obs_pad"], cfg["x_pad"], cfg["hidden"], cfg["zcount"]
    tile, lane = cfg["tile"], cfg["lane"]
    m = rows * len(xs)
    half = side // 2
    row_spots = lax.broadcasted_iota(jnp.int32, (rows, rows), 1).astype(F32)
    spots = lax.broadcasted_iota(jnp.int32, (rows, zcount), 1).astype(F32)
    blank = jnp.zeros((rows, x_pad - obs_pad - side), BF16)
    for j, x_ref in enumerate(xs):
        here = slice(j * rows, (j + 1) * rows)
        few = jnp.concatenate(
            [x_ref[rows:, 0:lane].astype(F32), x_ref[rows:, lane : 2 * lane].astype(F32)], axis=0
        ).T[:rows]
        near = x_ref[0:rows, 0:obs_pad]
        picks = jnp.where(few[:, act + 1 : act + 2] == spots, 1.0, 0.0).astype(BF16)
        hot = jnp.where(few[:, act : act + 1] == row_spots, 1.0, 0.0).astype(BF16)
        a_ref[here, 0:obs_pad] = near
        a_ref[here, obs_pad:x_pad] = jnp.concatenate([few.astype(BF16), blank], axis=1)
        a_ref[here, x_pad:] = dot_nn(picks, lat_ref[...]).astype(BF16)
        later_ref[here, :] = dot_nn(hot, near).astype(BF16)
    whole = a_ref[...]
    later = later_ref[...]
    f_acc = jnp.zeros((m, rank), F32)
    u = jnp.zeros((m, rank), F32)
    for n in range(0, hidden, tile):
        h = jnp.maximum(dot_nn(whole, wf_ref[:, n : n + tile]), 0.0).astype(BF16)
        f_acc = f_acc + dot_nn(h, fo_ref[n : n + tile, :])
        g = jnp.maximum(dot_nn(later, wb_ref[:, n : n + tile]), 0.0).astype(BF16)
        u = u + dot_nn(g, bo_ref[n : n + tile, :])
    emb = f_acc.astype(BF16)
    back = (u * lax.rsqrt(jnp.mean(u * u, axis=-1, keepdims=True) + EPSILON)).astype(BF16)
    f_ref[...] = emb
    u_ref[...] = u
    fh_ref[...] = jnp.maximum(dot_nt(wfb_ref[...], whole), 0.0).astype(BF16)
    bh_ref[...] = jnp.maximum(dot_nt(wbb_ref[...], later), 0.0).astype(BF16)
    cross = dot_tn(emb, emb)
    for j, x_ref in enumerate(xs):
        cross = cross - GAMMA * dot_tn(x_ref[0:rows, obs_pad:], emb[j * rows : (j + 1) * rows])
    return dot_tn(back, back), cross


def forward_kernel(cfg, count, first, *refs):
    xs, refs = refs[:count], refs[count:]
    weights, refs = refs[:7], refs[7:]
    if not first:
        gram_in, refs = refs[0], refs[1:]
    outs, gram_out = refs[:6], refs[6]
    gram, cross = forward_rows(cfg, xs, weights, outs)
    rank = cfg["rank"]
    gram_out[:, :rank] = gram if first else gram_in[:, :rank] + gram
    gram_out[:, rank:] = cross if first else gram_in[:, rank:] + cross


def last_kernel(cfg, early, count, *refs):
    groups = []
    for size in early:
        groups.append((refs[:size], refs[size : size + 6]))
        refs = refs[size + 6 :]
    xs, refs = refs[:count], refs[count:]
    weights, refs = refs[:7], refs[7:]
    gram_in, send_ref, keep_ref = refs[:3]
    outs, part_ref = refs[3:9], refs[9]
    rank, block, rows, obs_pad = cfg["rank"], cfg["block"], cfg["rows"], cfg["obs_pad"]
    group, replicas = cfg["group"], cfg["replicas"]
    factor = 1.0 / math.sqrt(cfg["total"])
    c1, c2, c3 = cfg["cols"]
    gram, cross = forward_rows(cfg, xs, weights, outs)
    gram_hi, gram_lo = split_two(gram_in[:, :rank] + gram)
    cross_hi, cross_lo = split_two(gram_in[:, rank:] + cross)
    groups.append((xs, outs))
    me = pl.multiple_of(lax.axis_index("dp") * block, ROW_TILE)
    fo = weights[2][pl.ds(me, block), :]
    bo = weights[3][pl.ds(me, block), :]
    square = jnp.zeros((1, rank), F32)
    diagonal = jnp.zeros((1, rank), F32)
    for index, (x_refs, (a_ref, later_ref, f_ref, u_ref, fh_ref, bh_ref)) in enumerate(groups):
        emb32 = f_ref[...].astype(F32)
        targets = [x_ref[0:rows, obs_pad:] for x_ref in x_refs]
        target = jnp.concatenate(targets, axis=0) if len(targets) > 1 else targets[0]
        error = emb32 - GAMMA * target.astype(F32)
        err_hi, err_lo = split_two(error)
        u = u_ref[...]
        scale = lax.rsqrt(jnp.mean(u * u, axis=-1, keepdims=True) + EPSILON)
        back = (u * scale).astype(BF16)
        back32 = back.astype(F32)
        pulled = dot_nn(err_hi, gram_hi) + (dot_nn(err_hi, gram_lo) + dot_nn(err_lo, gram_hi))
        square = square + jnp.sum(pulled * error, axis=0, keepdims=True)
        diagonal = diagonal + jnp.sum(emb32 * back32, axis=0, keepdims=True)
        d_f = (factor * (pulled / group - back32)).astype(BF16)
        pushed = dot_nn(back, cross_hi) + dot_nn(back, cross_lo)
        d_b = factor * (pushed / group - emb32)
        inner = jnp.mean(u * d_b, axis=-1, keepdims=True)
        d_u = (scale * d_b - u * (scale * scale * scale * inner)).astype(BF16)
        f_hid, b_hid = fh_ref[...], bh_ref[...]
        zero = jnp.zeros_like(f_hid)
        f_delta = jnp.where(f_hid > 0, dot_nt(fo, d_f).astype(BF16), zero)
        b_delta = jnp.where(b_hid > 0, dot_nt(bo, d_u).astype(BF16), zero)
        sums = (
            (0, c1, dot_nn(f_delta, a_ref[...])),
            (c1, c2, dot_nn(f_hid, d_f)),
            (c2, c3, dot_nn(b_delta, later_ref[...])),
            (c3, part_ref.shape[1], dot_nn(b_hid, d_u)),
        )
        for low, high, value in sums:
            if index == 0:
                part_ref[:, low:high] = value
            else:
                part_ref[:, low:high] += value
    loss = (0.5 / group) * jnp.sum(square) - jnp.sum(diagonal)
    lanes = lax.broadcasted_iota(jnp.int32, (block, LANES), 1)
    spot = cfg["loss_spot"]
    base = spot // LANES * LANES
    first = spot - base + 3 * lax.axis_index("replica")
    rest = jnp.full((block, LANES), loss, F32)
    piece_tile = part_ref[:, base : base + LANES]
    piece_tile = jnp.where(lanes >= spot - base, 0.0, piece_tile)
    for j in range(3):
        piece = rest.astype(BF16).astype(F32)
        piece_tile = jnp.where(lanes == first + j, piece, piece_tile)
        rest = rest - piece
    part_ref[:, base : base + LANES] = piece_tile
    core = lax.rem(lax.axis_index("replica"), 2)
    half = block // 2
    keep_ref[...] = part_ref[pl.ds(pl.multiple_of(core * half, ROW_TILE), half), :]
    other = pl.multiple_of((1 - core) * half, ROW_TILE)
    send_ref[...] = part_ref[pl.ds(other, half), :].astype(BF16)


def finish_kernel(cfg, one_ref, two_ref, far_ref, fs, fa, fl, fo, bs, bo, loss_ref, act_ref):
    obs, act, rank, x_pad, obs_pad = (cfg[k] for k in ("obs", "act", "rank", "x_pad", "obs_pad"))
    half = cfg["block"] // 2
    c1, c2, c3 = cfg["cols"]
    core = lax.rem(lax.axis_index("replica"), 2)
    mine32 = one_ref[...].astype(F32) + two_ref[...].astype(F32)
    mine = mine32.astype(BF16)
    far = far_ref[...]
    for start, value in ((core * half, mine), ((1 - core) * half, far)):
        here = pl.ds(pl.multiple_of(start, ROW_TILE), half)
        fs[here, :] = value[:, :obs]
        fl[here, :] = value[:, x_pad:c1]
        fo[here, :] = value[:, c1:c2]
        bs[here, :] = value[:, c2 : c2 + obs]
        bo[here, :] = value[:, c3:]
        act_ref[here, :] = value[:, obs_pad : obs_pad + LANES].astype(F32)
    fa[...] = act_ref[...].T[:act].astype(BF16)
    spot = cfg["loss_spot"]
    base = spot // LANES * LANES
    pieces = mine32[0:8, base : base + LANES]
    lanes = lax.broadcasted_iota(jnp.int32, (8, LANES), 1)
    rows = lax.broadcasted_iota(jnp.int32, (8, LANES), 0)
    ours = (lanes >= spot - base) & (lanes < spot - base + 3 * cfg["replicas"]) & (rows == 0)
    loss_ref[0, 0] = jnp.sum(jnp.where(ours, pieces, 0.0)) / cfg["total"]


def exchange(array, axis, size, bit):
    return lax.ppermute(array, axis, [(i, i ^ bit) for i in range(size)])


def shape(dims, kind):
    return jax.ShapeDtypeStruct(dims, kind)


def fast_local(
    states,
    actions,
    target_forward,
    next_index,
    latent_ids,
    latents,
    f_state,
    f_action,
    f_latent,
    f_output,
    b_state,
    b_output,
):
    size = lax.axis_size("dp")
    replicas = lax.axis_size("replica")
    rows, obs = states.shape[1:]
    act = actions.shape[2]
    zcount, rank = latents.shape
    hidden = f_state.shape[1]
    block = hidden // size
    group = rows * size
    side = round_up(act + 2, 2 * ROW_TILE)
    lane = round_up(rows, LANES)
    obs_pad = round_up(obs, LANES)
    x_pad = obs_pad + LANES
    c1 = x_pad + rank
    c2 = c1 + rank
    c3 = c2 + obs_pad
    width = c3 + rank
    cfg = dict(
        rows=rows,
        obs=obs,
        act=act,
        rank=rank,
        obs_pad=obs_pad,
        x_pad=x_pad,
        hidden=hidden,
        zcount=zcount,
        side=side,
        lane=lane,
        group=group,
        replicas=replicas,
        total=group * replicas,
        block=block,
        tile=512,
        cols=(c1, c2, c3),
        loss_spot=obs_pad + side,
    )
    params = pltpu.CompilerParams(vmem_limit_bytes=20 * 1024 * 1024)
    last_params = pltpu.CompilerParams(vmem_limit_bytes=28 * 1024 * 1024)
    own = pl.pallas_call(
        functools.partial(pack_kernel, cfg),
        out_shape=shape((rows + side // 2, obs_pad + rank), BF16),
        scratch_shapes=[pltpu.VMEM((side, lane), F32)],
        compiler_params=pltpu.CompilerParams(vmem_limit_bytes=VMEM_LIMIT),
        name="pack",
    )(states, actions[0].T, next_index, latent_ids, target_forward)
    x = {"own": own}
    middle = [(2 + i, 4 + i) for i in range(2)] + [(4 + i, 2 + i) for i in range(2)]
    outward = [(2 + i, i) for i in range(2)] + [(4 + i, 6 + i) for i in range(2)]
    across = lax.ppermute(own, "dp", middle)
    x["x own"] = exchange(own, "dp", size, 1)
    x["half"] = exchange(own, "dp", size, 2)
    handed = lax.ppermute(across, "dp", outward)
    x["x half"] = exchange(x["half"], "dp", size, 1)
    across_two = lax.ppermute(x["half"], "dp", middle)
    x["second"] = across + handed
    x["x second"] = exchange(x["second"], "dp", size, 1)
    handed_two = lax.ppermute(across_two, "dp", outward)
    x["third"] = across_two + handed_two
    x["x third"] = exchange(x["third"], "dp", size, 1)
    wf, wb, wfb, wbb = pl.pallas_call(
        functools.partial(weights_kernel, cfg),
        out_shape=(
            shape((x_pad + rank, hidden), BF16),
            shape((obs_pad, hidden), BF16),
            shape((block, x_pad + rank), BF16),
            shape((block, obs_pad), BF16),
        ),
        in_specs=[pl.BlockSpec(memory_space=pl.ANY)] * 4,
        scratch_shapes=[
            pltpu.VMEM((obs, hidden), BF16),
            pltpu.VMEM((act, hidden), BF16),
            pltpu.VMEM((rank, hidden), BF16),
            pltpu.VMEM((obs, hidden), BF16),
            pltpu.SemaphoreType.DMA((4,)),
        ],
        compiler_params=pltpu.CompilerParams(vmem_limit_bytes=16 * 1024 * 1024),
        cost_estimate=pl.CostEstimate(flops=0, bytes_accessed=1_000_000, transcendentals=0),
        name="weights",
    )(*(pltpu.with_memory_space_constraint(w, pltpu.HBM) for w in (f_state, f_action, f_latent, b_state)))
    weights = (wf, wb, f_output, b_output, latents, wfb, wbb)
    row_flops = 2 * (c1 + 2 * rank + obs_pad) * hidden + 8 * rank * rank

    def kept(count):
        m = rows * count
        return (
            ((m, x_pad + rank), BF16),
            ((m, obs_pad), BF16),
            ((m, rank), BF16),
            ((m, rank), F32),
            ((block, m), BF16),
            ((block, m), BF16),
        )

    grams = ()
    plan = (
        (("own",), 3.0),
        (("half",), 2.0),
        (("x own",), 1.5),
        (("x half", "second"), 1.0),
        (("third", "x second"), 3.0),
    )
    early = []
    for steps, work in plan:
        count = len(steps)
        xs = [x[step] for step in steps]
        *saved, total_grams = pl.pallas_call(
            functools.partial(forward_kernel, cfg, count, not early),
            out_shape=(*(shape(*item) for item in kept(count)), shape((rank, 2 * rank), F32)),
            compiler_params=params,
            cost_estimate=pl.CostEstimate(
                flops=int(work * rows * count * row_flops),
                bytes_accessed=1_000_000,
                transcendentals=0,
            ),
            name="forward",
        )(*xs, *weights, *grams)
        grams = (total_grams,)
        early.append((xs, saved))
    left = [x["x third"]]
    operands = []
    for xs, saved in early:
        operands += [*xs, *saved]
    send, keep = pl.pallas_call(
        functools.partial(last_kernel, cfg, [len(xs) for xs, _ in early], len(left)),
        out_shape=(shape((block // 2, width), BF16), shape((block // 2, width), F32)),
        scratch_shapes=[
            *(pltpu.VMEM(*item) for item in kept(len(left))),
            pltpu.VMEM((block, width), F32),
        ],
        compiler_params=last_params,
        cost_estimate=pl.CostEstimate(
            flops=4 * group * width * block, bytes_accessed=16_000_000, transcendentals=0
        ),
        name="last",
    )(*operands, *left, *weights, *grams)
    got = exchange(send, "replica", replicas, 1)
    one = (keep + got.astype(F32)).astype(BF16)
    two = exchange(one, "replica", replicas, 2)
    mine = (one.astype(F32) + two.astype(F32)).astype(BF16)
    far = exchange(mine, "replica", replicas, 1)
    fs, fa, fl, fo, bs, bo, loss = pl.pallas_call(
        functools.partial(finish_kernel, cfg),
        out_shape=(
            shape((block, obs), BF16),
            shape((act, block), BF16),
            shape((block, rank), BF16),
            shape((block, rank), BF16),
            shape((block, obs), BF16),
            shape((block, rank), BF16),
            shape((1, 1), F32),
        ),
        out_specs=(
            *(pl.BlockSpec(memory_space=pltpu.VMEM) for _ in range(6)),
            pl.BlockSpec(memory_space=pltpu.SMEM),
        ),
        scratch_shapes=[pltpu.VMEM((block, LANES), F32)],
        compiler_params=pltpu.CompilerParams(vmem_limit_bytes=16 * 1024 * 1024),
        name="finish",
    )(one, two, far)
    return (fs.T, fa, fl.T, fo, bs.T, bo, loss.reshape(()))


def forward_pass(
    current, later, moves, latent_rows, f_state, f_action, f_latent, f_output, b_state, b_output
):
    f_pre = (
        jnp.dot(current, f_state, preferred_element_type=F32)
        + jnp.dot(moves, f_action, preferred_element_type=F32)
        + jnp.dot(latent_rows, f_latent, preferred_element_type=F32)
    )
    f_hidden = jnp.maximum(f_pre, 0.0).astype(BF16)
    forward_emb = jnp.dot(f_hidden, f_output, preferred_element_type=F32).astype(BF16)
    b_pre = jnp.dot(later, b_state, preferred_element_type=F32)
    b_hidden = jnp.maximum(b_pre, 0.0).astype(BF16)
    b_raw = jnp.dot(b_hidden, b_output, preferred_element_type=F32)
    b_scale = lax.rsqrt(jnp.mean(b_raw * b_raw, axis=-1, keepdims=True) + EPSILON)
    backward_emb = (b_raw * b_scale).astype(BF16)
    return (f_pre, f_hidden, forward_emb, b_pre, b_hidden, b_raw, b_scale, backward_emb)


def general_local(
    states,
    actions,
    target_forward,
    next_index,
    latent_ids,
    latents,
    f_state,
    f_action,
    f_latent,
    f_output,
    b_state,
    b_output,
):
    current = states[0]
    moves = actions[0]
    later = jnp.take(current, next_index[0], axis=0)
    latent_rows = jnp.take(latents, latent_ids[0], axis=0)
    f_pre, f_hidden, forward_emb, b_pre, b_hidden, b_raw, b_scale, backward_emb = forward_pass(
        current, later, moves, latent_rows, f_state, f_action, f_latent, f_output, b_state, b_output
    )
    group = current.shape[0] * lax.axis_size("dp")
    total = group * lax.axis_size("replica")
    factor = 1.0 / math.sqrt(total)
    forward32 = forward_emb.astype(F32)
    back32 = backward_emb.astype(F32)
    error = forward32 - GAMMA * target_forward[0].astype(F32)
    gram, cross = lax.psum(
        (
            jnp.dot(backward_emb.T, backward_emb, preferred_element_type=F32),
            jnp.dot(forward32.T, error, precision=HIGH, preferred_element_type=F32),
        ),
        "dp",
    )
    pulled = jnp.dot(error, gram, precision=HIGH, preferred_element_type=F32)
    pushed = jnp.dot(back32, cross.T, precision=HIGH, preferred_element_type=F32)
    partial_loss = 0.5 / group * jnp.sum(pulled * error) - jnp.sum(forward32 * back32)
    grad_forward = (factor * (pulled / group - back32)).astype(BF16)
    grad_backward = factor * (pushed / group - forward32)
    inner = jnp.mean(b_raw * grad_backward, axis=-1, keepdims=True)
    grad_raw = (b_scale * grad_backward - b_raw * b_scale * b_scale * b_scale * inner).astype(BF16)
    part_bo = jnp.dot(b_hidden.T, grad_raw, preferred_element_type=F32)
    b_back = jnp.dot(grad_raw, b_output.T, preferred_element_type=F32)
    b_delta = jnp.where(b_pre > 0, b_back, 0.0).astype(BF16)
    part_bs = jnp.dot(later.T, b_delta, preferred_element_type=F32)
    part_fo = jnp.dot(f_hidden.T, grad_forward, preferred_element_type=F32)
    f_back = jnp.dot(grad_forward, f_output.T, preferred_element_type=F32)
    f_delta = jnp.where(f_pre > 0, f_back, 0.0).astype(BF16)
    part_fs = jnp.dot(current.T, f_delta, preferred_element_type=F32)
    part_fa = jnp.dot(moves.T, f_delta, preferred_element_type=F32)
    part_fl = jnp.dot(latent_rows.T, f_delta, preferred_element_type=F32)
    places = (1, 1, 1, 0, 1, 0)
    parts = (part_fs, part_fa, part_fl, part_fo, part_bs, part_bo)
    shares = tuple(
        lax.psum_scatter(part, "dp", scatter_dimension=place, tiled=True)
        for part, place in zip(parts, places)
    )
    summed = lax.psum(shares, "replica")
    loss_sum = lax.psum(partial_loss, ("dp", "replica"))
    return (*(item.astype(BF16) for item in summed), loss_sum / total)


def local(*args):
    size, replicas = lax.axis_size("dp"), lax.axis_size("replica")
    rows, hidden = args[0].shape[1], args[6].shape[1]
    fits = size == 8 and replicas == 4 and rows * size <= KERNEL_GROUP_LIMIT
    block = hidden // size
    whole = rows % ROW_TILE == 0 and hidden % (size * 64) == 0 and hidden % 512 == 0
    whole = whole and LANES < block <= 2 * LANES - 64 and args[6].shape[0] % 8 == 0
    exact = rows <= 256 and args[5].shape[0] <= 256
    return (fast_local if fits and whole and exact else general_local)(*args)


def solution(mesh):
    in_specs = (
        P("replica", "dp", None),
        P("replica", "dp", None),
        P("replica", "dp", None),
        P("replica", "dp"),
        P("replica", "dp"),
        P(),
        P(),
        P(),
        P(),
        P(),
        P(),
        P(),
    )
    out_specs = (
        P(None, "dp"),
        P(None, "dp"),
        P(None, "dp"),
        P("dp", None),
        P(None, "dp"),
        P("dp", None),
        P(),
    )
    return jax.shard_map(local, mesh=mesh, in_specs=in_specs, out_specs=out_specs, check_vma=False)
```

```python
import functools
import math

import jax
import jax.numpy as jnp
from jax import lax
from jax.experimental import pallas as pl
from jax.experimental.pallas import tpu as pltpu
from jax.sharding import PartitionSpec as P

GAMMA = 0.98
EPSILON = 1e-06
HIGH = lax.Precision.HIGHEST
BF16 = jnp.bfloat16
F32 = jnp.float32
LANES = 128
ROW_TILE = 16
VMEM_LIMIT = 56 * 1024 * 1024
KERNEL_GROUP_LIMIT = 2048


def round_up(value, unit):
    return -(-value // unit) * unit


def dot_nn(left, right):
    return lax.dot_general(left, right, (((1,), (0,)), ((), ())), preferred_element_type=F32)


def dot_nt(left, right):
    return lax.dot_general(left, right, (((1,), (1,)), ((), ())), preferred_element_type=F32)


def dot_tn(left, right):
    return lax.dot_general(left, right, (((0,), (0,)), ((), ())), preferred_element_type=F32)


def join(values, axis):
    return jnp.concatenate(values, axis=axis) if len(values) > 1 else values[0]


def stack(refs, axis):
    return join([ref[...] for ref in refs], axis)


def split_two(value):
    high = value.astype(BF16)
    return high, (value - high.astype(F32)).astype(BF16)


def pack_kernel(cfg, state_ref, move_ref, next_ref, latent_ref, target_ref, out_ref, side_ref):
    rows, obs, act, obs_pad, side = (cfg[k] for k in ("rows", "obs", "act", "obs_pad", "side"))
    lane = side_ref.shape[1]
    side_ref[...] = jnp.zeros_like(side_ref)
    side_ref[0:act, 0:rows] = move_ref[...].astype(F32)
    side_ref[act : act + 1, 0:rows] = next_ref[...].astype(F32)
    side_ref[act + 1 : act + 2, 0:rows] = latent_ref[...].astype(F32)
    gap = jnp.zeros((rows, obs_pad - obs), BF16)
    out_ref[0:rows, 0:obs_pad] = jnp.concatenate([state_ref[0], gap], axis=1)
    out_ref[0:rows, obs_pad:] = target_ref[0]
    half = side // 2
    out_ref[rows:, :] = jnp.zeros((half, out_ref.shape[1]), BF16)
    out_ref[rows:, 0:lane] = side_ref[0:half, :].astype(BF16)
    out_ref[rows:, lane : 2 * lane] = side_ref[half:side, :].astype(BF16)


def weights_kernel(cfg, fs_hbm, fa_hbm, fl_hbm, bs_hbm, *refs):
    obs, obs_pad, x_pad = cfg["obs"], cfg["obs_pad"], cfg["x_pad"]
    hidden, block, act = cfg["hidden"], cfg["block"], cfg["act"]
    wf_ref, wb_ref, wfb_ref, wbb_ref, fs_ref, fa_ref, fl_ref, bs_ref, sems = refs
    pairs = ((fs_hbm, fs_ref), (bs_hbm, bs_ref), (fl_hbm, fl_ref), (fa_hbm, fa_ref))
    copies = [pltpu.make_async_copy(a, b, sems.at[i]) for i, (a, b) in enumerate(pairs)]
    for copy in copies:
        copy.start()
    gap = jnp.zeros((obs_pad - obs, hidden), BF16)
    wf_ref[obs_pad:x_pad, :] = jnp.zeros((x_pad - obs_pad, hidden), BF16)
    copies[0].wait()
    wf_ref[0:obs_pad, :] = jnp.concatenate([fs_ref[...], gap], axis=0)
    copies[1].wait()
    wb_ref[...] = jnp.concatenate([bs_ref[...], gap], axis=0)
    copies[2].wait()
    wf_ref[x_pad:, :] = fl_ref[...]
    copies[3].wait()
    wf_ref[obs_pad : obs_pad + act, :] = fa_ref[...]
    me = lax.axis_index("dp")
    start = me * block
    base = pl.multiple_of(start // LANES * LANES, LANES)
    odd = lax.rem(me, 2) == 1
    span = pl.ds(base, 2 * LANES)

    def pick(ref):
        near = ref[:, span].astype(F32).T
        return jnp.where(odd, near[2 * LANES - block :], near[:block]).astype(BF16)

    wfb_ref[...] = pick(wf_ref)
    wbb_ref[...] = pick(wb_ref)


def forward_rows(cfg, xs, weights, outs):
    wf_ref, wb_ref, fo_ref, bo_ref, lat_ref, wfb_ref, wbb_ref = weights
    a_ref, later_ref, f_ref, u_ref, fh_ref, bh_ref = outs
    rows, act, rank, side = cfg["rows"], cfg["act"], cfg["rank"], cfg["side"]
    obs_pad, x_pad, hidden, zcount = cfg["obs_pad"], cfg["x_pad"], cfg["hidden"], cfg["zcount"]
    tile, lane = cfg["tile"], cfg["lane"]
    m = rows * len(xs)
    half = side // 2
    row_spots = lax.broadcasted_iota(jnp.int32, (rows, rows), 1).astype(F32)
    spots = lax.broadcasted_iota(jnp.int32, (rows, zcount), 1).astype(F32)
    blank = jnp.zeros((rows, x_pad - obs_pad - side), BF16)
    for j, x_ref in enumerate(xs):
        here = slice(j * rows, (j + 1) * rows)
        few = jnp.concatenate(
            [x_ref[rows:, 0:lane].astype(F32), x_ref[rows:, lane : 2 * lane].astype(F32)], axis=0
        ).T[:rows]
        near = x_ref[0:rows, 0:obs_pad]
        picks = jnp.where(few[:, act + 1 : act + 2] == spots, 1.0, 0.0).astype(BF16)
        hot = jnp.where(few[:, act : act + 1] == row_spots, 1.0, 0.0).astype(BF16)
        a_ref[here, 0:obs_pad] = near
        a_ref[here, obs_pad:x_pad] = jnp.concatenate([few.astype(BF16), blank], axis=1)
        a_ref[here, x_pad:] = dot_nn(picks, lat_ref[...]).astype(BF16)
        later_ref[here, :] = dot_nn(hot, near).astype(BF16)
    whole = a_ref[...]
    later = later_ref[...]
    f_acc = jnp.zeros((m, rank), F32)
    u = jnp.zeros((m, rank), F32)
    for n in range(0, hidden, tile):
        h = jnp.maximum(dot_nn(whole, wf_ref[:, n : n + tile]), 0.0).astype(BF16)
        f_acc = f_acc + dot_nn(h, fo_ref[n : n + tile, :])
        g = jnp.maximum(dot_nn(later, wb_ref[:, n : n + tile]), 0.0).astype(BF16)
        u = u + dot_nn(g, bo_ref[n : n + tile, :])
    emb = f_acc.astype(BF16)
    back = (u * lax.rsqrt(jnp.mean(u * u, axis=-1, keepdims=True) + EPSILON)).astype(BF16)
    f_ref[...] = emb
    u_ref[...] = u
    fh_ref[...] = jnp.maximum(dot_nt(wfb_ref[...], whole), 0.0).astype(BF16)
    bh_ref[...] = jnp.maximum(dot_nt(wbb_ref[...], later), 0.0).astype(BF16)
    cross = dot_tn(emb, emb)
    for j, x_ref in enumerate(xs):
        cross = cross - GAMMA * dot_tn(x_ref[0:rows, obs_pad:], emb[j * rows : (j + 1) * rows])
    return dot_tn(back, back), cross


def forward_kernel(cfg, count, first, *refs):
    xs, refs = refs[:count], refs[count:]
    weights, refs = refs[:7], refs[7:]
    if not first:
        gram_in, refs = refs[0], refs[1:]
    outs, gram_out = refs[:6], refs[6]
    gram, cross = forward_rows(cfg, xs, weights, outs)
    rank = cfg["rank"]
    gram_out[:, :rank] = gram if first else gram_in[:, :rank] + gram
    gram_out[:, rank:] = cross if first else gram_in[:, rank:] + cross


def last_kernel(cfg, early, count, *refs):
    groups = []
    for size in early:
        groups.append((refs[:size], refs[size : size + 6]))
        refs = refs[size + 6 :]
    xs, refs = refs[:count], refs[count:]
    weights, refs = refs[:7], refs[7:]
    gram_in, send_ref, keep_ref = refs[:3]
    outs, part_ref = refs[3:9], refs[9]
    rank, block, rows, obs_pad = cfg["rank"], cfg["block"], cfg["rows"], cfg["obs_pad"]
    group, replicas = cfg["group"], cfg["replicas"]
    factor = 1.0 / math.sqrt(cfg["total"])
    c1, c2, c3 = cfg["cols"]
    gram, cross = forward_rows(cfg, xs, weights, outs)
    gram_hi, gram_lo = split_two(gram_in[:, :rank] + gram)
    cross_hi, cross_lo = split_two(gram_in[:, rank:] + cross)
    groups.append((xs, outs))
    me = pl.multiple_of(lax.axis_index("dp") * block, ROW_TILE)
    fo = weights[2][pl.ds(me, block), :]
    bo = weights[3][pl.ds(me, block), :]
    few = [item for item in groups if len(item[0]) == 1]
    many = [item for item in groups if len(item[0]) > 1]
    square = jnp.zeros((1, rank), F32)
    diagonal = jnp.zeros((1, rank), F32)
    f_deltas, b_deltas, f_hids, b_hids, d_fs, d_us, wholes, laters = ([] for _ in range(8))
    for members in (few, many):
        if not members:
            continue
        saved = list(zip(*(item[1] for item in members)))
        emb32 = stack(saved[2], 0).astype(F32)
        target = join([x_ref[0:rows, obs_pad:] for item in members for x_ref in item[0]], 0)
        error = emb32 - GAMMA * target.astype(F32)
        err_hi, err_lo = split_two(error)
        u = stack(saved[3], 0)
        scale = lax.rsqrt(jnp.mean(u * u, axis=-1, keepdims=True) + EPSILON)
        back = (u * scale).astype(BF16)
        back32 = back.astype(F32)
        pulled = dot_nn(err_hi, gram_hi) + (dot_nn(err_hi, gram_lo) + dot_nn(err_lo, gram_hi))
        square = square + jnp.sum(pulled * error, axis=0, keepdims=True)
        diagonal = diagonal + jnp.sum(emb32 * back32, axis=0, keepdims=True)
        d_f = (factor * (pulled / group - back32)).astype(BF16)
        pushed = dot_nn(back, cross_hi) + dot_nn(back, cross_lo)
        d_b = factor * (pushed / group - emb32)
        inner = jnp.mean(u * d_b, axis=-1, keepdims=True)
        d_u = (scale * d_b - u * (scale * scale * scale * inner)).astype(BF16)
        f_hid, b_hid = stack(saved[4], 1), stack(saved[5], 1)
        zero = jnp.zeros_like(f_hid)
        f_deltas.append(jnp.where(f_hid > 0, dot_nt(fo, d_f).astype(BF16), zero))
        b_deltas.append(jnp.where(b_hid > 0, dot_nt(bo, d_u).astype(BF16), zero))
        f_hids.append(f_hid)
        b_hids.append(b_hid)
        d_fs.append(d_f)
        d_us.append(d_u)
        wholes += saved[0]
        laters += saved[1]
    part_ref[:, :c1] = dot_nn(join(f_deltas, 1), stack(wholes, 0))
    part_ref[:, c1:c2] = dot_nn(join(f_hids, 1), join(d_fs, 0))
    part_ref[:, c2:c3] = dot_nn(join(b_deltas, 1), stack(laters, 0))
    part_ref[:, c3:] = dot_nn(join(b_hids, 1), join(d_us, 0))
    loss = (0.5 / group) * jnp.sum(square) - jnp.sum(diagonal)
    lanes = lax.broadcasted_iota(jnp.int32, (block, LANES), 1)
    spot = cfg["loss_spot"]
    base = spot // LANES * LANES
    first = spot - base + 3 * lax.axis_index("replica")
    rest = jnp.full((block, LANES), loss, F32)
    piece_tile = part_ref[:, base : base + LANES]
    piece_tile = jnp.where(lanes >= spot - base, 0.0, piece_tile)
    for j in range(3):
        piece = rest.astype(BF16).astype(F32)
        piece_tile = jnp.where(lanes == first + j, piece, piece_tile)
        rest = rest - piece
    part_ref[:, base : base + LANES] = piece_tile
    core = lax.rem(lax.axis_index("replica"), 2)
    half = block // 2
    keep_ref[...] = part_ref[pl.ds(pl.multiple_of(core * half, ROW_TILE), half), :]
    other = pl.multiple_of((1 - core) * half, ROW_TILE)
    send_ref[...] = part_ref[pl.ds(other, half), :].astype(BF16)


def finish_kernel(cfg, one_ref, two_ref, far_ref, fs, fa, fl, fo, bs, bo, loss_ref, act_ref):
    obs, act, rank, x_pad, obs_pad = (cfg[k] for k in ("obs", "act", "rank", "x_pad", "obs_pad"))
    half = cfg["block"] // 2
    c1, c2, c3 = cfg["cols"]
    core = lax.rem(lax.axis_index("replica"), 2)
    mine32 = one_ref[...].astype(F32) + two_ref[...].astype(F32)
    mine = mine32.astype(BF16)
    far = far_ref[...]
    for start, value in ((core * half, mine), ((1 - core) * half, far)):
        here = pl.ds(pl.multiple_of(start, ROW_TILE), half)
        fs[here, :] = value[:, :obs]
        fl[here, :] = value[:, x_pad:c1]
        fo[here, :] = value[:, c1:c2]
        bs[here, :] = value[:, c2 : c2 + obs]
        bo[here, :] = value[:, c3:]
        act_ref[here, :] = value[:, obs_pad : obs_pad + LANES].astype(F32)
    fa[...] = act_ref[...].T[:act].astype(BF16)
    spot = cfg["loss_spot"]
    base = spot // LANES * LANES
    pieces = mine32[0:8, base : base + LANES]
    lanes = lax.broadcasted_iota(jnp.int32, (8, LANES), 1)
    rows = lax.broadcasted_iota(jnp.int32, (8, LANES), 0)
    ours = (lanes >= spot - base) & (lanes < spot - base + 3 * cfg["replicas"]) & (rows == 0)
    loss_ref[0, 0] = jnp.sum(jnp.where(ours, pieces, 0.0)) / cfg["total"]


def exchange(array, axis, size, bit):
    return lax.ppermute(array, axis, [(i, i ^ bit) for i in range(size)])


def shape(dims, kind):
    return jax.ShapeDtypeStruct(dims, kind)


def fast_local(
    states,
    actions,
    target_forward,
    next_index,
    latent_ids,
    latents,
    f_state,
    f_action,
    f_latent,
    f_output,
    b_state,
    b_output,
):
    size = lax.axis_size("dp")
    replicas = lax.axis_size("replica")
    rows, obs = states.shape[1:]
    act = actions.shape[2]
    zcount, rank = latents.shape
    hidden = f_state.shape[1]
    block = hidden // size
    group = rows * size
    side = round_up(act + 2, 2 * ROW_TILE)
    lane = round_up(rows, LANES)
    obs_pad = round_up(obs, LANES)
    x_pad = obs_pad + LANES
    c1 = x_pad + rank
    c2 = c1 + rank
    c3 = c2 + obs_pad
    width = c3 + rank
    cfg = dict(
        rows=rows,
        obs=obs,
        act=act,
        rank=rank,
        obs_pad=obs_pad,
        x_pad=x_pad,
        hidden=hidden,
        zcount=zcount,
        side=side,
        lane=lane,
        group=group,
        replicas=replicas,
        total=group * replicas,
        block=block,
        tile=512,
        cols=(c1, c2, c3),
        loss_spot=obs_pad + side,
    )
    params = pltpu.CompilerParams(vmem_limit_bytes=20 * 1024 * 1024)
    last_params = pltpu.CompilerParams(vmem_limit_bytes=28 * 1024 * 1024)
    own = pl.pallas_call(
        functools.partial(pack_kernel, cfg),
        out_shape=shape((rows + side // 2, obs_pad + rank), BF16),
        scratch_shapes=[pltpu.VMEM((side, lane), F32)],
        compiler_params=pltpu.CompilerParams(vmem_limit_bytes=VMEM_LIMIT),
        name="pack",
    )(states, actions[0].T, next_index, latent_ids, target_forward)
    x = {"own": own}
    middle = [(2 + i, 4 + i) for i in range(2)] + [(4 + i, 2 + i) for i in range(2)]
    outward = [(2 + i, i) for i in range(2)] + [(4 + i, 6 + i) for i in range(2)]
    across = lax.ppermute(own, "dp", middle)
    x["x own"] = exchange(own, "dp", size, 1)
    x["half"] = exchange(own, "dp", size, 2)
    handed = lax.ppermute(across, "dp", outward)
    x["x half"] = exchange(x["half"], "dp", size, 1)
    across_two = lax.ppermute(x["half"], "dp", middle)
    x["second"] = across + handed
    x["x second"] = exchange(x["second"], "dp", size, 1)
    handed_two = lax.ppermute(across_two, "dp", outward)
    x["third"] = across_two + handed_two
    x["x third"] = exchange(x["third"], "dp", size, 1)
    wf, wb, wfb, wbb = pl.pallas_call(
        functools.partial(weights_kernel, cfg),
        out_shape=(
            shape((x_pad + rank, hidden), BF16),
            shape((obs_pad, hidden), BF16),
            shape((block, x_pad + rank), BF16),
            shape((block, obs_pad), BF16),
        ),
        in_specs=[pl.BlockSpec(memory_space=pl.ANY)] * 4,
        scratch_shapes=[
            pltpu.VMEM((obs, hidden), BF16),
            pltpu.VMEM((act, hidden), BF16),
            pltpu.VMEM((rank, hidden), BF16),
            pltpu.VMEM((obs, hidden), BF16),
            pltpu.SemaphoreType.DMA((4,)),
        ],
        compiler_params=pltpu.CompilerParams(vmem_limit_bytes=16 * 1024 * 1024),
        cost_estimate=pl.CostEstimate(flops=0, bytes_accessed=1_000_000, transcendentals=0),
        name="weights",
    )(*(pltpu.with_memory_space_constraint(w, pltpu.HBM) for w in (f_state, f_action, f_latent, b_state)))
    weights = (wf, wb, f_output, b_output, latents, wfb, wbb)
    row_flops = 2 * (c1 + 2 * rank + obs_pad) * hidden + 8 * rank * rank

    def kept(count):
        m = rows * count
        return (
            ((m, x_pad + rank), BF16),
            ((m, obs_pad), BF16),
            ((m, rank), BF16),
            ((m, rank), F32),
            ((block, m), BF16),
            ((block, m), BF16),
        )

    grams = ()
    plan = (
        (("own",), 3.0),
        (("half",), 2.0),
        (("x own",), 1.5),
        (("x half", "second"), 1.0),
        (("third", "x second"), 3.0),
    )
    early = []
    for steps, work in plan:
        count = len(steps)
        xs = [x[step] for step in steps]
        *saved, total_grams = pl.pallas_call(
            functools.partial(forward_kernel, cfg, count, not early),
            out_shape=(*(shape(*item) for item in kept(count)), shape((rank, 2 * rank), F32)),
            compiler_params=params,
            cost_estimate=pl.CostEstimate(
                flops=int(work * rows * count * row_flops),
                bytes_accessed=1_000_000,
                transcendentals=0,
            ),
            name="forward",
        )(*xs, *weights, *grams)
        grams = (total_grams,)
        early.append((xs, saved))
    left = [x["x third"]]
    operands = []
    for xs, saved in early:
        operands += [*xs, *saved]
    send, keep = pl.pallas_call(
        functools.partial(last_kernel, cfg, [len(xs) for xs, _ in early], len(left)),
        out_shape=(shape((block // 2, width), BF16), shape((block // 2, width), F32)),
        scratch_shapes=[
            *(pltpu.VMEM(*item) for item in kept(len(left))),
            pltpu.VMEM((block, width), F32),
        ],
        compiler_params=last_params,
        cost_estimate=pl.CostEstimate(
            flops=4 * group * width * block, bytes_accessed=16_000_000, transcendentals=0
        ),
        name="last",
    )(*operands, *left, *weights, *grams)
    got = exchange(send, "replica", replicas, 1)
    one = (keep + got.astype(F32)).astype(BF16)
    two = exchange(one, "replica", replicas, 2)
    mine = (one.astype(F32) + two.astype(F32)).astype(BF16)
    far = exchange(mine, "replica", replicas, 1)
    fs, fa, fl, fo, bs, bo, loss = pl.pallas_call(
        functools.partial(finish_kernel, cfg),
        out_shape=(
            shape((block, obs), BF16),
            shape((act, block), BF16),
            shape((block, rank), BF16),
            shape((block, rank), BF16),
            shape((block, obs), BF16),
            shape((block, rank), BF16),
            shape((1, 1), F32),
        ),
        out_specs=(
            *(pl.BlockSpec(memory_space=pltpu.VMEM) for _ in range(6)),
            pl.BlockSpec(memory_space=pltpu.SMEM),
        ),
        scratch_shapes=[pltpu.VMEM((block, LANES), F32)],
        compiler_params=pltpu.CompilerParams(vmem_limit_bytes=16 * 1024 * 1024),
        name="finish",
    )(one, two, far)
    return (fs.T, fa, fl.T, fo, bs.T, bo, loss.reshape(()))


def forward_pass(
    current, later, moves, latent_rows, f_state, f_action, f_latent, f_output, b_state, b_output
):
    f_pre = (
        jnp.dot(current, f_state, preferred_element_type=F32)
        + jnp.dot(moves, f_action, preferred_element_type=F32)
        + jnp.dot(latent_rows, f_latent, preferred_element_type=F32)
    )
    f_hidden = jnp.maximum(f_pre, 0.0).astype(BF16)
    forward_emb = jnp.dot(f_hidden, f_output, preferred_element_type=F32).astype(BF16)
    b_pre = jnp.dot(later, b_state, preferred_element_type=F32)
    b_hidden = jnp.maximum(b_pre, 0.0).astype(BF16)
    b_raw = jnp.dot(b_hidden, b_output, preferred_element_type=F32)
    b_scale = lax.rsqrt(jnp.mean(b_raw * b_raw, axis=-1, keepdims=True) + EPSILON)
    backward_emb = (b_raw * b_scale).astype(BF16)
    return (f_pre, f_hidden, forward_emb, b_pre, b_hidden, b_raw, b_scale, backward_emb)


def general_local(
    states,
    actions,
    target_forward,
    next_index,
    latent_ids,
    latents,
    f_state,
    f_action,
    f_latent,
    f_output,
    b_state,
    b_output,
):
    current = states[0]
    moves = actions[0]
    later = jnp.take(current, next_index[0], axis=0)
    latent_rows = jnp.take(latents, latent_ids[0], axis=0)
    f_pre, f_hidden, forward_emb, b_pre, b_hidden, b_raw, b_scale, backward_emb = forward_pass(
        current, later, moves, latent_rows, f_state, f_action, f_latent, f_output, b_state, b_output
    )
    group = current.shape[0] * lax.axis_size("dp")
    total = group * lax.axis_size("replica")
    factor = 1.0 / math.sqrt(total)
    forward32 = forward_emb.astype(F32)
    back32 = backward_emb.astype(F32)
    error = forward32 - GAMMA * target_forward[0].astype(F32)
    gram, cross = lax.psum(
        (
            jnp.dot(backward_emb.T, backward_emb, preferred_element_type=F32),
            jnp.dot(forward32.T, error, precision=HIGH, preferred_element_type=F32),
        ),
        "dp",
    )
    pulled = jnp.dot(error, gram, precision=HIGH, preferred_element_type=F32)
    pushed = jnp.dot(back32, cross.T, precision=HIGH, preferred_element_type=F32)
    partial_loss = 0.5 / group * jnp.sum(pulled * error) - jnp.sum(forward32 * back32)
    grad_forward = (factor * (pulled / group - back32)).astype(BF16)
    grad_backward = factor * (pushed / group - forward32)
    inner = jnp.mean(b_raw * grad_backward, axis=-1, keepdims=True)
    grad_raw = (b_scale * grad_backward - b_raw * b_scale * b_scale * b_scale * inner).astype(BF16)
    part_bo = jnp.dot(b_hidden.T, grad_raw, preferred_element_type=F32)
    b_back = jnp.dot(grad_raw, b_output.T, preferred_element_type=F32)
    b_delta = jnp.where(b_pre > 0, b_back, 0.0).astype(BF16)
    part_bs = jnp.dot(later.T, b_delta, preferred_element_type=F32)
    part_fo = jnp.dot(f_hidden.T, grad_forward, preferred_element_type=F32)
    f_back = jnp.dot(grad_forward, f_output.T, preferred_element_type=F32)
    f_delta = jnp.where(f_pre > 0, f_back, 0.0).astype(BF16)
    part_fs = jnp.dot(current.T, f_delta, preferred_element_type=F32)
    part_fa = jnp.dot(moves.T, f_delta, preferred_element_type=F32)
    part_fl = jnp.dot(latent_rows.T, f_delta, preferred_element_type=F32)
    places = (1, 1, 1, 0, 1, 0)
    parts = (part_fs, part_fa, part_fl, part_fo, part_bs, part_bo)
    shares = tuple(
        lax.psum_scatter(part, "dp", scatter_dimension=place, tiled=True)
        for part, place in zip(parts, places)
    )
    summed = lax.psum(shares, "replica")
    loss_sum = lax.psum(partial_loss, ("dp", "replica"))
    return (*(item.astype(BF16) for item in summed), loss_sum / total)


def local(*args):
    size, replicas = lax.axis_size("dp"), lax.axis_size("replica")
    rows, hidden = args[0].shape[1], args[6].shape[1]
    fits = size == 8 and replicas == 4 and rows * size <= KERNEL_GROUP_LIMIT
    block = hidden // size
    whole = rows % ROW_TILE == 0 and hidden % (size * 64) == 0 and hidden % 512 == 0
    whole = whole and LANES < block <= 2 * LANES - 64 and args[6].shape[0] % 8 == 0
    exact = rows <= 256 and args[5].shape[0] <= 256
    return (fast_local if fits and whole and exact else general_local)(*args)


def solution(mesh):
    in_specs = (
        P("replica", "dp", None),
        P("replica", "dp", None),
        P("replica", "dp", None),
        P("replica", "dp"),
        P("replica", "dp"),
        P(),
        P(),
        P(),
        P(),
        P(),
        P(),
        P(),
    )
    out_specs = (
        P(None, "dp"),
        P(None, "dp"),
        P(None, "dp"),
        P("dp", None),
        P(None, "dp"),
        P("dp", None),
        P(),
    )
    return jax.shard_map(local, mesh=mesh, in_specs=in_specs, out_specs=out_specs, check_vma=False)
```

```python
import functools
import math

import jax
import jax.numpy as jnp
from jax import lax
from jax.experimental import pallas as pl
from jax.experimental.pallas import tpu as pltpu
from jax.sharding import PartitionSpec as P

GAMMA = 0.98
EPSILON = 1e-06
HIGH = lax.Precision.HIGHEST
BF16 = jnp.bfloat16
F32 = jnp.float32
LANES = 128
ROW_TILE = 16
VMEM_LIMIT = 56 * 1024 * 1024
KERNEL_GROUP_LIMIT = 2048


def round_up(value, unit):
    return -(-value // unit) * unit


def dot_nn(left, right):
    return lax.dot_general(left, right, (((1,), (0,)), ((), ())), preferred_element_type=F32)


def dot_nt(left, right):
    return lax.dot_general(left, right, (((1,), (1,)), ((), ())), preferred_element_type=F32)


def dot_tn(left, right):
    return lax.dot_general(left, right, (((0,), (0,)), ((), ())), preferred_element_type=F32)


def join(values, axis):
    return jnp.concatenate(values, axis=axis) if len(values) > 1 else values[0]


def stack(refs, axis):
    return join([ref[...] for ref in refs], axis)


def split_two(value):
    high = value.astype(BF16)
    return high, (value - high.astype(F32)).astype(BF16)


def pack_kernel(cfg, state_ref, move_ref, next_ref, latent_ref, target_ref, out_ref, side_ref):
    rows, obs, act, obs_pad, side = (cfg[k] for k in ("rows", "obs", "act", "obs_pad", "side"))
    lane = side_ref.shape[1]
    side_ref[...] = jnp.zeros_like(side_ref)
    side_ref[0:act, 0:rows] = move_ref[...].astype(F32)
    side_ref[act : act + 1, 0:rows] = next_ref[...].astype(F32)
    side_ref[act + 1 : act + 2, 0:rows] = latent_ref[...].astype(F32)
    gap = jnp.zeros((rows, obs_pad - obs), BF16)
    out_ref[0:rows, 0:obs_pad] = jnp.concatenate([state_ref[0], gap], axis=1)
    out_ref[0:rows, obs_pad:] = target_ref[0]
    half = side // 2
    out_ref[rows:, :] = jnp.zeros((half, out_ref.shape[1]), BF16)
    out_ref[rows:, 0:lane] = side_ref[0:half, :].astype(BF16)
    out_ref[rows:, lane : 2 * lane] = side_ref[half:side, :].astype(BF16)


def weights_kernel(cfg, fs_hbm, fa_hbm, fl_hbm, bs_hbm, *refs):
    obs, obs_pad, x_pad = cfg["obs"], cfg["obs_pad"], cfg["x_pad"]
    hidden, block, act = cfg["hidden"], cfg["block"], cfg["act"]
    wf_ref, wb_ref, wfb_ref, wbb_ref, fs_ref, fa_ref, fl_ref, bs_ref, sems = refs
    pairs = ((fs_hbm, fs_ref), (bs_hbm, bs_ref), (fl_hbm, fl_ref), (fa_hbm, fa_ref))
    copies = [pltpu.make_async_copy(a, b, sems.at[i]) for i, (a, b) in enumerate(pairs)]
    for copy in copies:
        copy.start()
    gap = jnp.zeros((obs_pad - obs, hidden), BF16)
    wf_ref[obs_pad:x_pad, :] = jnp.zeros((x_pad - obs_pad, hidden), BF16)
    copies[0].wait()
    wf_ref[0:obs_pad, :] = jnp.concatenate([fs_ref[...], gap], axis=0)
    copies[1].wait()
    wb_ref[...] = jnp.concatenate([bs_ref[...], gap], axis=0)
    copies[2].wait()
    wf_ref[x_pad:, :] = fl_ref[...]
    copies[3].wait()
    wf_ref[obs_pad : obs_pad + act, :] = fa_ref[...]
    me = lax.axis_index("dp")
    start = me * block
    base = pl.multiple_of(start // LANES * LANES, LANES)
    odd = lax.rem(me, 2) == 1
    span = pl.ds(base, 2 * LANES)

    def pick(ref):
        near = ref[:, span].astype(F32).T
        return jnp.where(odd, near[2 * LANES - block :], near[:block]).astype(BF16)

    wfb_ref[...] = pick(wf_ref)
    wbb_ref[...] = pick(wb_ref)


def forward_rows(cfg, xs, weights, outs):
    wf_ref, wb_ref, fo_ref, bo_ref, lat_ref, wfb_ref, wbb_ref = weights
    a_ref, later_ref, f_ref, u_ref, fh_ref, bh_ref = outs
    rows, act, rank, side = cfg["rows"], cfg["act"], cfg["rank"], cfg["side"]
    obs_pad, x_pad, hidden, zcount = cfg["obs_pad"], cfg["x_pad"], cfg["hidden"], cfg["zcount"]
    tile, lane = cfg["tile"], cfg["lane"]
    half = side // 2
    row_spots = lax.broadcasted_iota(jnp.int32, (rows, rows), 1).astype(F32)
    spots = lax.broadcasted_iota(jnp.int32, (rows, zcount), 1).astype(F32)
    blank = jnp.zeros((rows, x_pad - obs_pad - side), BF16)
    for j, x_ref in enumerate(xs):
        here = slice(j * rows, (j + 1) * rows)
        few = jnp.concatenate(
            [x_ref[rows:, 0:lane].astype(F32), x_ref[rows:, lane : 2 * lane].astype(F32)], axis=0
        ).T[:rows]
        near = x_ref[0:rows, 0:obs_pad]
        picks = jnp.where(few[:, act + 1 : act + 2] == spots, 1.0, 0.0).astype(BF16)
        hot = jnp.where(few[:, act : act + 1] == row_spots, 1.0, 0.0).astype(BF16)
        a_ref[here, 0:obs_pad] = near
        a_ref[here, obs_pad:x_pad] = jnp.concatenate([few.astype(BF16), blank], axis=1)
        a_ref[here, x_pad:] = dot_nn(picks, lat_ref[...]).astype(BF16)
        later_ref[here, :] = dot_nn(hot, near).astype(BF16)
    whole = a_ref[...]
    later = later_ref[...]
    tiles = [slice(n, n + tile) for n in range(0, hidden, tile)]
    hs = [jnp.maximum(dot_nn(whole, wf_ref[:, part]), 0.0).astype(BF16) for part in tiles]
    emb = dot_nn(join(hs, 1), fo_ref[...]).astype(BF16)
    gs = [jnp.maximum(dot_nn(later, wb_ref[:, part]), 0.0).astype(BF16) for part in tiles]
    u = dot_nn(join(gs, 1), bo_ref[...])
    back = (u * lax.rsqrt(jnp.mean(u * u, axis=-1, keepdims=True) + EPSILON)).astype(BF16)
    f_ref[...] = emb
    u_ref[...] = u
    fh_ref[...] = jnp.maximum(dot_nt(wfb_ref[...], whole), 0.0).astype(BF16)
    bh_ref[...] = jnp.maximum(dot_nt(wbb_ref[...], later), 0.0).astype(BF16)
    cross = dot_tn(emb, emb)
    for j, x_ref in enumerate(xs):
        cross = cross - GAMMA * dot_tn(x_ref[0:rows, obs_pad:], emb[j * rows : (j + 1) * rows])
    return dot_tn(back, back), cross


def forward_kernel(cfg, count, first, *refs):
    xs, refs = refs[:count], refs[count:]
    weights, refs = refs[:7], refs[7:]
    if not first:
        gram_in, refs = refs[0], refs[1:]
    outs, gram_out = refs[:6], refs[6]
    gram, cross = forward_rows(cfg, xs, weights, outs)
    rank = cfg["rank"]
    gram_out[:, :rank] = gram if first else gram_in[:, :rank] + gram
    gram_out[:, rank:] = cross if first else gram_in[:, rank:] + cross


def last_kernel(cfg, early, count, *refs):
    groups = []
    for size in early:
        groups.append((refs[:size], refs[size : size + 6]))
        refs = refs[size + 6 :]
    xs, refs = refs[:count], refs[count:]
    weights, refs = refs[:7], refs[7:]
    gram_in, send_ref, keep_ref = refs[:3]
    outs, part_ref = refs[3:9], refs[9]
    rank, block, rows, obs_pad = cfg["rank"], cfg["block"], cfg["rows"], cfg["obs_pad"]
    group, replicas = cfg["group"], cfg["replicas"]
    factor = 1.0 / math.sqrt(cfg["total"])
    c1, c2, c3 = cfg["cols"]
    gram, cross = forward_rows(cfg, xs, weights, outs)
    gram_hi, gram_lo = split_two(gram_in[:, :rank] + gram)
    cross_hi, cross_lo = split_two(gram_in[:, rank:] + cross)
    groups.append((xs, outs))
    me = pl.multiple_of(lax.axis_index("dp") * block, ROW_TILE)
    fo = weights[2][pl.ds(me, block), :]
    bo = weights[3][pl.ds(me, block), :]
    few = [item for item in groups if len(item[0]) == 1]
    many = [item for item in groups if len(item[0]) > 1]
    square = jnp.zeros((1, rank), F32)
    diagonal = jnp.zeros((1, rank), F32)
    f_deltas, b_deltas, f_hids, b_hids, d_fs, d_us, wholes, laters = ([] for _ in range(8))
    for members in (few, many):
        if not members:
            continue
        saved = list(zip(*(item[1] for item in members)))
        emb32 = stack(saved[2], 0).astype(F32)
        target = join([x_ref[0:rows, obs_pad:] for item in members for x_ref in item[0]], 0)
        error = emb32 - GAMMA * target.astype(F32)
        err_hi, err_lo = split_two(error)
        u = stack(saved[3], 0)
        scale = lax.rsqrt(jnp.mean(u * u, axis=-1, keepdims=True) + EPSILON)
        back = (u * scale).astype(BF16)
        back32 = back.astype(F32)
        pulled = dot_nn(err_hi, gram_hi) + (dot_nn(err_hi, gram_lo) + dot_nn(err_lo, gram_hi))
        square = square + jnp.sum(pulled * error, axis=0, keepdims=True)
        diagonal = diagonal + jnp.sum(emb32 * back32, axis=0, keepdims=True)
        d_f = (factor * (pulled / group - back32)).astype(BF16)
        pushed = dot_nn(back, cross_hi) + dot_nn(back, cross_lo)
        d_b = factor * (pushed / group - emb32)
        inner = jnp.mean(u * d_b, axis=-1, keepdims=True)
        d_u = (scale * d_b - u * (scale * scale * scale * inner)).astype(BF16)
        f_hid, b_hid = stack(saved[4], 1), stack(saved[5], 1)
        zero = jnp.zeros_like(f_hid)
        f_deltas.append(jnp.where(f_hid > 0, dot_nt(fo, d_f).astype(BF16), zero))
        b_deltas.append(jnp.where(b_hid > 0, dot_nt(bo, d_u).astype(BF16), zero))
        f_hids.append(f_hid)
        b_hids.append(b_hid)
        d_fs.append(d_f)
        d_us.append(d_u)
        wholes += saved[0]
        laters += saved[1]
    part_ref[:, :c1] = dot_nn(join(f_deltas, 1), stack(wholes, 0))
    part_ref[:, c1:c2] = dot_nn(join(f_hids, 1), join(d_fs, 0))
    part_ref[:, c2:c3] = dot_nn(join(b_deltas, 1), stack(laters, 0))
    part_ref[:, c3:] = dot_nn(join(b_hids, 1), join(d_us, 0))
    loss = (0.5 / group) * jnp.sum(square) - jnp.sum(diagonal)
    lanes = lax.broadcasted_iota(jnp.int32, (block, LANES), 1)
    spot = cfg["loss_spot"]
    base = spot // LANES * LANES
    first = spot - base + 3 * lax.axis_index("replica")
    rest = jnp.full((block, LANES), loss, F32)
    piece_tile = part_ref[:, base : base + LANES]
    piece_tile = jnp.where(lanes >= spot - base, 0.0, piece_tile)
    for j in range(3):
        piece = rest.astype(BF16).astype(F32)
        piece_tile = jnp.where(lanes == first + j, piece, piece_tile)
        rest = rest - piece
    part_ref[:, base : base + LANES] = piece_tile
    core = lax.rem(lax.axis_index("replica"), 2)
    half = block // 2
    keep_ref[...] = part_ref[pl.ds(pl.multiple_of(core * half, ROW_TILE), half), :]
    other = pl.multiple_of((1 - core) * half, ROW_TILE)
    send_ref[...] = part_ref[pl.ds(other, half), :].astype(BF16)


def finish_kernel(cfg, one_ref, two_ref, far_ref, fs, fa, fl, fo, bs, bo, loss_ref, act_ref):
    obs, act, rank, x_pad, obs_pad = (cfg[k] for k in ("obs", "act", "rank", "x_pad", "obs_pad"))
    half = cfg["block"] // 2
    c1, c2, c3 = cfg["cols"]
    core = lax.rem(lax.axis_index("replica"), 2)
    mine32 = one_ref[...].astype(F32) + two_ref[...].astype(F32)
    mine = mine32.astype(BF16)
    far = far_ref[...]
    for start, value in ((core * half, mine), ((1 - core) * half, far)):
        here = pl.ds(pl.multiple_of(start, ROW_TILE), half)
        fs[here, :] = value[:, :obs]
        fl[here, :] = value[:, x_pad:c1]
        fo[here, :] = value[:, c1:c2]
        bs[here, :] = value[:, c2 : c2 + obs]
        bo[here, :] = value[:, c3:]
        act_ref[here, :] = value[:, obs_pad : obs_pad + LANES].astype(F32)
    fa[...] = act_ref[...].T[:act].astype(BF16)
    spot = cfg["loss_spot"]
    base = spot // LANES * LANES
    pieces = mine32[0:8, base : base + LANES]
    lanes = lax.broadcasted_iota(jnp.int32, (8, LANES), 1)
    rows = lax.broadcasted_iota(jnp.int32, (8, LANES), 0)
    ours = (lanes >= spot - base) & (lanes < spot - base + 3 * cfg["replicas"]) & (rows == 0)
    loss_ref[0, 0] = jnp.sum(jnp.where(ours, pieces, 0.0)) / cfg["total"]


def exchange(array, axis, size, bit):
    return lax.ppermute(array, axis, [(i, i ^ bit) for i in range(size)])


def shape(dims, kind):
    return jax.ShapeDtypeStruct(dims, kind)


def fast_local(
    states,
    actions,
    target_forward,
    next_index,
    latent_ids,
    latents,
    f_state,
    f_action,
    f_latent,
    f_output,
    b_state,
    b_output,
):
    size = lax.axis_size("dp")
    replicas = lax.axis_size("replica")
    rows, obs = states.shape[1:]
    act = actions.shape[2]
    zcount, rank = latents.shape
    hidden = f_state.shape[1]
    block = hidden // size
    group = rows * size
    side = round_up(act + 2, 2 * ROW_TILE)
    lane = round_up(rows, LANES)
    obs_pad = round_up(obs, LANES)
    x_pad = obs_pad + LANES
    c1 = x_pad + rank
    c2 = c1 + rank
    c3 = c2 + obs_pad
    width = c3 + rank
    cfg = dict(
        rows=rows,
        obs=obs,
        act=act,
        rank=rank,
        obs_pad=obs_pad,
        x_pad=x_pad,
        hidden=hidden,
        zcount=zcount,
        side=side,
        lane=lane,
        group=group,
        replicas=replicas,
        total=group * replicas,
        block=block,
        tile=256,
        cols=(c1, c2, c3),
        loss_spot=obs_pad + side,
    )
    params = pltpu.CompilerParams(vmem_limit_bytes=20 * 1024 * 1024)
    last_params = pltpu.CompilerParams(vmem_limit_bytes=28 * 1024 * 1024)
    own = pl.pallas_call(
        functools.partial(pack_kernel, cfg),
        out_shape=shape((rows + side // 2, obs_pad + rank), BF16),
        scratch_shapes=[pltpu.VMEM((side, lane), F32)],
        compiler_params=pltpu.CompilerParams(vmem_limit_bytes=VMEM_LIMIT),
        name="pack",
    )(states, actions[0].T, next_index, latent_ids, target_forward)
    x = {"own": own}
    middle = [(2 + i, 4 + i) for i in range(2)] + [(4 + i, 2 + i) for i in range(2)]
    outward = [(2 + i, i) for i in range(2)] + [(4 + i, 6 + i) for i in range(2)]
    across = lax.ppermute(own, "dp", middle)
    x["x own"] = exchange(own, "dp", size, 1)
    x["half"] = exchange(own, "dp", size, 2)
    handed = lax.ppermute(across, "dp", outward)
    x["x half"] = exchange(x["half"], "dp", size, 1)
    across_two = lax.ppermute(x["half"], "dp", middle)
    x["second"] = across + handed
    x["x second"] = exchange(x["second"], "dp", size, 1)
    handed_two = lax.ppermute(across_two, "dp", outward)
    x["third"] = across_two + handed_two
    x["x third"] = exchange(x["third"], "dp", size, 1)
    wf, wb, wfb, wbb = pl.pallas_call(
        functools.partial(weights_kernel, cfg),
        out_shape=(
            shape((x_pad + rank, hidden), BF16),
            shape((obs_pad, hidden), BF16),
            shape((block, x_pad + rank), BF16),
            shape((block, obs_pad), BF16),
        ),
        in_specs=[pl.BlockSpec(memory_space=pl.ANY)] * 4,
        scratch_shapes=[
            pltpu.VMEM((obs, hidden), BF16),
            pltpu.VMEM((act, hidden), BF16),
            pltpu.VMEM((rank, hidden), BF16),
            pltpu.VMEM((obs, hidden), BF16),
            pltpu.SemaphoreType.DMA((4,)),
        ],
        compiler_params=pltpu.CompilerParams(vmem_limit_bytes=16 * 1024 * 1024),
        cost_estimate=pl.CostEstimate(flops=0, bytes_accessed=1_000_000, transcendentals=0),
        name="weights",
    )(*(pltpu.with_memory_space_constraint(w, pltpu.HBM) for w in (f_state, f_action, f_latent, b_state)))
    weights = (wf, wb, f_output, b_output, latents, wfb, wbb)
    row_flops = 2 * (c1 + 2 * rank + obs_pad) * hidden + 8 * rank * rank

    def kept(count):
        m = rows * count
        return (
            ((m, x_pad + rank), BF16),
            ((m, obs_pad), BF16),
            ((m, rank), BF16),
            ((m, rank), F32),
            ((block, m), BF16),
            ((block, m), BF16),
        )

    grams = ()
    plan = (
        (("own",), 3.0),
        (("half",), 2.0),
        (("x own",), 1.5),
        (("x half", "second"), 1.0),
        (("third", "x second"), 3.0),
    )
    early = []
    for steps, work in plan:
        count = len(steps)
        xs = [x[step] for step in steps]
        *saved, total_grams = pl.pallas_call(
            functools.partial(forward_kernel, cfg, count, not early),
            out_shape=(*(shape(*item) for item in kept(count)), shape((rank, 2 * rank), F32)),
            compiler_params=params,
            cost_estimate=pl.CostEstimate(
                flops=int(work * rows * count * row_flops),
                bytes_accessed=1_000_000,
                transcendentals=0,
            ),
            name="forward",
        )(*xs, *weights, *grams)
        grams = (total_grams,)
        early.append((xs, saved))
    left = [x["x third"]]
    operands = []
    for xs, saved in early:
        operands += [*xs, *saved]
    send, keep = pl.pallas_call(
        functools.partial(last_kernel, cfg, [len(xs) for xs, _ in early], len(left)),
        out_shape=(shape((block // 2, width), BF16), shape((block // 2, width), F32)),
        scratch_shapes=[
            *(pltpu.VMEM(*item) for item in kept(len(left))),
            pltpu.VMEM((block, width), F32),
        ],
        compiler_params=last_params,
        cost_estimate=pl.CostEstimate(
            flops=4 * group * width * block, bytes_accessed=16_000_000, transcendentals=0
        ),
        name="last",
    )(*operands, *left, *weights, *grams)
    got = exchange(send, "replica", replicas, 1)
    one = (keep + got.astype(F32)).astype(BF16)
    two = exchange(one, "replica", replicas, 2)
    mine = (one.astype(F32) + two.astype(F32)).astype(BF16)
    far = exchange(mine, "replica", replicas, 1)
    fs, fa, fl, fo, bs, bo, loss = pl.pallas_call(
        functools.partial(finish_kernel, cfg),
        out_shape=(
            shape((block, obs), BF16),
            shape((act, block), BF16),
            shape((block, rank), BF16),
            shape((block, rank), BF16),
            shape((block, obs), BF16),
            shape((block, rank), BF16),
            shape((1, 1), F32),
        ),
        out_specs=(
            *(pl.BlockSpec(memory_space=pltpu.VMEM) for _ in range(6)),
            pl.BlockSpec(memory_space=pltpu.SMEM),
        ),
        scratch_shapes=[pltpu.VMEM((block, LANES), F32)],
        compiler_params=pltpu.CompilerParams(vmem_limit_bytes=16 * 1024 * 1024),
        name="finish",
    )(one, two, far)
    return (fs.T, fa, fl.T, fo, bs.T, bo, loss.reshape(()))


def forward_pass(
    current, later, moves, latent_rows, f_state, f_action, f_latent, f_output, b_state, b_output
):
    f_pre = (
        jnp.dot(current, f_state, preferred_element_type=F32)
        + jnp.dot(moves, f_action, preferred_element_type=F32)
        + jnp.dot(latent_rows, f_latent, preferred_element_type=F32)
    )
    f_hidden = jnp.maximum(f_pre, 0.0).astype(BF16)
    forward_emb = jnp.dot(f_hidden, f_output, preferred_element_type=F32).astype(BF16)
    b_pre = jnp.dot(later, b_state, preferred_element_type=F32)
    b_hidden = jnp.maximum(b_pre, 0.0).astype(BF16)
    b_raw = jnp.dot(b_hidden, b_output, preferred_element_type=F32)
    b_scale = lax.rsqrt(jnp.mean(b_raw * b_raw, axis=-1, keepdims=True) + EPSILON)
    backward_emb = (b_raw * b_scale).astype(BF16)
    return (f_pre, f_hidden, forward_emb, b_pre, b_hidden, b_raw, b_scale, backward_emb)


def general_local(
    states,
    actions,
    target_forward,
    next_index,
    latent_ids,
    latents,
    f_state,
    f_action,
    f_latent,
    f_output,
    b_state,
    b_output,
):
    current = states[0]
    moves = actions[0]
    later = jnp.take(current, next_index[0], axis=0)
    latent_rows = jnp.take(latents, latent_ids[0], axis=0)
    f_pre, f_hidden, forward_emb, b_pre, b_hidden, b_raw, b_scale, backward_emb = forward_pass(
        current, later, moves, latent_rows, f_state, f_action, f_latent, f_output, b_state, b_output
    )
    group = current.shape[0] * lax.axis_size("dp")
    total = group * lax.axis_size("replica")
    factor = 1.0 / math.sqrt(total)
    forward32 = forward_emb.astype(F32)
    back32 = backward_emb.astype(F32)
    error = forward32 - GAMMA * target_forward[0].astype(F32)
    gram, cross = lax.psum(
        (
            jnp.dot(backward_emb.T, backward_emb, preferred_element_type=F32),
            jnp.dot(forward32.T, error, precision=HIGH, preferred_element_type=F32),
        ),
        "dp",
    )
    pulled = jnp.dot(error, gram, precision=HIGH, preferred_element_type=F32)
    pushed = jnp.dot(back32, cross.T, precision=HIGH, preferred_element_type=F32)
    partial_loss = 0.5 / group * jnp.sum(pulled * error) - jnp.sum(forward32 * back32)
    grad_forward = (factor * (pulled / group - back32)).astype(BF16)
    grad_backward = factor * (pushed / group - forward32)
    inner = jnp.mean(b_raw * grad_backward, axis=-1, keepdims=True)
    grad_raw = (b_scale * grad_backward - b_raw * b_scale * b_scale * b_scale * inner).astype(BF16)
    part_bo = jnp.dot(b_hidden.T, grad_raw, preferred_element_type=F32)
    b_back = jnp.dot(grad_raw, b_output.T, preferred_element_type=F32)
    b_delta = jnp.where(b_pre > 0, b_back, 0.0).astype(BF16)
    part_bs = jnp.dot(later.T, b_delta, preferred_element_type=F32)
    part_fo = jnp.dot(f_hidden.T, grad_forward, preferred_element_type=F32)
    f_back = jnp.dot(grad_forward, f_output.T, preferred_element_type=F32)
    f_delta = jnp.where(f_pre > 0, f_back, 0.0).astype(BF16)
    part_fs = jnp.dot(current.T, f_delta, preferred_element_type=F32)
    part_fa = jnp.dot(moves.T, f_delta, preferred_element_type=F32)
    part_fl = jnp.dot(latent_rows.T, f_delta, preferred_element_type=F32)
    places = (1, 1, 1, 0, 1, 0)
    parts = (part_fs, part_fa, part_fl, part_fo, part_bs, part_bo)
    shares = tuple(
        lax.psum_scatter(part, "dp", scatter_dimension=place, tiled=True)
        for part, place in zip(parts, places)
    )
    summed = lax.psum(shares, "replica")
    loss_sum = lax.psum(partial_loss, ("dp", "replica"))
    return (*(item.astype(BF16) for item in summed), loss_sum / total)


def local(*args):
    size, replicas = lax.axis_size("dp"), lax.axis_size("replica")
    rows, hidden = args[0].shape[1], args[6].shape[1]
    fits = size == 8 and replicas == 4 and rows * size <= KERNEL_GROUP_LIMIT
    block = hidden // size
    whole = rows % ROW_TILE == 0 and hidden % (size * 64) == 0 and hidden % 512 == 0
    whole = whole and LANES < block <= 2 * LANES - 64 and args[6].shape[0] % 8 == 0
    exact = rows <= 256 and args[5].shape[0] <= 256
    return (fast_local if fits and whole and exact else general_local)(*args)


def solution(mesh):
    in_specs = (
        P("replica", "dp", None),
        P("replica", "dp", None),
        P("replica", "dp", None),
        P("replica", "dp"),
        P("replica", "dp"),
        P(),
        P(),
        P(),
        P(),
        P(),
        P(),
        P(),
    )
    out_specs = (
        P(None, "dp"),
        P(None, "dp"),
        P(None, "dp"),
        P("dp", None),
        P(None, "dp"),
        P("dp", None),
        P(),
    )
    return jax.shard_map(local, mesh=mesh, in_specs=in_specs, out_specs=out_specs, check_vma=False)
```

```python
import functools
import math

import jax
import jax.numpy as jnp
from jax import lax
from jax.experimental import pallas as pl
from jax.experimental.pallas import tpu as pltpu
from jax.sharding import PartitionSpec as P

GAMMA = 0.98
EPSILON = 1e-06
HIGH = lax.Precision.HIGHEST
BF16 = jnp.bfloat16
F32 = jnp.float32
LANES = 128
ROW_TILE = 16
KERNEL_GROUP_LIMIT = 2048


def round_up(value, unit):
    return -(-value // unit) * unit


def dot_nn(left, right):
    return lax.dot_general(left, right, (((1,), (0,)), ((), ())), preferred_element_type=F32)


def dot_nt(left, right):
    return lax.dot_general(left, right, (((1,), (1,)), ((), ())), preferred_element_type=F32)


def dot_tn(left, right):
    return lax.dot_general(left, right, (((0,), (0,)), ((), ())), preferred_element_type=F32)


def join(values, axis):
    return jnp.concatenate(values, axis=axis) if len(values) > 1 else values[0]


def stack(refs, axis):
    return join([ref[...] for ref in refs], axis)


def split_two(value):
    high = value.astype(BF16)
    return high, (value - high.astype(F32)).astype(BF16)


def pack_kernel(cfg, state_ref, move_ref, next_ref, latent_ref, target_ref, out_ref, side_ref):
    rows, obs, act, obs_pad, side = (cfg[k] for k in ("rows", "obs", "act", "obs_pad", "side"))
    lane = side_ref.shape[1]
    side_ref[...] = jnp.zeros_like(side_ref)
    side_ref[0:act, 0:rows] = move_ref[...].astype(F32)
    side_ref[act : act + 1, 0:rows] = next_ref[...].astype(F32)
    side_ref[act + 1 : act + 2, 0:rows] = latent_ref[...].astype(F32)
    gap = jnp.zeros((rows, obs_pad - obs), BF16)
    out_ref[0:rows, 0:obs_pad] = jnp.concatenate([state_ref[0], gap], axis=1)
    out_ref[0:rows, obs_pad:] = target_ref[0]
    half = side // 2
    out_ref[rows:, :] = jnp.zeros((half, out_ref.shape[1]), BF16)
    out_ref[rows:, 0:lane] = side_ref[0:half, :].astype(BF16)
    out_ref[rows:, lane : 2 * lane] = side_ref[half:side, :].astype(BF16)


def weights_kernel(cfg, fs_hbm, fa_hbm, fl_hbm, bs_hbm, *refs):
    obs, obs_pad, x_pad = cfg["obs"], cfg["obs_pad"], cfg["x_pad"]
    hidden, block, act = cfg["hidden"], cfg["block"], cfg["act"]
    wf_ref, wb_ref, wfb_ref, wbb_ref, fs_ref, fa_ref, fl_ref, bs_ref, sems = refs
    pairs = ((fs_hbm, fs_ref), (bs_hbm, bs_ref), (fl_hbm, fl_ref), (fa_hbm, fa_ref))
    copies = [pltpu.make_async_copy(a, b, sems.at[i]) for i, (a, b) in enumerate(pairs)]
    for copy in copies:
        copy.start()
    gap = jnp.zeros((obs_pad - obs, hidden), BF16)
    wf_ref[obs_pad:x_pad, :] = jnp.zeros((x_pad - obs_pad, hidden), BF16)
    copies[0].wait()
    wf_ref[0:obs_pad, :] = jnp.concatenate([fs_ref[...], gap], axis=0)
    copies[1].wait()
    wb_ref[...] = jnp.concatenate([bs_ref[...], gap], axis=0)
    copies[2].wait()
    wf_ref[x_pad:, :] = fl_ref[...]
    copies[3].wait()
    wf_ref[obs_pad : obs_pad + act, :] = fa_ref[...]
    me = lax.axis_index("dp")
    start = me * block
    base = pl.multiple_of(start // LANES * LANES, LANES)
    odd = lax.rem(me, 2) == 1
    span = pl.ds(base, 2 * LANES)

    def pick(ref):
        near = ref[:, span].astype(F32).T
        return jnp.where(odd, near[2 * LANES - block :], near[:block]).astype(BF16)

    wfb_ref[...] = pick(wf_ref)
    wbb_ref[...] = pick(wb_ref)


def forward_rows(cfg, xs, weights, outs):
    wf_ref, wb_ref, fo_ref, bo_ref, lat_ref, wfb_ref, wbb_ref = weights
    a_ref, later_ref, f_ref, u_ref, fh_ref, bh_ref = outs
    rows, act, rank, side = cfg["rows"], cfg["act"], cfg["rank"], cfg["side"]
    obs_pad, x_pad, hidden, zcount = cfg["obs_pad"], cfg["x_pad"], cfg["hidden"], cfg["zcount"]
    tile, lane = cfg["tile"], cfg["lane"]
    half = side // 2
    row_spots = lax.broadcasted_iota(jnp.int32, (rows, rows), 1).astype(F32)
    spots = lax.broadcasted_iota(jnp.int32, (rows, zcount), 1).astype(F32)
    blank = jnp.zeros((rows, x_pad - obs_pad - side), BF16)
    for j, x_ref in enumerate(xs):
        here = slice(j * rows, (j + 1) * rows)
        few = jnp.concatenate(
            [x_ref[rows:, 0:lane].astype(F32), x_ref[rows:, lane : 2 * lane].astype(F32)], axis=0
        ).T[:rows]
        near = x_ref[0:rows, 0:obs_pad]
        picks = jnp.where(few[:, act + 1 : act + 2] == spots, 1.0, 0.0).astype(BF16)
        hot = jnp.where(few[:, act : act + 1] == row_spots, 1.0, 0.0).astype(BF16)
        a_ref[here, 0:obs_pad] = near
        a_ref[here, obs_pad:x_pad] = jnp.concatenate([few.astype(BF16), blank], axis=1)
        a_ref[here, x_pad:] = dot_nn(picks, lat_ref[...]).astype(BF16)
        later_ref[here, :] = dot_nn(hot, near).astype(BF16)
    whole = a_ref[...]
    later = later_ref[...]
    tiles = [slice(n, n + tile) for n in range(0, hidden, tile)]
    hs = [jnp.maximum(dot_nn(whole, wf_ref[:, part]), 0.0).astype(BF16) for part in tiles]
    emb = dot_nn(join(hs, 1), fo_ref[...]).astype(BF16)
    gs = [jnp.maximum(dot_nn(later, wb_ref[:, part]), 0.0).astype(BF16) for part in tiles]
    u = dot_nn(join(gs, 1), bo_ref[...])
    back = (u * lax.rsqrt(jnp.mean(u * u, axis=-1, keepdims=True) + EPSILON)).astype(BF16)
    f_ref[...] = emb
    u_ref[...] = u
    fh_ref[...] = jnp.maximum(dot_nt(wfb_ref[...], whole), 0.0).astype(BF16)
    bh_ref[...] = jnp.maximum(dot_nt(wbb_ref[...], later), 0.0).astype(BF16)
    cross = dot_tn(emb, emb)
    for j, x_ref in enumerate(xs):
        cross = cross - GAMMA * dot_tn(x_ref[0:rows, obs_pad:], emb[j * rows : (j + 1) * rows])
    return dot_tn(back, back), cross


def forward_kernel(cfg, count, first, *refs):
    xs, refs = refs[:count], refs[count:]
    weights, refs = refs[:7], refs[7:]
    if not first:
        gram_in, refs = refs[0], refs[1:]
    outs, gram_out = refs[:6], refs[6]
    gram, cross = forward_rows(cfg, xs, weights, outs)
    rank = cfg["rank"]
    gram_out[:, :rank] = gram if first else gram_in[:, :rank] + gram
    gram_out[:, rank:] = cross if first else gram_in[:, rank:] + cross


def last_kernel(cfg, early, count, *refs):
    groups = []
    for size in early:
        groups.append((refs[:size], refs[size : size + 6]))
        refs = refs[size + 6 :]
    xs, refs = refs[:count], refs[count:]
    weights, refs = refs[:7], refs[7:]
    gram_in, send_ref, keep_ref = refs[:3]
    outs, part_ref = refs[3:9], refs[9]
    rank, block, rows, obs_pad = cfg["rank"], cfg["block"], cfg["rows"], cfg["obs_pad"]
    group, replicas = cfg["group"], cfg["replicas"]
    factor = 1.0 / math.sqrt(cfg["total"])
    c1, c2, c3 = cfg["cols"]
    gram, cross = forward_rows(cfg, xs, weights, outs)
    gram_hi, gram_lo = split_two(gram_in[:, :rank] + gram)
    cross_hi, cross_lo = split_two(gram_in[:, rank:] + cross)
    groups.append((xs, outs))
    me = pl.multiple_of(lax.axis_index("dp") * block, ROW_TILE)
    fo = weights[2][pl.ds(me, block), :]
    bo = weights[3][pl.ds(me, block), :]
    few = [item for item in groups if len(item[0]) == 1]
    many = [item for item in groups if len(item[0]) > 1]
    square = jnp.zeros((1, rank), F32)
    diagonal = jnp.zeros((1, rank), F32)
    f_deltas, b_deltas, f_hids, b_hids, d_fs, d_us, wholes, laters = ([] for _ in range(8))
    for members in (few, many):
        if not members:
            continue
        saved = list(zip(*(item[1] for item in members)))
        emb32 = stack(saved[2], 0).astype(F32)
        target = join([x_ref[0:rows, obs_pad:] for item in members for x_ref in item[0]], 0)
        error = emb32 - GAMMA * target.astype(F32)
        err_hi, err_lo = split_two(error)
        u = stack(saved[3], 0)
        scale = lax.rsqrt(jnp.mean(u * u, axis=-1, keepdims=True) + EPSILON)
        back = (u * scale).astype(BF16)
        back32 = back.astype(F32)
        pulled = dot_nn(err_hi, gram_hi) + (dot_nn(err_hi, gram_lo) + dot_nn(err_lo, gram_hi))
        square = square + jnp.sum(pulled * error, axis=0, keepdims=True)
        diagonal = diagonal + jnp.sum(emb32 * back32, axis=0, keepdims=True)
        d_f = (factor * (pulled / group - back32)).astype(BF16)
        pushed = dot_nn(back, cross_hi) + dot_nn(back, cross_lo)
        d_b = factor * (pushed / group - emb32)
        inner = jnp.mean(u * d_b, axis=-1, keepdims=True)
        d_u = (scale * d_b - u * (scale * scale * scale * inner)).astype(BF16)
        f_hid, b_hid = stack(saved[4], 1), stack(saved[5], 1)
        zero = jnp.zeros_like(f_hid)
        f_deltas.append(jnp.where(f_hid > 0, dot_nt(fo, d_f).astype(BF16), zero))
        b_deltas.append(jnp.where(b_hid > 0, dot_nt(bo, d_u).astype(BF16), zero))
        f_hids.append(f_hid)
        b_hids.append(b_hid)
        d_fs.append(d_f)
        d_us.append(d_u)
        wholes += saved[0]
        laters += saved[1]
    part_ref[:, :c1] = dot_nn(join(f_deltas, 1), stack(wholes, 0))
    part_ref[:, c1:c2] = dot_nn(join(f_hids, 1), join(d_fs, 0))
    part_ref[:, c2:c3] = dot_nn(join(b_deltas, 1), stack(laters, 0))
    part_ref[:, c3:] = dot_nn(join(b_hids, 1), join(d_us, 0))
    loss = (0.5 / group) * jnp.sum(square) - jnp.sum(diagonal)
    lanes = lax.broadcasted_iota(jnp.int32, (block, LANES), 1)
    spot = cfg["loss_spot"]
    base = spot // LANES * LANES
    first = spot - base + 3 * lax.axis_index("replica")
    rest = jnp.full((block, LANES), loss, F32)
    piece_tile = part_ref[:, base : base + LANES]
    piece_tile = jnp.where(lanes >= spot - base, 0.0, piece_tile)
    for j in range(3):
        piece = rest.astype(BF16).astype(F32)
        piece_tile = jnp.where(lanes == first + j, piece, piece_tile)
        rest = rest - piece
    part_ref[:, base : base + LANES] = piece_tile
    core = lax.rem(lax.axis_index("replica"), 2)
    half = block // 2
    keep_ref[...] = part_ref[pl.ds(pl.multiple_of(core * half, ROW_TILE), half), :]
    other = pl.multiple_of((1 - core) * half, ROW_TILE)
    send_ref[...] = part_ref[pl.ds(other, half), :].astype(BF16)


def finish_kernel(cfg, one_ref, two_ref, far_ref, fs, fa, fl, fo, bs, bo, loss_ref, act_ref):
    obs, act, rank, x_pad, obs_pad = (cfg[k] for k in ("obs", "act", "rank", "x_pad", "obs_pad"))
    half = cfg["block"] // 2
    c1, c2, c3 = cfg["cols"]
    core = lax.rem(lax.axis_index("replica"), 2)
    mine32 = one_ref[...].astype(F32) + two_ref[...].astype(F32)
    mine = mine32.astype(BF16)
    far = far_ref[...]
    for start, value in ((core * half, mine), ((1 - core) * half, far)):
        here = pl.ds(pl.multiple_of(start, ROW_TILE), half)
        fs[here, :] = value[:, :obs]
        fl[here, :] = value[:, x_pad:c1]
        fo[here, :] = value[:, c1:c2]
        bs[here, :] = value[:, c2 : c2 + obs]
        bo[here, :] = value[:, c3:]
        act_ref[here, :] = value[:, obs_pad : obs_pad + LANES].astype(F32)
    fa[...] = act_ref[...].T[:act].astype(BF16)
    spot = cfg["loss_spot"]
    base = spot // LANES * LANES
    pieces = mine32[0:8, base : base + LANES]
    lanes = lax.broadcasted_iota(jnp.int32, (8, LANES), 1)
    rows = lax.broadcasted_iota(jnp.int32, (8, LANES), 0)
    ours = (lanes >= spot - base) & (lanes < spot - base + 3 * cfg["replicas"]) & (rows == 0)
    loss_ref[0, 0] = jnp.sum(jnp.where(ours, pieces, 0.0)) / cfg["total"]


def exchange(array, axis, size, bit):
    return lax.ppermute(array, axis, [(i, i ^ bit) for i in range(size)])


def in_hbm(*arrays):
    return [pltpu.with_memory_space_constraint(array, pltpu.HBM) for array in arrays]


def shape(dims, kind):
    return jax.ShapeDtypeStruct(dims, kind)


def fast_local(
    states,
    actions,
    target_forward,
    next_index,
    latent_ids,
    latents,
    f_state,
    f_action,
    f_latent,
    f_output,
    b_state,
    b_output,
):
    size = lax.axis_size("dp")
    replicas = lax.axis_size("replica")
    rows, obs = states.shape[1:]
    act = actions.shape[2]
    zcount, rank = latents.shape
    hidden = f_state.shape[1]
    block = hidden // size
    group = rows * size
    side = round_up(act + 2, 2 * ROW_TILE)
    lane = round_up(rows, LANES)
    obs_pad = round_up(obs, LANES)
    x_pad = obs_pad + LANES
    c1 = x_pad + rank
    c2 = c1 + rank
    c3 = c2 + obs_pad
    width = c3 + rank
    cfg = dict(
        rows=rows,
        obs=obs,
        act=act,
        rank=rank,
        obs_pad=obs_pad,
        x_pad=x_pad,
        hidden=hidden,
        zcount=zcount,
        side=side,
        lane=lane,
        group=group,
        replicas=replicas,
        total=group * replicas,
        block=block,
        tile=256,
        cols=(c1, c2, c3),
        loss_spot=obs_pad + side,
    )
    params = pltpu.CompilerParams(vmem_limit_bytes=20 * 1024 * 1024)
    last_params = pltpu.CompilerParams(vmem_limit_bytes=28 * 1024 * 1024)
    own = pl.pallas_call(
        functools.partial(pack_kernel, cfg),
        out_shape=shape((rows + side // 2, obs_pad + rank), BF16),
        scratch_shapes=[pltpu.VMEM((side, lane), F32)],
        compiler_params=pltpu.CompilerParams(vmem_limit_bytes=8 * 1024 * 1024),
        name="pack",
    )(*in_hbm(states, actions[0].T, next_index, latent_ids, target_forward))
    x = {"own": own}
    middle = [(2 + i, 4 + i) for i in range(2)] + [(4 + i, 2 + i) for i in range(2)]
    outward = [(2 + i, i) for i in range(2)] + [(4 + i, 6 + i) for i in range(2)]
    across = lax.ppermute(own, "dp", middle)
    x["x own"] = exchange(own, "dp", size, 1)
    x["half"] = exchange(own, "dp", size, 2)
    handed = lax.ppermute(across, "dp", outward)
    x["x half"] = exchange(x["half"], "dp", size, 1)
    across_two = lax.ppermute(x["half"], "dp", middle)
    x["second"] = across + handed
    x["x second"] = exchange(x["second"], "dp", size, 1)
    handed_two = lax.ppermute(across_two, "dp", outward)
    x["third"] = across_two + handed_two
    x["x third"] = exchange(x["third"], "dp", size, 1)
    wf, wb, wfb, wbb = pl.pallas_call(
        functools.partial(weights_kernel, cfg),
        out_shape=(
            shape((x_pad + rank, hidden), BF16),
            shape((obs_pad, hidden), BF16),
            shape((block, x_pad + rank), BF16),
            shape((block, obs_pad), BF16),
        ),
        in_specs=[pl.BlockSpec(memory_space=pl.ANY)] * 4,
        scratch_shapes=[
            pltpu.VMEM((obs, hidden), BF16),
            pltpu.VMEM((act, hidden), BF16),
            pltpu.VMEM((rank, hidden), BF16),
            pltpu.VMEM((obs, hidden), BF16),
            pltpu.SemaphoreType.DMA((4,)),
        ],
        compiler_params=pltpu.CompilerParams(vmem_limit_bytes=16 * 1024 * 1024),
        cost_estimate=pl.CostEstimate(flops=0, bytes_accessed=1_000_000, transcendentals=0),
        name="weights",
    )(*in_hbm(f_state, f_action, f_latent, b_state))
    weights = (wf, wb, f_output, b_output, latents, wfb, wbb)
    row_flops = 2 * (c1 + 2 * rank + obs_pad) * hidden + 8 * rank * rank

    def kept(count):
        m = rows * count
        return (
            ((m, x_pad + rank), BF16),
            ((m, obs_pad), BF16),
            ((m, rank), BF16),
            ((m, rank), F32),
            ((block, m), BF16),
            ((block, m), BF16),
        )

    grams = ()
    plan = (
        (("own",), 3.0),
        (("half",), 2.0),
        (("x own",), 1.5),
        (("x half", "second"), 1.0),
        (("third", "x second"), 3.0),
    )
    early = []
    for steps, work in plan:
        count = len(steps)
        xs = [x[step] for step in steps]
        *saved, total_grams = pl.pallas_call(
            functools.partial(forward_kernel, cfg, count, not early),
            out_shape=(*(shape(*item) for item in kept(count)), shape((rank, 2 * rank), F32)),
            compiler_params=params,
            cost_estimate=pl.CostEstimate(
                flops=int(work * rows * count * row_flops),
                bytes_accessed=1_000_000,
                transcendentals=0,
            ),
            name="forward",
        )(*xs, *weights, *grams)
        grams = (total_grams,)
        early.append((xs, saved))
    left = [x["x third"]]
    operands = []
    for xs, saved in early:
        operands += [*xs, *saved]
    send, keep = pl.pallas_call(
        functools.partial(last_kernel, cfg, [len(xs) for xs, _ in early], len(left)),
        out_shape=(shape((block // 2, width), BF16), shape((block // 2, width), F32)),
        scratch_shapes=[
            *(pltpu.VMEM(*item) for item in kept(len(left))),
            pltpu.VMEM((block, width), F32),
        ],
        compiler_params=last_params,
        cost_estimate=pl.CostEstimate(
            flops=4 * group * width * block, bytes_accessed=16_000_000, transcendentals=0
        ),
        name="last",
    )(*operands, *left, *weights, *grams)
    got = exchange(send, "replica", replicas, 1)
    one = (keep + got.astype(F32)).astype(BF16)
    two = exchange(one, "replica", replicas, 2)
    mine = (one.astype(F32) + two.astype(F32)).astype(BF16)
    far = exchange(mine, "replica", replicas, 1)
    fs, fa, fl, fo, bs, bo, loss = pl.pallas_call(
        functools.partial(finish_kernel, cfg),
        out_shape=(
            shape((block, obs), BF16),
            shape((act, block), BF16),
            shape((block, rank), BF16),
            shape((block, rank), BF16),
            shape((block, obs), BF16),
            shape((block, rank), BF16),
            shape((1, 1), F32),
        ),
        out_specs=(
            *(pl.BlockSpec(memory_space=pltpu.VMEM) for _ in range(6)),
            pl.BlockSpec(memory_space=pltpu.SMEM),
        ),
        scratch_shapes=[pltpu.VMEM((block, LANES), F32)],
        compiler_params=pltpu.CompilerParams(vmem_limit_bytes=16 * 1024 * 1024),
        name="finish",
    )(one, two, far)
    return (fs.T, fa, fl.T, fo, bs.T, bo, loss.reshape(()))


def forward_pass(
    current, later, moves, latent_rows, f_state, f_action, f_latent, f_output, b_state, b_output
):
    f_pre = (
        jnp.dot(current, f_state, preferred_element_type=F32)
        + jnp.dot(moves, f_action, preferred_element_type=F32)
        + jnp.dot(latent_rows, f_latent, preferred_element_type=F32)
    )
    f_hidden = jnp.maximum(f_pre, 0.0).astype(BF16)
    forward_emb = jnp.dot(f_hidden, f_output, preferred_element_type=F32).astype(BF16)
    b_pre = jnp.dot(later, b_state, preferred_element_type=F32)
    b_hidden = jnp.maximum(b_pre, 0.0).astype(BF16)
    b_raw = jnp.dot(b_hidden, b_output, preferred_element_type=F32)
    b_scale = lax.rsqrt(jnp.mean(b_raw * b_raw, axis=-1, keepdims=True) + EPSILON)
    backward_emb = (b_raw * b_scale).astype(BF16)
    return (f_pre, f_hidden, forward_emb, b_pre, b_hidden, b_raw, b_scale, backward_emb)


def general_local(
    states,
    actions,
    target_forward,
    next_index,
    latent_ids,
    latents,
    f_state,
    f_action,
    f_latent,
    f_output,
    b_state,
    b_output,
):
    current = states[0]
    moves = actions[0]
    later = jnp.take(current, next_index[0], axis=0)
    latent_rows = jnp.take(latents, latent_ids[0], axis=0)
    f_pre, f_hidden, forward_emb, b_pre, b_hidden, b_raw, b_scale, backward_emb = forward_pass(
        current, later, moves, latent_rows, f_state, f_action, f_latent, f_output, b_state, b_output
    )
    group = current.shape[0] * lax.axis_size("dp")
    total = group * lax.axis_size("replica")
    factor = 1.0 / math.sqrt(total)
    forward32 = forward_emb.astype(F32)
    back32 = backward_emb.astype(F32)
    error = forward32 - GAMMA * target_forward[0].astype(F32)
    gram, cross = lax.psum(
        (
            jnp.dot(backward_emb.T, backward_emb, preferred_element_type=F32),
            jnp.dot(forward32.T, error, precision=HIGH, preferred_element_type=F32),
        ),
        "dp",
    )
    pulled = jnp.dot(error, gram, precision=HIGH, preferred_element_type=F32)
    pushed = jnp.dot(back32, cross.T, precision=HIGH, preferred_element_type=F32)
    partial_loss = 0.5 / group * jnp.sum(pulled * error) - jnp.sum(forward32 * back32)
    grad_forward = (factor * (pulled / group - back32)).astype(BF16)
    grad_backward = factor * (pushed / group - forward32)
    inner = jnp.mean(b_raw * grad_backward, axis=-1, keepdims=True)
    grad_raw = (b_scale * grad_backward - b_raw * b_scale * b_scale * b_scale * inner).astype(BF16)
    part_bo = jnp.dot(b_hidden.T, grad_raw, preferred_element_type=F32)
    b_back = jnp.dot(grad_raw, b_output.T, preferred_element_type=F32)
    b_delta = jnp.where(b_pre > 0, b_back, 0.0).astype(BF16)
    part_bs = jnp.dot(later.T, b_delta, preferred_element_type=F32)
    part_fo = jnp.dot(f_hidden.T, grad_forward, preferred_element_type=F32)
    f_back = jnp.dot(grad_forward, f_output.T, preferred_element_type=F32)
    f_delta = jnp.where(f_pre > 0, f_back, 0.0).astype(BF16)
    part_fs = jnp.dot(current.T, f_delta, preferred_element_type=F32)
    part_fa = jnp.dot(moves.T, f_delta, preferred_element_type=F32)
    part_fl = jnp.dot(latent_rows.T, f_delta, preferred_element_type=F32)
    places = (1, 1, 1, 0, 1, 0)
    parts = (part_fs, part_fa, part_fl, part_fo, part_bs, part_bo)
    shares = tuple(
        lax.psum_scatter(part, "dp", scatter_dimension=place, tiled=True)
        for part, place in zip(parts, places)
    )
    summed = lax.psum(shares, "replica")
    loss_sum = lax.psum(partial_loss, ("dp", "replica"))
    return (*(item.astype(BF16) for item in summed), loss_sum / total)


def local(*args):
    size, replicas = lax.axis_size("dp"), lax.axis_size("replica")
    rows, hidden = args[0].shape[1], args[6].shape[1]
    fits = size == 8 and replicas == 4 and rows * size <= KERNEL_GROUP_LIMIT
    block = hidden // size
    whole = rows % ROW_TILE == 0 and hidden % (size * 64) == 0 and hidden % 512 == 0
    whole = whole and LANES < block <= 2 * LANES - 64 and args[6].shape[0] % 8 == 0
    exact = rows <= 256 and args[5].shape[0] <= 256
    return (fast_local if fits and whole and exact else general_local)(*args)


def solution(mesh):
    in_specs = (
        P("replica", "dp", None),
        P("replica", "dp", None),
        P("replica", "dp", None),
        P("replica", "dp"),
        P("replica", "dp"),
        P(),
        P(),
        P(),
        P(),
        P(),
        P(),
        P(),
    )
    out_specs = (
        P(None, "dp"),
        P(None, "dp"),
        P(None, "dp"),
        P("dp", None),
        P(None, "dp"),
        P("dp", None),
        P(),
    )
    return jax.shard_map(local, mesh=mesh, in_specs=in_specs, out_specs=out_specs, check_vma=False)
```

```python
import functools
import math

import jax
import jax.numpy as jnp
from jax import lax
from jax.experimental import pallas as pl
from jax.experimental.pallas import tpu as pltpu
from jax.sharding import PartitionSpec as P

GAMMA = 0.98
EPSILON = 1e-06
HIGH = lax.Precision.HIGHEST
BF16 = jnp.bfloat16
F32 = jnp.float32
LANES = 128
ROW_TILE = 16
KERNEL_GROUP_LIMIT = 2048


def round_up(value, unit):
    return -(-value // unit) * unit


def dot_nn(left, right):
    return lax.dot_general(left, right, (((1,), (0,)), ((), ())), preferred_element_type=F32)


def dot_nt(left, right):
    return lax.dot_general(left, right, (((1,), (1,)), ((), ())), preferred_element_type=F32)


def dot_tn(left, right):
    return lax.dot_general(left, right, (((0,), (0,)), ((), ())), preferred_element_type=F32)


def join(values, axis):
    return jnp.concatenate(values, axis=axis) if len(values) > 1 else values[0]


def stack(refs, axis):
    return join([ref[...] for ref in refs], axis)


def split_two(value):
    high = value.astype(BF16)
    return high, (value - high.astype(F32)).astype(BF16)


def pack_kernel(cfg, state_ref, move_ref, next_ref, latent_ref, target_ref, out_ref, side_ref):
    rows, obs, act, obs_pad, side = (cfg[k] for k in ("rows", "obs", "act", "obs_pad", "side"))
    lane = side_ref.shape[1]
    side_ref[...] = jnp.zeros_like(side_ref)
    side_ref[0:act, 0:rows] = move_ref[...].astype(F32)
    side_ref[act : act + 1, 0:rows] = next_ref[...].astype(F32)
    side_ref[act + 1 : act + 2, 0:rows] = latent_ref[...].astype(F32)
    gap = jnp.zeros((rows, obs_pad - obs), BF16)
    out_ref[0:rows, 0:obs_pad] = jnp.concatenate([state_ref[0], gap], axis=1)
    out_ref[0:rows, obs_pad:] = target_ref[0]
    half = side // 2
    out_ref[rows:, :] = jnp.zeros((half, out_ref.shape[1]), BF16)
    out_ref[rows:, 0:lane] = side_ref[0:half, :].astype(BF16)
    out_ref[rows:, lane : 2 * lane] = side_ref[half:side, :].astype(BF16)


def weights_kernel(cfg, fs_hbm, fa_hbm, fl_hbm, bs_hbm, *refs):
    obs, obs_pad, x_pad = cfg["obs"], cfg["obs_pad"], cfg["x_pad"]
    hidden, block, act = cfg["hidden"], cfg["block"], cfg["act"]
    wf_ref, wb_ref, wfb_ref, wbb_ref, fs_ref, fa_ref, fl_ref, bs_ref, sems = refs
    pairs = ((fs_hbm, fs_ref), (bs_hbm, bs_ref), (fl_hbm, fl_ref), (fa_hbm, fa_ref))
    copies = [pltpu.make_async_copy(a, b, sems.at[i]) for i, (a, b) in enumerate(pairs)]
    for copy in copies:
        copy.start()
    gap = jnp.zeros((obs_pad - obs, hidden), BF16)
    wf_ref[obs_pad:x_pad, :] = jnp.zeros((x_pad - obs_pad, hidden), BF16)
    copies[0].wait()
    wf_ref[0:obs_pad, :] = jnp.concatenate([fs_ref[...], gap], axis=0)
    copies[1].wait()
    wb_ref[...] = jnp.concatenate([bs_ref[...], gap], axis=0)
    copies[2].wait()
    wf_ref[x_pad:, :] = fl_ref[...]
    copies[3].wait()
    wf_ref[obs_pad : obs_pad + act, :] = fa_ref[...]
    me = lax.axis_index("dp")
    start = me * block
    base = pl.multiple_of(start // LANES * LANES, LANES)
    odd = lax.rem(me, 2) == 1
    span = pl.ds(base, 2 * LANES)

    def pick(ref):
        near = ref[:, span].astype(F32).T
        return jnp.where(odd, near[2 * LANES - block :], near[:block]).astype(BF16)

    wfb_ref[...] = pick(wf_ref)
    wbb_ref[...] = pick(wb_ref)


def forward_rows(cfg, xs, weights, outs):
    wf_ref, wb_ref, fo_ref, bo_ref, lat_ref, wfb_ref, wbb_ref = weights
    a_ref, later_ref, f_ref, u_ref, fh_ref, bh_ref = outs
    rows, act, rank, side = cfg["rows"], cfg["act"], cfg["rank"], cfg["side"]
    obs_pad, x_pad, hidden, zcount = cfg["obs_pad"], cfg["x_pad"], cfg["hidden"], cfg["zcount"]
    tile, lane = cfg["tile"], cfg["lane"]
    half = side // 2
    row_spots = lax.broadcasted_iota(jnp.int32, (rows, rows), 1).astype(F32)
    spots = lax.broadcasted_iota(jnp.int32, (rows, zcount), 1).astype(F32)
    blank = jnp.zeros((rows, x_pad - obs_pad - side), BF16)
    for j, x_ref in enumerate(xs):
        here = slice(j * rows, (j + 1) * rows)
        few = jnp.concatenate(
            [x_ref[rows:, 0:lane].astype(F32), x_ref[rows:, lane : 2 * lane].astype(F32)], axis=0
        ).T[:rows]
        near = x_ref[0:rows, 0:obs_pad]
        picks = jnp.where(few[:, act + 1 : act + 2] == spots, 1.0, 0.0).astype(BF16)
        hot = jnp.where(few[:, act : act + 1] == row_spots, 1.0, 0.0).astype(BF16)
        a_ref[here, 0:obs_pad] = near
        a_ref[here, obs_pad:x_pad] = jnp.concatenate([few.astype(BF16), blank], axis=1)
        a_ref[here, x_pad:] = dot_nn(picks, lat_ref[...]).astype(BF16)
        later_ref[here, :] = dot_nn(hot, near).astype(BF16)
    whole = a_ref[...]
    later = later_ref[...]
    tiles = [slice(n, n + tile) for n in range(0, hidden, tile)]
    hs = [jnp.maximum(dot_nn(whole, wf_ref[:, part]), 0.0).astype(BF16) for part in tiles]
    emb = dot_nn(join(hs, 1), fo_ref[...]).astype(BF16)
    gs = [jnp.maximum(dot_nn(later, wb_ref[:, part]), 0.0).astype(BF16) for part in tiles]
    u = dot_nn(join(gs, 1), bo_ref[...])
    back = (u * lax.rsqrt(jnp.mean(u * u, axis=-1, keepdims=True) + EPSILON)).astype(BF16)
    f_ref[...] = emb
    u_ref[...] = u
    fh_ref[...] = jnp.maximum(dot_nt(wfb_ref[...], whole), 0.0).astype(BF16)
    bh_ref[...] = jnp.maximum(dot_nt(wbb_ref[...], later), 0.0).astype(BF16)
    target = join([x_ref[0:rows, obs_pad:] for x_ref in xs], 0)
    both = dot_tn(join([emb, target], 1), emb)
    return dot_tn(back, back), both[:rank] - GAMMA * both[rank:]


def forward_kernel(cfg, count, first, *refs):
    xs, refs = refs[:count], refs[count:]
    weights, refs = refs[:7], refs[7:]
    if not first:
        gram_in, refs = refs[0], refs[1:]
    outs, gram_out = refs[:6], refs[6]
    gram, cross = forward_rows(cfg, xs, weights, outs)
    rank = cfg["rank"]
    gram_out[:, :rank] = gram if first else gram_in[:, :rank] + gram
    gram_out[:, rank:] = cross if first else gram_in[:, rank:] + cross


def last_kernel(cfg, early, count, *refs):
    groups = []
    for size in early:
        groups.append((refs[:size], refs[size : size + 6]))
        refs = refs[size + 6 :]
    xs, refs = refs[:count], refs[count:]
    weights, refs = refs[:7], refs[7:]
    gram_in, send_ref, keep_ref = refs[:3]
    outs, part_ref = refs[3:9], refs[9]
    rank, block, rows, obs_pad = cfg["rank"], cfg["block"], cfg["rows"], cfg["obs_pad"]
    group, replicas = cfg["group"], cfg["replicas"]
    factor = 1.0 / math.sqrt(cfg["total"])
    c1, c2, c3 = cfg["cols"]
    gram, cross = forward_rows(cfg, xs, weights, outs)
    gram_hi, gram_lo = split_two(gram_in[:, :rank] + gram)
    cross_hi, cross_lo = split_two(gram_in[:, rank:] + cross)
    groups.append((xs, outs))
    me = pl.multiple_of(lax.axis_index("dp") * block, ROW_TILE)
    fo = weights[2][pl.ds(me, block), :]
    bo = weights[3][pl.ds(me, block), :]
    few = [item for item in groups if len(item[0]) == 1]
    many = [item for item in groups if len(item[0]) > 1]
    square = jnp.zeros((1, rank), F32)
    diagonal = jnp.zeros((1, rank), F32)
    f_deltas, b_deltas, f_hids, b_hids, d_fs, d_us, wholes, laters = ([] for _ in range(8))
    for members in (few, many):
        if not members:
            continue
        saved = list(zip(*(item[1] for item in members)))
        emb32 = stack(saved[2], 0).astype(F32)
        target = join([x_ref[0:rows, obs_pad:] for item in members for x_ref in item[0]], 0)
        error = emb32 - GAMMA * target.astype(F32)
        err_hi, err_lo = split_two(error)
        u = stack(saved[3], 0)
        scale = lax.rsqrt(jnp.mean(u * u, axis=-1, keepdims=True) + EPSILON)
        back = (u * scale).astype(BF16)
        back32 = back.astype(F32)
        pulled = dot_nn(err_hi, gram_hi) + (dot_nn(err_hi, gram_lo) + dot_nn(err_lo, gram_hi))
        square = square + jnp.sum(pulled * error, axis=0, keepdims=True)
        diagonal = diagonal + jnp.sum(emb32 * back32, axis=0, keepdims=True)
        d_f = (factor * (pulled / group - back32)).astype(BF16)
        pushed = dot_nn(back, cross_hi) + dot_nn(back, cross_lo)
        d_b = factor * (pushed / group - emb32)
        inner = jnp.mean(u * d_b, axis=-1, keepdims=True)
        d_u = (scale * d_b - u * (scale * scale * scale * inner)).astype(BF16)
        f_hid, b_hid = stack(saved[4], 1), stack(saved[5], 1)
        zero = jnp.zeros_like(f_hid)
        f_deltas.append(jnp.where(f_hid > 0, dot_nt(fo, d_f).astype(BF16), zero))
        b_deltas.append(jnp.where(b_hid > 0, dot_nt(bo, d_u).astype(BF16), zero))
        f_hids.append(f_hid)
        b_hids.append(b_hid)
        d_fs.append(d_f)
        d_us.append(d_u)
        wholes += saved[0]
        laters += saved[1]
    part_ref[:, :c1] = dot_nn(join(f_deltas, 1), stack(wholes, 0))
    part_ref[:, c1:c2] = dot_nn(join(f_hids, 1), join(d_fs, 0))
    part_ref[:, c2:c3] = dot_nn(join(b_deltas, 1), stack(laters, 0))
    part_ref[:, c3:] = dot_nn(join(b_hids, 1), join(d_us, 0))
    loss = (0.5 / group) * jnp.sum(square) - jnp.sum(diagonal)
    lanes = lax.broadcasted_iota(jnp.int32, (block, LANES), 1)
    spot = cfg["loss_spot"]
    base = spot // LANES * LANES
    first = spot - base + 3 * lax.axis_index("replica")
    rest = jnp.full((block, LANES), loss, F32)
    piece_tile = part_ref[:, base : base + LANES]
    piece_tile = jnp.where(lanes >= spot - base, 0.0, piece_tile)
    for j in range(3):
        piece = rest.astype(BF16).astype(F32)
        piece_tile = jnp.where(lanes == first + j, piece, piece_tile)
        rest = rest - piece
    part_ref[:, base : base + LANES] = piece_tile
    core = lax.rem(lax.axis_index("replica"), 2)
    half = block // 2
    keep_ref[...] = part_ref[pl.ds(pl.multiple_of(core * half, ROW_TILE), half), :]
    other = pl.multiple_of((1 - core) * half, ROW_TILE)
    send_ref[...] = part_ref[pl.ds(other, half), :].astype(BF16)


def finish_kernel(cfg, one_ref, two_ref, far_ref, fs, fa, fl, fo, bs, bo, loss_ref, act_ref):
    obs, act, rank, x_pad, obs_pad = (cfg[k] for k in ("obs", "act", "rank", "x_pad", "obs_pad"))
    half = cfg["block"] // 2
    c1, c2, c3 = cfg["cols"]
    core = lax.rem(lax.axis_index("replica"), 2)
    mine32 = one_ref[...].astype(F32) + two_ref[...].astype(F32)
    mine = mine32.astype(BF16)
    far = far_ref[...]
    for start, value in ((core * half, mine), ((1 - core) * half, far)):
        here = pl.ds(pl.multiple_of(start, ROW_TILE), half)
        fs[here, :] = value[:, :obs]
        fl[here, :] = value[:, x_pad:c1]
        fo[here, :] = value[:, c1:c2]
        bs[here, :] = value[:, c2 : c2 + obs]
        bo[here, :] = value[:, c3:]
        act_ref[here, :] = value[:, obs_pad : obs_pad + LANES].astype(F32)
    fa[...] = act_ref[...].T[:act].astype(BF16)
    spot = cfg["loss_spot"]
    base = spot // LANES * LANES
    pieces = mine32[0:8, base : base + LANES]
    lanes = lax.broadcasted_iota(jnp.int32, (8, LANES), 1)
    rows = lax.broadcasted_iota(jnp.int32, (8, LANES), 0)
    ours = (lanes >= spot - base) & (lanes < spot - base + 3 * cfg["replicas"]) & (rows == 0)
    loss_ref[0, 0] = jnp.sum(jnp.where(ours, pieces, 0.0)) / cfg["total"]


def exchange(array, axis, size, bit):
    return lax.ppermute(array, axis, [(i, i ^ bit) for i in range(size)])


def in_hbm(*arrays):
    return [pltpu.with_memory_space_constraint(array, pltpu.HBM) for array in arrays]


def shape(dims, kind):
    return jax.ShapeDtypeStruct(dims, kind)


def fast_local(
    states,
    actions,
    target_forward,
    next_index,
    latent_ids,
    latents,
    f_state,
    f_action,
    f_latent,
    f_output,
    b_state,
    b_output,
):
    size = lax.axis_size("dp")
    replicas = lax.axis_size("replica")
    rows, obs = states.shape[1:]
    act = actions.shape[2]
    zcount, rank = latents.shape
    hidden = f_state.shape[1]
    block = hidden // size
    group = rows * size
    side = round_up(act + 2, 2 * ROW_TILE)
    lane = round_up(rows, LANES)
    obs_pad = round_up(obs, LANES)
    x_pad = obs_pad + LANES
    c1 = x_pad + rank
    c2 = c1 + rank
    c3 = c2 + obs_pad
    width = c3 + rank
    cfg = dict(
        rows=rows,
        obs=obs,
        act=act,
        rank=rank,
        obs_pad=obs_pad,
        x_pad=x_pad,
        hidden=hidden,
        zcount=zcount,
        side=side,
        lane=lane,
        group=group,
        replicas=replicas,
        total=group * replicas,
        block=block,
        tile=256,
        cols=(c1, c2, c3),
        loss_spot=obs_pad + side,
    )
    params = pltpu.CompilerParams(vmem_limit_bytes=20 * 1024 * 1024)
    last_params = pltpu.CompilerParams(vmem_limit_bytes=28 * 1024 * 1024)
    own = pl.pallas_call(
        functools.partial(pack_kernel, cfg),
        out_shape=shape((rows + side // 2, obs_pad + rank), BF16),
        scratch_shapes=[pltpu.VMEM((side, lane), F32)],
        compiler_params=pltpu.CompilerParams(vmem_limit_bytes=8 * 1024 * 1024),
        name="pack",
    )(*in_hbm(states, actions[0].T, next_index, latent_ids, target_forward))
    x = {"own": own}
    middle = [(2 + i, 4 + i) for i in range(2)] + [(4 + i, 2 + i) for i in range(2)]
    outward = [(2 + i, i) for i in range(2)] + [(4 + i, 6 + i) for i in range(2)]
    across = lax.ppermute(own, "dp", middle)
    x["x own"] = exchange(own, "dp", size, 1)
    x["half"] = exchange(own, "dp", size, 2)
    handed = lax.ppermute(across, "dp", outward)
    x["x half"] = exchange(x["half"], "dp", size, 1)
    across_two = lax.ppermute(x["half"], "dp", middle)
    x["second"] = across + handed
    x["x second"] = exchange(x["second"], "dp", size, 1)
    handed_two = lax.ppermute(across_two, "dp", outward)
    x["third"] = across_two + handed_two
    x["x third"] = exchange(x["third"], "dp", size, 1)
    wf, wb, wfb, wbb = pl.pallas_call(
        functools.partial(weights_kernel, cfg),
        out_shape=(
            shape((x_pad + rank, hidden), BF16),
            shape((obs_pad, hidden), BF16),
            shape((block, x_pad + rank), BF16),
            shape((block, obs_pad), BF16),
        ),
        in_specs=[pl.BlockSpec(memory_space=pl.ANY)] * 4,
        scratch_shapes=[
            pltpu.VMEM((obs, hidden), BF16),
            pltpu.VMEM((act, hidden), BF16),
            pltpu.VMEM((rank, hidden), BF16),
            pltpu.VMEM((obs, hidden), BF16),
            pltpu.SemaphoreType.DMA((4,)),
        ],
        compiler_params=pltpu.CompilerParams(vmem_limit_bytes=16 * 1024 * 1024),
        cost_estimate=pl.CostEstimate(flops=0, bytes_accessed=1_000_000, transcendentals=0),
        name="weights",
    )(*in_hbm(f_state, f_action, f_latent, b_state))
    weights = (wf, wb, f_output, b_output, latents, wfb, wbb)
    row_flops = 2 * (c1 + 2 * rank + obs_pad) * hidden + 8 * rank * rank

    def kept(count):
        m = rows * count
        return (
            ((m, x_pad + rank), BF16),
            ((m, obs_pad), BF16),
            ((m, rank), BF16),
            ((m, rank), F32),
            ((block, m), BF16),
            ((block, m), BF16),
        )

    grams = ()
    plan = (
        (("own",), 3.0),
        (("half",), 2.0),
        (("x own",), 1.5),
        (("x half", "second"), 1.0),
        (("third", "x second"), 3.0),
    )
    early = []
    for steps, work in plan:
        count = len(steps)
        xs = [x[step] for step in steps]
        *saved, total_grams = pl.pallas_call(
            functools.partial(forward_kernel, cfg, count, not early),
            out_shape=(*(shape(*item) for item in kept(count)), shape((rank, 2 * rank), F32)),
            compiler_params=params,
            cost_estimate=pl.CostEstimate(
                flops=int(work * rows * count * row_flops),
                bytes_accessed=1_000_000,
                transcendentals=0,
            ),
            name="forward",
        )(*xs, *weights, *grams)
        grams = (total_grams,)
        early.append((xs, saved))
    left = [x["x third"]]
    operands = []
    for xs, saved in early:
        operands += [*xs, *saved]
    send, keep = pl.pallas_call(
        functools.partial(last_kernel, cfg, [len(xs) for xs, _ in early], len(left)),
        out_shape=(shape((block // 2, width), BF16), shape((block // 2, width), F32)),
        scratch_shapes=[
            *(pltpu.VMEM(*item) for item in kept(len(left))),
            pltpu.VMEM((block, width), F32),
        ],
        compiler_params=last_params,
        cost_estimate=pl.CostEstimate(
            flops=4 * group * width * block, bytes_accessed=16_000_000, transcendentals=0
        ),
        name="last",
    )(*operands, *left, *weights, *grams)
    got = exchange(send, "replica", replicas, 1)
    one = (keep + got.astype(F32)).astype(BF16)
    two = exchange(one, "replica", replicas, 2)
    mine = (one.astype(F32) + two.astype(F32)).astype(BF16)
    far = exchange(mine, "replica", replicas, 1)
    fs, fa, fl, fo, bs, bo, loss = pl.pallas_call(
        functools.partial(finish_kernel, cfg),
        out_shape=(
            shape((block, obs), BF16),
            shape((act, block), BF16),
            shape((block, rank), BF16),
            shape((block, rank), BF16),
            shape((block, obs), BF16),
            shape((block, rank), BF16),
            shape((1, 1), F32),
        ),
        out_specs=(
            *(pl.BlockSpec(memory_space=pltpu.VMEM) for _ in range(6)),
            pl.BlockSpec(memory_space=pltpu.SMEM),
        ),
        scratch_shapes=[pltpu.VMEM((block, LANES), F32)],
        compiler_params=pltpu.CompilerParams(vmem_limit_bytes=16 * 1024 * 1024),
        name="finish",
    )(one, two, far)
    return (fs.T, fa, fl.T, fo, bs.T, bo, loss.reshape(()))


def forward_pass(
    current, later, moves, latent_rows, f_state, f_action, f_latent, f_output, b_state, b_output
):
    f_pre = (
        jnp.dot(current, f_state, preferred_element_type=F32)
        + jnp.dot(moves, f_action, preferred_element_type=F32)
        + jnp.dot(latent_rows, f_latent, preferred_element_type=F32)
    )
    f_hidden = jnp.maximum(f_pre, 0.0).astype(BF16)
    forward_emb = jnp.dot(f_hidden, f_output, preferred_element_type=F32).astype(BF16)
    b_pre = jnp.dot(later, b_state, preferred_element_type=F32)
    b_hidden = jnp.maximum(b_pre, 0.0).astype(BF16)
    b_raw = jnp.dot(b_hidden, b_output, preferred_element_type=F32)
    b_scale = lax.rsqrt(jnp.mean(b_raw * b_raw, axis=-1, keepdims=True) + EPSILON)
    backward_emb = (b_raw * b_scale).astype(BF16)
    return (f_pre, f_hidden, forward_emb, b_pre, b_hidden, b_raw, b_scale, backward_emb)


def general_local(
    states,
    actions,
    target_forward,
    next_index,
    latent_ids,
    latents,
    f_state,
    f_action,
    f_latent,
    f_output,
    b_state,
    b_output,
):
    current = states[0]
    moves = actions[0]
    later = jnp.take(current, next_index[0], axis=0)
    latent_rows = jnp.take(latents, latent_ids[0], axis=0)
    f_pre, f_hidden, forward_emb, b_pre, b_hidden, b_raw, b_scale, backward_emb = forward_pass(
        current, later, moves, latent_rows, f_state, f_action, f_latent, f_output, b_state, b_output
    )
    group = current.shape[0] * lax.axis_size("dp")
    total = group * lax.axis_size("replica")
    factor = 1.0 / math.sqrt(total)
    forward32 = forward_emb.astype(F32)
    back32 = backward_emb.astype(F32)
    error = forward32 - GAMMA * target_forward[0].astype(F32)
    gram, cross = lax.psum(
        (
            jnp.dot(backward_emb.T, backward_emb, preferred_element_type=F32),
            jnp.dot(forward32.T, error, precision=HIGH, preferred_element_type=F32),
        ),
        "dp",
    )
    pulled = jnp.dot(error, gram, precision=HIGH, preferred_element_type=F32)
    pushed = jnp.dot(back32, cross.T, precision=HIGH, preferred_element_type=F32)
    partial_loss = 0.5 / group * jnp.sum(pulled * error) - jnp.sum(forward32 * back32)
    grad_forward = (factor * (pulled / group - back32)).astype(BF16)
    grad_backward = factor * (pushed / group - forward32)
    inner = jnp.mean(b_raw * grad_backward, axis=-1, keepdims=True)
    grad_raw = (b_scale * grad_backward - b_raw * b_scale * b_scale * b_scale * inner).astype(BF16)
    part_bo = jnp.dot(b_hidden.T, grad_raw, preferred_element_type=F32)
    b_back = jnp.dot(grad_raw, b_output.T, preferred_element_type=F32)
    b_delta = jnp.where(b_pre > 0, b_back, 0.0).astype(BF16)
    part_bs = jnp.dot(later.T, b_delta, preferred_element_type=F32)
    part_fo = jnp.dot(f_hidden.T, grad_forward, preferred_element_type=F32)
    f_back = jnp.dot(grad_forward, f_output.T, preferred_element_type=F32)
    f_delta = jnp.where(f_pre > 0, f_back, 0.0).astype(BF16)
    part_fs = jnp.dot(current.T, f_delta, preferred_element_type=F32)
    part_fa = jnp.dot(moves.T, f_delta, preferred_element_type=F32)
    part_fl = jnp.dot(latent_rows.T, f_delta, preferred_element_type=F32)
    places = (1, 1, 1, 0, 1, 0)
    parts = (part_fs, part_fa, part_fl, part_fo, part_bs, part_bo)
    shares = tuple(
        lax.psum_scatter(part, "dp", scatter_dimension=place, tiled=True)
        for part, place in zip(parts, places)
    )
    summed = lax.psum(shares, "replica")
    loss_sum = lax.psum(partial_loss, ("dp", "replica"))
    return (*(item.astype(BF16) for item in summed), loss_sum / total)


def local(*args):
    size, replicas = lax.axis_size("dp"), lax.axis_size("replica")
    rows, hidden = args[0].shape[1], args[6].shape[1]
    fits = size == 8 and replicas == 4 and rows * size <= KERNEL_GROUP_LIMIT
    block = hidden // size
    whole = rows % ROW_TILE == 0 and hidden % (size * 64) == 0 and hidden % 512 == 0
    whole = whole and LANES < block <= 2 * LANES - 64 and args[6].shape[0] % 8 == 0
    exact = rows <= 256 and args[5].shape[0] <= 256
    return (fast_local if fits and whole and exact else general_local)(*args)


def solution(mesh):
    in_specs = (
        P("replica", "dp", None),
        P("replica", "dp", None),
        P("replica", "dp", None),
        P("replica", "dp"),
        P("replica", "dp"),
        P(),
        P(),
        P(),
        P(),
        P(),
        P(),
        P(),
    )
    out_specs = (
        P(None, "dp"),
        P(None, "dp"),
        P(None, "dp"),
        P("dp", None),
        P(None, "dp"),
        P("dp", None),
        P(),
    )
    return jax.shard_map(local, mesh=mesh, in_specs=in_specs, out_specs=out_specs, check_vma=False)
```
